256 devices in a mesh: space: 64 (over z, y, core), mp: 4 (over x).
Axes of the slice: x: 4, y: 4, z: 8, core: 2. Of those that a mesh axis runs over, the one named last changes fastest.
Arguments:
- activations: bfloat16 [16384, 1024], P('space'), may hold values from -30 to 30
- w_query: bfloat16 [1024, 1024], P(None, 'mp'), may hold values from -1 to 1
- w_key: bfloat16 [1024, 1024], P(None, 'mp'), may hold values from -1 to 1
- w_value: bfloat16 [1024, 1024], P(None, 'mp'), may hold values from -0.1875 to 0.1875
- w_out: bfloat16 [1024, 1024], P('mp'), may hold values from -0.1875 to 0.1875
- grad_output: bfloat16 [16384, 1024], P('space', 'mp'), may hold values from -6 to 6
- neighbours: int32 [256, 9], P('space'), may hold values from 0 to 255, as said below
- pad_mask: int32 [256, 9], P('space'), may hold values from 0 to 1, as said below
Outputs:
- output: bfloat16 [16384, 1024], P('space', 'mp')
- grad_input: bfloat16 [16384, 1024], P('space', 'mp')
- weight_grads: float32 [4, 1024, 1024], P(None, 'space', 'mp')
The draws below stay inside these ranges and needn't reach their ends.
Inputs may be any that keep to these rules, and one draw needn't show every extreme that they name: `neighbours`: patch r * 4 + c is column c of row r of patches, and row r lies on index r of space; every slot names a patch of row r - 1, r or r + 1; slot 4 names the patch itself; slots that would leave the band name the patch itself. `pad_mask`: slot 4 is always live; slots that leave the band are 0.
All inputs are finite; a program needn't handle non-finite values.
Results may differ from the reference program's by a relative error of at most 0.019.
Values may be sent and summed in bfloat16 or wider, within the bound.
No kernel may reach another device: no remote copies, remote signals or barrier semaphores. Data moves between devices by JAX's collectives and lax.ppermute only.
A program may use at most 64 MiB of HBM per device.

```python
import jax
import jax.numpy as jnp
from jax import lax

D = 1024
HD = 64
PATCH = 64
NB = 9
CYCLE = 4
PATCHES = 256
CELLS = 16384
N_SPACE = 64


def shared_normal(key):
    return jnp.clip(jax.random.normal(key, (D, D), jnp.float32), -6.0, 6.0)


def layout(key):
    row_count = PATCHES // CYCLE
    offsets = jax.random.randint(jax.random.fold_in(key, 11), (row_count, 2), -1, 2)
    numbers = jnp.arange(PATCHES, dtype=jnp.int32)
    band_of = numbers // CYCLE
    column = numbers % CYCLE
    row_step = jnp.array([-1, -1, -1, 0, 0, 0, 1, 1, 1], jnp.int32)
    column_step = jnp.array([-1, 0, 1, -1, 0, 1, -1, 0, 1], jnp.int32)
    below_shift = offsets[band_of, 0][:, None]
    above_shift = offsets[band_of, 1][:, None]
    shifted = jnp.where(row_step[None, :] < 0, below_shift, jnp.where(row_step[None, :] > 0, above_shift, 0))
    target_band = band_of[:, None] + row_step[None, :]
    target_column = (column[:, None] + column_step[None, :] + shifted) % CYCLE
    inside = (target_band >= 0) & (target_band < row_count)
    slots = jnp.where(inside, target_band * CYCLE + target_column, numbers[:, None])
    dropped = jax.random.randint(jax.random.fold_in(key, 12), (PATCHES, NB), 0, 6) == 0
    centre = jnp.arange(NB, dtype=jnp.int32)[None, :] == 4
    live = inside & (centre | jnp.logical_not(dropped))
    return (slots.astype(jnp.int32), live.astype(jnp.int32))


def draw_neighbours(key, part):
    slots, live = layout(key)
    return slots


def draw_pad_mask(key, part):
    slots, live = layout(key)
    return live


def draw_w_query(key, part):
    common = shared_normal(key)
    return (common * D ** (-0.5)).astype(jnp.bfloat16)


def draw_w_key(key, part):
    key = jax.random.fold_in(key, 2)
    own_part = jnp.clip(jax.random.normal(key, (D, D), jnp.float32), -6.0, 6.0)
    mixed = own_part
    return (mixed * D ** (-0.5)).astype(jnp.bfloat16)


def draw_activations(key, part):
    key = jax.random.fold_in(key, 3)
    first = jax.random.fold_in(key, 0)
    values = jax.random.normal(first, (CELLS, D), jnp.float32)
    return jnp.clip(values, -30.0, 30.0).astype(jnp.bfloat16)


def levels(own_key, extent, cuts, smallest, largest):
    level, own = 1.0, jax.random.fold_in(own_key, 6)
    for dim, shards_of in cuts:
        draws = jnp.exp(jax.random.uniform(jax.random.fold_in(own, dim), (shards_of,), jnp.float32, smallest / len(cuts), largest / len(cuts)))
        level = level * jnp.repeat(draws, extent[dim] // shards_of).reshape([-1 if axis == dim else 1 for axis in range(len(extent))])
    return level


def bell_draw(rng, dims, spread, limit, shards=(), held_as=jnp.bfloat16):
    factor_of = levels(rng, dims, shards, -0.22, 0.18) if shards else 1.0
    entries = jax.random.normal(rng, dims, jnp.float32) * spread * factor_of
    return jnp.minimum(jnp.maximum(entries, -limit), limit).astype(held_as)


def setup_inputs(seed: int = 0) -> dict:
    key_of = jax.random.split(jax.random.key(seed), 9)
    activations = draw_activations(jax.random.fold_in(key_of[8], 71), 0)
    w_query = draw_w_query(jax.random.fold_in(key_of[8], 71), 0)
    w_key = draw_w_key(jax.random.fold_in(key_of[8], 71), 0)
    w_value = bell_draw(key_of[3], (D, D), D ** -0.5, 0.1875, ((1, 4),))
    w_out = bell_draw(key_of[4], (D, D), D ** -0.5, 0.1875, ((0, 4),))
    grad_output = bell_draw(key_of[5], (CELLS, D), 1.0, 6.0, ((0, 64), (1, 4)))
    neighbours = draw_neighbours(jax.random.fold_in(key_of[8], 71), 0)
    pad_mask = draw_pad_mask(jax.random.fold_in(key_of[8], 71), 0)
    return {"activations": activations, "w_query": w_query, "w_key": w_key, "w_value": w_value, "w_out": w_out, "grad_output": grad_output, "neighbours": neighbours, "pad_mask": pad_mask}


masked_score = -1.0e30


def attend(queries, key_tiles, value_tiles, keep_mask, grad_attended):
    count, slots, patch_len, head_count, head_dim = key_tiles.shape
    key_flat = key_tiles.reshape(count, slots * patch_len, head_count, head_dim).astype(jnp.float32)
    value_flat = value_tiles.reshape(count, slots * patch_len, head_count, head_dim).astype(jnp.float32)
    query_wide = queries.astype(jnp.float32)
    grad_wide = grad_attended.astype(jnp.float32)
    factor = head_dim ** -0.5
    scores = jnp.einsum("rihe,rjhe->rhij", query_wide, key_flat) * factor
    visible = jnp.repeat(keep_mask, patch_len, axis=1) > 0
    scores = jnp.where(visible[:, None, None, :], scores, masked_score)
    peak_score = jnp.max(scores, axis=-1, keepdims=True)
    weights = jnp.exp(scores - peak_score)
    probs = weights / jnp.sum(weights, axis=-1, keepdims=True)
    probs_low = probs.astype(jnp.bfloat16)
    probs_wide = probs_low.astype(jnp.float32)
    attended = jnp.einsum("rhij,rjhe->rihe", probs_wide, value_flat).astype(jnp.bfloat16)
    grad_probs = jnp.einsum("rihe,rjhe->rhij", grad_wide, value_flat)
    grad_values = jnp.einsum("rhij,rihe->rjhe", probs_wide, grad_wide)
    centre = jnp.sum(probs * grad_probs, axis=-1, keepdims=True)
    grad_scores = (probs * (grad_probs - centre) * factor).astype(jnp.bfloat16).astype(jnp.float32)
    grad_queries = jnp.einsum("rhij,rjhe->rihe", grad_scores, key_flat)
    grad_keys = jnp.einsum("rhij,rihe->rjhe", grad_scores, query_wide)
    return attended, grad_queries, grad_keys.reshape(key_tiles.shape), grad_values.reshape(key_tiles.shape)


def reference(activations, w_query, w_key, w_value, w_out, grad_output, neighbours, pad_mask):
    def project(weight):
        return jnp.dot(activations, weight, preferred_element_type=jnp.float32).astype(jnp.bfloat16)

    query = project(w_query)
    key_rows = project(w_key)
    value_rows = project(w_value)
    grad_attended = jnp.dot(grad_output, w_out.T, preferred_element_type=jnp.float32).astype(jnp.bfloat16)
    head_count = D // HD
    query_blocks = query.reshape(N_SPACE, CYCLE, PATCH, head_count, HD)
    grad_blocks = grad_attended.reshape(N_SPACE, CYCLE, PATCH, head_count, HD)
    key_patches = key_rows.reshape(PATCHES, PATCH, head_count, HD)
    value_patches = value_rows.reshape(PATCHES, PATCH, head_count, HD)
    slot_blocks = neighbours.reshape(N_SPACE, CYCLE, NB).astype(jnp.int32)
    mask_blocks = pad_mask.reshape(N_SPACE, CYCLE, NB)

    def one_band(carry, inputs):
        key_sums, value_sums = carry
        query_band, grad_band, slot_band, mask_band = inputs
        key_tiles = key_patches[slot_band]
        value_tiles = value_patches[slot_band]
        attended, grad_queries, grad_keys, grad_values = attend(query_band, key_tiles, value_tiles, mask_band, grad_band)
        flat_slots = slot_band.reshape(-1)
        key_sums = key_sums.at[flat_slots].add(grad_keys.reshape(CYCLE * NB, PATCH, head_count, HD))
        value_sums = value_sums.at[flat_slots].add(grad_values.reshape(CYCLE * NB, PATCH, head_count, HD))
        return (key_sums, value_sums), (attended, grad_queries)

    empty = jnp.zeros((PATCHES, PATCH, head_count, HD), jnp.float32)
    (key_sums, value_sums), (attended, grad_queries) = lax.scan(
        one_band, (empty, empty), (query_blocks, grad_blocks, slot_blocks, mask_blocks))
    attended = attended.reshape(CELLS, D)
    grad_query = grad_queries.reshape(CELLS, D).astype(jnp.bfloat16)
    grad_key = key_sums.reshape(CELLS, D).astype(jnp.bfloat16)
    grad_value = value_sums.reshape(CELLS, D).astype(jnp.bfloat16)
    output = jnp.dot(attended, w_out, preferred_element_type=jnp.float32).astype(jnp.bfloat16)
    grad_input = (jnp.dot(grad_query, w_query.T, preferred_element_type=jnp.float32)
                  + jnp.dot(grad_key, w_key.T, preferred_element_type=jnp.float32)
                  + jnp.dot(grad_value, w_value.T, preferred_element_type=jnp.float32)).astype(jnp.bfloat16)
    weight_grads = jnp.stack([
        jnp.dot(activations.T, grad_query, preferred_element_type=jnp.float32),
        jnp.dot(activations.T, grad_key, preferred_element_type=jnp.float32),
        jnp.dot(activations.T, grad_value, preferred_element_type=jnp.float32),
        jnp.dot(grad_output.T, attended, preferred_element_type=jnp.float32)])
    return output, grad_input, weight_grads
```

```python
import jax
import jax.numpy as jnp
from jax import lax
from jax.experimental import pallas as pl
from jax.experimental.pallas import tpu as pltpu
from jax.sharding import Mesh
from jax.sharding import PartitionSpec as P

HD = 64
PATCH = 64
D = 1024
ROW = 256
WIDTH = 256
HEADS = WIDTH // HD
KEYS = 3 * ROW
LOG2E = 1.4426950408889634
BF = jnp.bfloat16
F32 = jnp.float32
VMEM_BYTES = 56 * 1024 * 1024

NN = (((1,), (0,)), ((), ()))
NT = (((1,), (1,)), ((), ()))


def mm(a, b, dims=NN):
    return lax.dot_general(a, b, dims, preferred_element_type=F32)


def attention_kernel(
    pos, bias, a_lo, a_own, a_hi, wq, wk, wv, wo, c0, c1, c2, c3,
    att_out, gq_out, lo_out, own_out, hi_out, send_out, keep_out,
    key_s, value_s, dw_s,
):
    core, y, z, x = pos[0], pos[1], pos[2], pos[3]
    query = mm(a_own[...], wq[...]).astype(BF)
    for band, block in enumerate((a_lo, a_own, a_hi)):
        rows = slice(band * ROW, (band + 1) * ROW)
        key_s[rows, :] = mm(block[...], wk[...]).astype(BF)
        value_s[rows, :] = mm(block[...], wv[...]).astype(BF)
    cots = (c0, c1, c2, c3)
    grad_att = jnp.zeros((ROW, WIDTH), F32)
    for step in range(4):
        cols = pl.ds(pl.multiple_of(lax.rem(x + 4 - step, 4) * WIDTH, WIDTH), WIDTH)
        grad_att += mm(cots[step][...], wo[:, cols], NT)
    grad_att = grad_att.astype(BF)

    keys = key_s[...]
    values = value_s[...]
    keys_t = keys.T
    values_t = values.T
    lane_head = lax.broadcasted_iota(jnp.int32, (ROW, WIDTH), 1) // HD
    bias_rows = jnp.concatenate(
        [jnp.broadcast_to(bias[patch : patch + 1, :], (PATCH, ROW)) for patch in range(KEYS // PATCH)],
        axis=0,
    )
    grad_key = jnp.zeros((KEYS, WIDTH), F32)
    grad_value = jnp.zeros((KEYS, WIDTH), F32)
    att_rows, gq_rows = [], []
    for head in range(HEADS):
        feats = slice(head * HD, (head + 1) * HD)
        q_head = jnp.where(lane_head == head, query, jnp.zeros_like(query))
        g_head = jnp.where(lane_head == head, grad_att, jnp.zeros_like(grad_att))
        scores = mm(keys, q_head, NT) * (LOG2E * HD**-0.5) + bias_rows
        peak = jnp.max(scores, axis=0, keepdims=True)
        weights = jnp.exp2(scores - peak)
        probs = weights * (1.0 / jnp.sum(weights, axis=0, keepdims=True))
        probs_low = probs.astype(BF)
        grad_probs = mm(values, g_head, NT)
        centre = jnp.sum(probs * grad_probs, axis=0, keepdims=True)
        grad_scores = (probs * (grad_probs - centre) * HD**-0.5).astype(BF)
        att_rows.append(mm(values_t[feats, :], probs_low))
        gq_rows.append(mm(keys_t[feats, :], grad_scores))
        grad_key += mm(grad_scores, q_head)
        grad_value += mm(probs_low, g_head)
    att = jnp.concatenate(att_rows, axis=0).astype(BF).T
    gq = jnp.concatenate(gq_rows, axis=0).astype(BF).T
    att_out[...] = att
    gq_out[...] = gq
    lo_out[0], lo_out[1] = grad_key[:ROW].astype(BF), grad_value[:ROW].astype(BF)
    own_out[0], own_out[1] = grad_key[ROW : 2 * ROW], grad_value[ROW : 2 * ROW]
    hi_out[0], hi_out[1] = grad_key[2 * ROW :].astype(BF), grad_value[2 * ROW :].astype(BF)

    grad_key = grad_key.astype(BF)
    grad_value = grad_value.astype(BF)
    act_t = jnp.concatenate([a_lo[...], a_own[...], a_hi[...]], axis=0).T
    dw_s[0] = mm(act_t[:, ROW : 2 * ROW], gq)
    dw_s[1] = mm(act_t, grad_key)
    dw_s[2] = mm(act_t, grad_value)
    for step in range(4):
        rows = pl.ds(pl.multiple_of(lax.rem(x + 4 - step, 4) * WIDTH, WIDTH), WIDTH)
        dw_s[3, rows, :] = mm(cots[step][...].T, att)
    for mine, out in ((0, send_out), (1, keep_out)):
        c = core if mine else 1 - core
        for ys in range(4):
            yy = lax.rem(y + ys, 4)
            for low in range(2):
                for hs in range(4):
                    zl = lax.rem(z, 2)
                    zl = zl if low else 1 - zl
                    zz = 2 * lax.rem(z // 2 + hs, 4) + zl
                    row = pl.multiple_of(((zz * 4 + yy) * 2 + c) * 16, 16)
                    out[ys, low, hs] = dw_s[:, pl.ds(row, 16), :].astype(BF)


def input_kernel(pos, att, gq, own, from_lo, from_hi, wq, wk, wv, wo, p0, p1, p2, p3):
    x = pos[3]
    total = own[...] + from_lo[...].astype(F32) + from_hi[...].astype(F32)
    grad_key = total[0].astype(BF)
    grad_value = total[1].astype(BF)
    for step, out in enumerate((p0, p1, p2, p3)):
        block = pl.ds(pl.multiple_of(lax.rem(x + step, 4) * WIDTH, WIDTH), WIDTH)
        out[0] = mm(att[...], wo[:, block]).astype(out.dtype)
        out[1] = (
            mm(gq[...], wq[block, :], NT)
            + mm(grad_key, wk[block, :], NT)
            + mm(grad_value, wv[block, :], NT)
        ).astype(out.dtype)


def vmem(count):
    return [pl.BlockSpec(memory_space=pltpu.VMEM)] * count


def smem():
    return [pl.BlockSpec(memory_space=pltpu.SMEM)]


def shift(value, axis, steps):
    count = lax.axis_size(axis)
    return lax.ppermute(value, axis, [(i, (i + steps) % count) for i in range(count)])


def shift_open(value, axis, steps):
    count = lax.axis_size(axis)
    return lax.ppermute(
        value, axis, [(i, i + steps) for i in range(count) if 0 <= i + steps < count]
    )


def swap(value, axis):
    count = lax.axis_size(axis)
    return lax.ppermute(value, axis, [(i, i ^ 1) for i in range(count)])


def body(activations, w_query, w_key, w_value, w_out, grad_output, neighbours, pad_mask):
    space = ("z", "y", "core")
    act_lo = shift_open(activations, space, 1)
    act_hi = shift_open(activations, space, -1)
    cots = [grad_output] + [shift(grad_output, "mp", s) for s in (1, 2, 3)]
    pos = jnp.stack([lax.axis_index(a) for a in ("core", "y", "z", "mp")]).astype(jnp.int32)

    local = neighbours - (lax.axis_index(space) - 1) * 4
    table = lax.broadcasted_iota(jnp.int32, (16, 4, 9), 0)
    live = jnp.where((local[None] == table) & (pad_mask[None] > 0), 1.0, 0.0)
    count = jnp.sum(live, axis=-1)
    bias = jnp.where(count > 0, jnp.log2(jnp.maximum(count, 1.0)), -1e30)
    bias = jnp.repeat(bias, PATCH, axis=1)

    half = (4, 2, 4, 4, 16, WIDTH)
    att, gq, lo, own, hi, dw_send, dw_keep = pl.pallas_call(
        attention_kernel,
        out_shape=(
            jax.ShapeDtypeStruct((ROW, WIDTH), BF),
            jax.ShapeDtypeStruct((ROW, WIDTH), BF),
            jax.ShapeDtypeStruct((2, ROW, WIDTH), BF),
            jax.ShapeDtypeStruct((2, ROW, WIDTH), F32),
            jax.ShapeDtypeStruct((2, ROW, WIDTH), BF),
            jax.ShapeDtypeStruct(half, BF),
            jax.ShapeDtypeStruct(half, BF),
        ),
        in_specs=smem() + vmem(12),
        out_specs=tuple(vmem(7)),
        scratch_shapes=[
            pltpu.VMEM((KEYS, WIDTH), BF),
            pltpu.VMEM((KEYS, WIDTH), BF),
            pltpu.VMEM((4, D, WIDTH), F32),
        ],
        compiler_params=pltpu.CompilerParams(vmem_limit_bytes=VMEM_BYTES),
        cost_estimate=pl.CostEstimate(flops=4_000_000_000, bytes_accessed=8_000_000, transcendentals=800_000),
        name="attention",
    )(pos, bias, act_lo, activations, act_hi, w_query, w_key, w_value, w_out, *cots)

    def add(*terms):
        return sum(t.astype(F32) for t in terms)

    dw = add(dw_keep, swap(dw_send, "core")).astype(BF)
    from_lo = shift_open(hi, space, 1)
    from_hi = shift_open(lo, space, -1)
    dw = add(dw[0], *[shift(dw[s], "y", s) for s in (1, 2, 3)]).astype(BF)

    piece = (2, ROW, WIDTH)
    pieces = pl.pallas_call(
        input_kernel,
        out_shape=(jax.ShapeDtypeStruct(piece, F32),) + (jax.ShapeDtypeStruct(piece, BF),) * 3,
        in_specs=smem() + vmem(9),
        out_specs=tuple(vmem(4)),
        compiler_params=pltpu.CompilerParams(vmem_limit_bytes=VMEM_BYTES),
        cost_estimate=pl.CostEstimate(flops=540_000_000, bytes_accessed=4_000_000, transcendentals=0),
        name="input_grad",
    )(pos, att, gq, own, from_lo, from_hi, w_query, w_key, w_value, w_out)
    outs = add(pieces[0], *[shift(pieces[s], "mp", s) for s in (1, 2, 3)]).astype(BF)

    dw = add(dw[1], swap(dw[0], "z")).astype(BF)
    z_count = lax.axis_size("z")
    dw = add(
        dw[0],
        *[
            lax.ppermute(dw[s], "z", [(i, (i + 2 * s) % z_count) for i in range(z_count)])
            for s in (1, 2, 3)
        ],
    )
    return outs[0], outs[1], dw


def solution(mesh):
    fine = Mesh(mesh.devices.reshape(8, 4, 2, 4), ("z", "y", "core", "mp"))
    space = ("z", "y", "core")
    in_specs = (
        P(space, None),
        P(None, "mp"),
        P(None, "mp"),
        P(None, "mp"),
        P("mp", None),
        P(space, "mp"),
        P(space, None),
        P(space, None),
    )
    out_specs = (P(space, "mp"), P(space, "mp"), P(None, space, "mp"))
    return jax.shard_map(body, mesh=fine, in_specs=in_specs, out_specs=out_specs, check_vma=False)
```

```python
import jax
import jax.numpy as jnp
from jax import lax
from jax.experimental import pallas as pl
from jax.experimental.pallas import tpu as pltpu
from jax.sharding import Mesh
from jax.sharding import PartitionSpec as P

HD = 64
PATCH = 64
D = 1024
ROW = 256
WIDTH = 256
HEADS = WIDTH // HD
KEYS = 3 * ROW
LOG2E = 1.4426950408889634
BF = jnp.bfloat16
F32 = jnp.float32
SPACE = ("z", "y", "core")

NN = (((1,), (0,)), ((), ()))
NT = (((1,), (1,)), ((), ()))


def mm(a, b, dims=NN):
    return lax.dot_general(a, b, dims, preferred_element_type=F32)


def places():
    return [lax.axis_index(a) for a in ("core", "y", "z", "mp")]


def slot_bias(nb, mask, core, y, z):
    row = (z * 4 + y) * 2 + core
    sign = 1 - 2 * core
    patch_of_lane = lax.broadcasted_iota(jnp.int32, (16, ROW), 1) // PATCH
    patch_of_row = lax.broadcasted_iota(jnp.int32, (16, ROW), 0)
    count = jnp.zeros((16, ROW), F32)
    for slot in range(9):
        named = jnp.zeros((16, ROW), jnp.int32)
        for patch in range(4):
            number = nb[patch, slot]
            band = 1 + sign * (lax.div(number, 4) - row)
            place = jnp.where(mask[patch, slot] > 0, band * 4 + lax.rem(number, 4), -1)
            named = jnp.where(patch_of_lane == patch, place, named)
        count += jnp.where(named == patch_of_row, 1.0, 0.0)
    return jnp.where(count > 0, jnp.where(count > 1, jnp.log(count) * LOG2E, 0.0), -1e30)


def columns(ref, x, step):
    return ref[:, pl.ds(pl.multiple_of(lax.rem(x + step, 4) * WIDTH, WIDTH), WIDTH)]


def own_kernel(
    act, w_q, w_k, w_v, w_o, cot, slots, live,
    wq, wk, wv, wo, query_out, key_out, value_out, act_t, grad_out, cot_t, bias_out,
    act_s, cot_s, nb, mask, sems,
):
    core, y, z, x = places()
    pairs = (
        (act, act_s), (w_q, wq), (w_k, wk), (w_v, wv), (cot, cot_s), (w_o, wo), (slots, nb), (live, mask)
    )
    copies = [pltpu.make_async_copy(a, b, sems.at[i]) for i, (a, b) in enumerate(pairs)]
    for copy in copies:
        copy.start()
    copies[0].wait()
    act_t[...] = act_s[...].T
    for index, weight, out in ((1, wq, query_out), (2, wk, key_out), (3, wv, value_out)):
        copies[index].wait()
        out[...] = mm(act_s[...], weight[...]).astype(BF)
    copies[4].wait()
    cot_t[...] = cot_s[...].T
    copies[5].wait()
    grad_out[...] = mm(cot_s[...], columns(wo, x, 0), NT)
    copies[6].wait()
    copies[7].wait()
    bias_out[...] = slot_bias(nb, mask, core, y, z)


def attention_kernel(
    a_far, a_near, wk, wv, wo, query_in, key_own, value_own, act_t, grad_in, cot_t, bias, c1, c2, c3,
    att_out, gq_out, far_out, own_out, send_out, keep_out,
    key_s, value_s, dw_s,
):
    core, y, z, x = places()
    query = query_in[...]
    key_s[ROW : 2 * ROW, :] = key_own[...]
    value_s[ROW : 2 * ROW, :] = value_own[...]
    for band, block in ((0, a_far), (2, a_near)):
        rows = slice(band * ROW, (band + 1) * ROW)
        key_s[rows, :] = mm(block[...], wk[...]).astype(BF)
        value_s[rows, :] = mm(block[...], wv[...]).astype(BF)
    grad_att = grad_in[...]
    for step, block in ((3, c1), (2, c2), (1, c3)):
        grad_att += mm(block[...], columns(wo, x, step), NT)
    grad_att = grad_att.astype(BF)

    keys = key_s[...]
    values = value_s[...]
    keys_t = keys.T
    values_t = values.T
    lane_head = lax.broadcasted_iota(jnp.int32, (ROW, WIDTH), 1) // HD
    bias_rows = jnp.concatenate(
        [jnp.broadcast_to(bias[patch : patch + 1, :], (PATCH, ROW)) for patch in range(KEYS // PATCH)],
        axis=0,
    )
    grad_key = jnp.zeros((KEYS, WIDTH), F32)
    grad_value = jnp.zeros((KEYS, WIDTH), F32)
    att_rows, gq_rows = [], []
    for head in range(HEADS):
        feats = slice(head * HD, (head + 1) * HD)
        q_head = jnp.where(lane_head == head, query, jnp.zeros_like(query))
        g_head = jnp.where(lane_head == head, grad_att, jnp.zeros_like(grad_att))
        scores = mm(keys, q_head, NT) * (LOG2E * HD**-0.5) + bias_rows
        peak = jnp.max(scores, axis=0, keepdims=True)
        weights = jnp.exp2(scores - peak)
        probs = weights * (1.0 / jnp.sum(weights, axis=0, keepdims=True))
        probs_low = probs.astype(BF)
        grad_probs = mm(values, g_head, NT)
        centre = jnp.sum(probs * grad_probs, axis=0, keepdims=True)
        grad_scores = (probs * (grad_probs - centre) * HD**-0.5).astype(BF)
        att_rows.append(mm(values_t[feats, :], probs_low))
        gq_rows.append(mm(keys_t[feats, :], grad_scores))
        grad_key += mm(grad_scores, q_head)
        grad_value += mm(probs_low, g_head)
    att = jnp.concatenate(att_rows, axis=0).astype(BF).T
    gq = jnp.concatenate(gq_rows, axis=0).astype(BF).T
    att_out[...] = att
    gq_out[...] = gq
    far_out[0], far_out[1] = grad_key[:ROW].astype(BF), grad_value[:ROW].astype(BF)
    own_out[0], own_out[1] = grad_key[ROW : 2 * ROW], grad_value[ROW : 2 * ROW]
    for part, grad in enumerate((grad_key, grad_value)):
        for block in range(16):
            rows = slice(2 * ROW + 16 * block, 2 * ROW + 16 * (block + 1))
            send_out[128 + 16 * part + block] = grad[rows].astype(BF)

    grad_key = grad_key.astype(BF)
    grad_value = grad_value.astype(BF)
    own = slice(ROW, 2 * ROW)
    far_t, near_t = a_far[...].T, a_near[...].T
    dw_s[0] = mm(act_t[...], gq)
    for index, grad in ((1, grad_key), (2, grad_value)):
        dw_s[index] = (
            mm(act_t[...], grad[own]) + mm(far_t, grad[:ROW]) + mm(near_t, grad[2 * ROW :])
        )
    for step, block_t in ((0, cot_t[...]), (3, c1[...].T), (2, c2[...].T), (1, c3[...].T)):
        rows = pl.ds(pl.multiple_of(lax.rem(x + step, 4) * WIDTH, WIDTH), WIDTH)
        dw_s[3, rows, :] = mm(block_t, att)
    for mine, out in ((0, send_out), (1, keep_out)):
        c = core if mine else 1 - core
        for ys in range(4):
            yy = lax.rem(y + ys, 4)
            for low in range(2):
                for hs in range(4):
                    zl = lax.rem(z, 2)
                    zl = zl if low else 1 - zl
                    zz = 2 * lax.rem(z // 2 + hs, 4) + zl
                    row = pl.multiple_of(((zz * 4 + yy) * 2 + c) * 16, 16)
                    block = ((ys * 2 + low) * 4 + hs) * 4
                    out[block : block + 4] = dw_s[:, pl.ds(row, 16), :].astype(BF)


def core_sum_kernel(keep, got, o0, o1, o2, o3):
    for step, out in enumerate((o0, o1, o2, o3)):
        part = slice(32 * step, 32 * (step + 1))
        out[...] = (keep[part].astype(F32) + got[part].astype(F32)).astype(out.dtype)


def input_kernel(att, gq, own, near, far, wq, wk, wv, wo, p0, p1, p2, p3):
    x = places()[3]
    grads = []
    for part in range(2):
        from_near = near[128 + 16 * part : 144 + 16 * part].reshape(ROW, WIDTH)
        grads.append((own[part] + from_near.astype(F32) + far[part].astype(F32)).astype(BF))
    grad_key, grad_value = grads
    for step, out in enumerate((p0, p1, p2, p3)):
        block = pl.ds(pl.multiple_of(lax.rem(x + step, 4) * WIDTH, WIDTH), WIDTH)
        out[0] = mm(att[...], wo[:, block]).astype(out.dtype)
        out[1] = (
            mm(gq[...], wq[block, :], NT)
            + mm(grad_key, wk[block, :], NT)
            + mm(grad_value, wv[block, :], NT)
        ).astype(out.dtype)


def y_sum_kernel(a, b, c, d, send, keep):
    for part, out in ((slice(0, 16), send), (slice(16, 32), keep)):
        total = (a[part].astype(F32) + b[part].astype(F32)) + (c[part].astype(F32) + d[part].astype(F32))
        out[...] = total.astype(out.dtype)


def pair_sum_kernel(keep, got, o0, o1, o2, o3):
    for step, out in enumerate((o0, o1, o2, o3)):
        part = slice(4 * step, 4 * (step + 1))
        out[...] = (keep[part].astype(F32) + got[part].astype(F32)).astype(out.dtype)


def last_sum_kernel(d0, d1, d2, d3, p0, p1, p2, p3, out, grad, dw):
    dw[...] = (d0[...] + d1[...].astype(F32)) + (d2[...].astype(F32) + d3[...].astype(F32))
    for part, ref in ((0, out), (1, grad)):
        total = (p0[part] + p1[part].astype(F32)) + (p2[part].astype(F32) + p3[part].astype(F32))
        ref[...] = total.astype(BF)


def on_chip(*arrays):
    return [pltpu.with_memory_space_constraint(a, pltpu.VMEM) for a in arrays]


def call(
    kernel, name, outs, arrays, apart=(), scratch=(), limit=16, flops=0, moved=1_000_000, keep=True
):
    kept = [pltpu.VMEM(shape, dtype) if keep else jax.ShapeDtypeStruct(shape, dtype) for shape, dtype in outs]
    return pl.pallas_call(
        kernel,
        out_shape=tuple(kept),
        in_specs=[pl.BlockSpec(memory_space=pltpu.HBM)] * len(apart)
        + [pl.BlockSpec(memory_space=pltpu.VMEM)] * len(arrays),
        out_specs=(pl.BlockSpec(memory_space=pltpu.VMEM),) * len(kept),
        scratch_shapes=list(scratch),
        compiler_params=pltpu.CompilerParams(vmem_limit_bytes=limit * 1024 * 1024),
        cost_estimate=pl.CostEstimate(flops=flops, bytes_accessed=moved, transcendentals=0),
        name=name,
    )(*[pltpu.with_memory_space_constraint(a, pltpu.HBM) for a in apart], *on_chip(*arrays))


def move(value, axis, target):
    count = lax.axis_size(axis)
    return lax.ppermute(
        value, axis, [(i, target(i)) for i in range(count) if 0 <= target(i) < count]
    )


def ring(value, axis, steps):
    count = lax.axis_size(axis)
    return move(value, axis, lambda i: (i + steps) % count)


def near_row(value):
    return move(value, SPACE, lambda i: i ^ 1)


def far_row(value):
    return move(value, SPACE, lambda i: i + 1 if i % 2 else i - 1)


def body(activations, w_query, w_key, w_value, w_out, grad_output, neighbours, pad_mask):
    act_far = far_row(activations)
    cots = [ring(grad_output, "mp", s) for s in (1, 2, 3)]
    act_near = near_row(activations)

    square = (ROW, WIDTH)
    wq, wk, wv, wo, *own_parts = call(
        own_kernel,
        "own_part",
        [((D, WIDTH), BF)] * 3 + [((WIDTH, D), BF)]
        + [(square, BF)] * 3 + [((D, ROW), BF), (square, F32), (square, BF), ((16, ROW), F32)],
        [],
        apart=(activations, w_query, w_key, w_value, w_out, grad_output, neighbours, pad_mask),
        scratch=[
            pltpu.VMEM((ROW, D), BF),
            pltpu.VMEM(square, BF),
            pltpu.SMEM((4, 9), jnp.int32),
            pltpu.SMEM((4, 9), jnp.int32),
            pltpu.SemaphoreType.DMA((8,)),
        ],
        flops=600_000_000,
        moved=6_000_000,
    )

    block = (16, WIDTH)
    att, gq, far, own, dw_send, dw_keep = call(
        attention_kernel,
        "attention",
        [
            (square, BF),
            (square, BF),
            ((2, ROW, WIDTH), BF),
            ((2, ROW, WIDTH), F32),
            ((160,) + block, BF),
            ((128,) + block, BF),
        ],
        [act_far, act_near, wk, wv, wo, *own_parts, *cots],
        scratch=[
            pltpu.VMEM((KEYS, WIDTH), BF),
            pltpu.VMEM((KEYS, WIDTH), BF),
            pltpu.VMEM((4, D, WIDTH), F32),
        ],
        limit=32,
        flops=4_000_000_000,
        moved=8_000_000,
    )

    got = near_row(dw_send)
    grad_far = far_row(far)
    dw = call(core_sum_kernel, "core_sum", [((32,) + block, BF)] * 4, [dw_keep, got])
    dw_y = [dw[0]] + [ring(dw[s], "y", s) for s in (1, 2, 3)]

    piece = (2, ROW, WIDTH)
    pieces = call(
        input_kernel,
        "input_grad",
        [(piece, F32)] + [(piece, BF)] * 3,
        [att, gq, own, got, grad_far, wq, wk, wv, wo],
        flops=540_000_000,
        moved=4_000_000,
    )
    outs = [pieces[0]] + [ring(pieces[s], "mp", s) for s in (1, 2, 3)]

    send, keep = call(y_sum_kernel, "y_sum", [((16,) + block, BF)] * 2, dw_y)
    pair = move(send, "z", lambda i: i ^ 1)
    dw = call(
        pair_sum_kernel, "pair_sum", [((4,) + block, F32)] + [((4,) + block, BF)] * 3, [keep, pair]
    )
    dw_z = [dw[0]] + [ring(dw[s], "z", 2 * s) for s in (1, 2, 3)]
    return call(
        last_sum_kernel,
        "last_sum",
        [((ROW, WIDTH), BF), ((ROW, WIDTH), BF), ((4,) + block, F32)],
        dw_z + outs,
        keep=False,
    )


def solution(mesh):
    fine = Mesh(mesh.devices.reshape(8, 4, 2, 4), SPACE + ("mp",))
    in_specs = (
        P(SPACE, None),
        P(None, "mp"),
        P(None, "mp"),
        P(None, "mp"),
        P("mp", None),
        P(SPACE, "mp"),
        P(SPACE, None),
        P(SPACE, None),
    )
    out_specs = (P(SPACE, "mp"), P(SPACE, "mp"), P(None, SPACE, "mp"))
    return jax.shard_map(body, mesh=fine, in_specs=in_specs, out_specs=out_specs, check_vma=False)
```

```python
import jax
import jax.numpy as jnp
from jax import lax
from jax.experimental import pallas as pl
from jax.experimental.pallas import tpu as pltpu
from jax.sharding import Mesh
from jax.sharding import PartitionSpec as P

HD = 64
PATCH = 64
D = 1024
ROW = 256
WIDTH = 256
HEADS = WIDTH // HD
KEYS = 3 * ROW
LOG2E = 1.4426950408889634
BF = jnp.bfloat16
F32 = jnp.float32
SPACE = ("z", "y", "core")

NN = (((1,), (0,)), ((), ()))
NT = (((1,), (1,)), ((), ()))


def mm(a, b, dims=NN):
    return lax.dot_general(a, b, dims, preferred_element_type=F32)


def places():
    return [lax.axis_index(a) for a in ("core", "y", "z", "mp")]


def slot_bias(nb, mask, core, y, z):
    row = (z * 4 + y) * 2 + core
    sign = 1 - 2 * core
    patch_of_lane = lax.broadcasted_iota(jnp.int32, (16, ROW), 1) // PATCH
    patch_of_row = lax.broadcasted_iota(jnp.int32, (16, ROW), 0)
    count = jnp.zeros((16, ROW), F32)
    for slot in range(9):
        named = jnp.zeros((16, ROW), jnp.int32)
        for patch in range(4):
            number = nb[patch, slot]
            band = 1 + sign * (lax.div(number, 4) - row)
            place = jnp.where(mask[patch, slot] > 0, band * 4 + lax.rem(number, 4), -1)
            named = jnp.where(patch_of_lane == patch, place, named)
        count += jnp.where(named == patch_of_row, 1.0, 0.0)
    return jnp.where(count > 0, jnp.where(count > 1, jnp.log(count) * LOG2E, 0.0), -1e30)


def y_pair(y):
    return y + 1 - 2 * (y % 2)


def y_other(y):
    return 3 - y


def z_pair(z):
    return z + 1 - 2 * (z % 2)


def z_other(z):
    return (z + 7 + 2 * (z % 2)) % 8


def z_far(z):
    ends = (z % 4) * (3 - z % 4) // 2
    return (1 - ends) * (3 - 2 * (z % 4) + z) + ends * (7 - z)


def target_row(y, z, y_bits, z_bits):
    for bit, partner in zip(y_bits, (y_pair, y_other)):
        y = partner(y) if bit else y
    for bit, partner in zip(z_bits, (z_pair, z_other, z_far)):
        z = partner(z) if bit else z
    return z * 4 + y


def columns(ref, x, step):
    return ref[:, pl.ds(pl.multiple_of((x ^ step) * WIDTH, WIDTH), WIDTH)]


def own_kernel(
    act, w_q, w_k, w_v, w_o, cot, slots, live,
    wq, wk, wv, wo, query_out, key_out, value_out, act_t, grad_out, cot_t, bias_out,
    act_s, cot_s, nb, mask, sems,
):
    core, y, z, x = places()
    pairs = (
        (act, act_s), (w_q, wq), (w_k, wk), (w_v, wv), (cot, cot_s), (w_o, wo), (slots, nb), (live, mask)
    )
    copies = [pltpu.make_async_copy(a, b, sems.at[i]) for i, (a, b) in enumerate(pairs)]
    for copy in copies:
        copy.start()
    copies[0].wait()
    act_t[...] = act_s[...].T
    for index, weight, out in ((1, wq, query_out), (2, wk, key_out), (3, wv, value_out)):
        copies[index].wait()
        out[...] = mm(act_s[...], weight[...]).astype(BF)
    copies[4].wait()
    cot_t[...] = cot_s[...].T
    copies[5].wait()
    grad_out[...] = mm(cot_s[...], columns(wo, x, 0), NT)
    copies[6].wait()
    copies[7].wait()
    bias_out[...] = slot_bias(nb, mask, core, y, z)


def attention_kernel(
    a_far, a_near, wk, wv, wo, query_in, key_own, value_own, act_t, grad_in, cot_t, bias, c1, c2, c3,
    att_out, gq_out, far_out, own_out, send_out, keep_out,
    key_s, value_s, dw_s,
):
    core, y, z, x = places()
    query = query_in[...]
    key_s[ROW : 2 * ROW, :] = key_own[...]
    value_s[ROW : 2 * ROW, :] = value_own[...]
    for band, block in ((0, a_far), (2, a_near)):
        rows = slice(band * ROW, (band + 1) * ROW)
        key_s[rows, :] = mm(block[...], wk[...]).astype(BF)
        value_s[rows, :] = mm(block[...], wv[...]).astype(BF)
    grad_att = grad_in[...]
    for step, block in ((1, c1), (2, c2), (3, c3)):
        grad_att += mm(block[...], columns(wo, x, step), NT)
    grad_att = grad_att.astype(BF)

    keys = key_s[...]
    values = value_s[...]
    keys_t = keys.T
    values_t = values.T
    lane_head = lax.broadcasted_iota(jnp.int32, (ROW, WIDTH), 1) // HD
    bias_rows = jnp.concatenate(
        [jnp.broadcast_to(bias[patch : patch + 1, :], (PATCH, ROW)) for patch in range(KEYS // PATCH)],
        axis=0,
    )
    grad_key = jnp.zeros((KEYS, WIDTH), F32)
    grad_value = jnp.zeros((KEYS, WIDTH), F32)
    att_rows, gq_rows = [], []
    for head in range(HEADS):
        feats = slice(head * HD, (head + 1) * HD)
        q_head = jnp.where(lane_head == head, query, jnp.zeros_like(query))
        g_head = jnp.where(lane_head == head, grad_att, jnp.zeros_like(grad_att))
        scores = mm(keys, q_head, NT) * (LOG2E * HD**-0.5) + bias_rows
        peak = jnp.max(scores, axis=0, keepdims=True)
        weights = jnp.exp2(scores - peak)
        probs = weights * (1.0 / jnp.sum(weights, axis=0, keepdims=True))
        probs_low = probs.astype(BF)
        grad_probs = mm(values, g_head, NT)
        centre = jnp.sum(probs * grad_probs, axis=0, keepdims=True)
        grad_scores = (probs * (grad_probs - centre) * HD**-0.5).astype(BF)
        att_rows.append(mm(values_t[feats, :], probs_low))
        gq_rows.append(mm(keys_t[feats, :], grad_scores))
        grad_key += mm(grad_scores, q_head)
        grad_value += mm(probs_low, g_head)
    att = jnp.concatenate(att_rows, axis=0).astype(BF).T
    gq = jnp.concatenate(gq_rows, axis=0).astype(BF).T
    att_out[...] = att
    gq_out[...] = gq
    far_out[0], far_out[1] = grad_key[:ROW].astype(BF), grad_value[:ROW].astype(BF)
    own_out[0], own_out[1] = grad_key[ROW : 2 * ROW], grad_value[ROW : 2 * ROW]
    for part, grad in enumerate((grad_key, grad_value)):
        for block in range(16):
            rows = slice(2 * ROW + 16 * block, 2 * ROW + 16 * (block + 1))
            send_out[128 + 16 * part + block] = grad[rows].astype(BF)

    grad_key = grad_key.astype(BF)
    grad_value = grad_value.astype(BF)
    own = slice(ROW, 2 * ROW)
    far_t, near_t = a_far[...].T, a_near[...].T
    dw_s[0] = mm(act_t[...], gq)
    for index, grad in ((1, grad_key), (2, grad_value)):
        dw_s[index] = (
            mm(act_t[...], grad[own]) + mm(far_t, grad[:ROW]) + mm(near_t, grad[2 * ROW :])
        )
    for step, block_t in ((0, cot_t[...]), (1, c1[...].T), (2, c2[...].T), (3, c3[...].T)):
        rows = pl.ds(pl.multiple_of((x ^ step) * WIDTH, WIDTH), WIDTH)
        dw_s[3, rows, :] = mm(block_t, att)
    for c, out in ((1 - core, send_out), (core, keep_out)):
        for path in range(32):
            s1, s2, s3, s4, s5 = ((path >> (4 - step)) & 1 for step in range(5))
            y_first = target_row(y, z, (s1, s3), (s2, s4, s5))
            z_first = target_row(y, z, (s2, s4), (s1, s3, s5))
            row = jnp.where(c == 0, y_first, z_first) * 32 + c * 16
            out[4 * path : 4 * path + 4] = dw_s[:, pl.ds(pl.multiple_of(row, 16), 16), :].astype(BF)


def halve_kernel(kept, got, send, keep):
    half = send.shape[0]
    for part, out in ((slice(0, half), keep), (slice(half, 2 * half), send)):
        out[...] = (kept[part].astype(F32) + got[part].astype(F32)).astype(out.dtype)


def input_kernel(att, gq, own, near, far, wq, wk, wv, wo, p0, p1, p2, p3):
    x = places()[3]
    grads = []
    for part in range(2):
        from_near = near[128 + 16 * part : 144 + 16 * part].reshape(ROW, WIDTH)
        grads.append((own[part] + from_near.astype(F32) + far[part].astype(F32)).astype(BF))
    grad_key, grad_value = grads
    for step, out in enumerate((p0, p1, p2, p3)):
        block = pl.ds(pl.multiple_of((x ^ step) * WIDTH, WIDTH), WIDTH)
        out[0] = mm(att[...], wo[:, block]).astype(out.dtype)
        out[1] = (
            mm(gq[...], wq[block, :], NT)
            + mm(grad_key, wk[block, :], NT)
            + mm(grad_value, wv[block, :], NT)
        ).astype(out.dtype)


def last_sum_kernel(kept, got, p0, p1, p2, p3, out, grad, dw):
    dw[...] = kept[...] + got[...].astype(F32)
    for part, ref in ((0, out), (1, grad)):
        total = (p0[part] + p1[part].astype(F32)) + (p2[part].astype(F32) + p3[part].astype(F32))
        ref[...] = total.astype(BF)


def on_chip(*arrays):
    return [pltpu.with_memory_space_constraint(a, pltpu.VMEM) for a in arrays]


def call(
    kernel, name, outs, arrays, apart=(), scratch=(), limit=16, flops=0, moved=1_000_000, keep=True
):
    kept = [pltpu.VMEM(shape, dtype) if keep else jax.ShapeDtypeStruct(shape, dtype) for shape, dtype in outs]
    return pl.pallas_call(
        kernel,
        out_shape=tuple(kept),
        in_specs=[pl.BlockSpec(memory_space=pltpu.HBM)] * len(apart)
        + [pl.BlockSpec(memory_space=pltpu.VMEM)] * len(arrays),
        out_specs=(pl.BlockSpec(memory_space=pltpu.VMEM),) * len(kept),
        scratch_shapes=list(scratch),
        compiler_params=pltpu.CompilerParams(vmem_limit_bytes=limit * 1024 * 1024),
        cost_estimate=pl.CostEstimate(flops=flops, bytes_accessed=moved, transcendentals=0),
        name=name,
    )(*[pltpu.with_memory_space_constraint(a, pltpu.HBM) for a in apart], *on_chip(*arrays))


def move(value, axis, target):
    count = lax.axis_size(axis)
    return lax.ppermute(
        value, axis, [(i, target(i)) for i in range(count) if 0 <= target(i) < count]
    )


def across(value, step):
    return move(value, "mp", lambda i: i ^ step)


def near_row(value):
    return move(value, SPACE, lambda i: i ^ 1)


def far_row(value):
    return move(value, SPACE, lambda i: i + 1 if i % 2 else i - 1)


def body(activations, w_query, w_key, w_value, w_out, grad_output, neighbours, pad_mask):
    act_far = far_row(activations)
    cots = [across(grad_output, s) for s in (1, 2, 3)]
    act_near = near_row(activations)

    square = (ROW, WIDTH)
    wq, wk, wv, wo, *own_parts = call(
        own_kernel,
        "own_part",
        [((D, WIDTH), BF)] * 3 + [((WIDTH, D), BF)]
        + [(square, BF)] * 3 + [((D, ROW), BF), (square, F32), (square, BF), ((16, ROW), F32)],
        [],
        apart=(activations, w_query, w_key, w_value, w_out, grad_output, neighbours, pad_mask),
        scratch=[
            pltpu.VMEM((ROW, D), BF),
            pltpu.VMEM(square, BF),
            pltpu.SMEM((4, 9), jnp.int32),
            pltpu.SMEM((4, 9), jnp.int32),
            pltpu.SemaphoreType.DMA((8,)),
        ],
        flops=600_000_000,
        moved=6_000_000,
    )

    block = (16, WIDTH)
    att, gq, far, own, dw_send, dw_keep = call(
        attention_kernel,
        "attention",
        [
            (square, BF),
            (square, BF),
            ((2, ROW, WIDTH), BF),
            ((2, ROW, WIDTH), F32),
            ((160,) + block, BF),
            ((128,) + block, BF),
        ],
        [act_far, act_near, wk, wv, wo, *own_parts, *cots],
        scratch=[
            pltpu.VMEM((KEYS, WIDTH), BF),
            pltpu.VMEM((KEYS, WIDTH), BF),
            pltpu.VMEM((4, D, WIDTH), F32),
        ],
        limit=32,
        flops=4_000_000_000,
        moved=8_000_000,
    )

    def halve(kept, got, kept_as):
        half = (kept.shape[0] // 2,) + block
        return call(halve_kernel, "halve", [(half, BF), (half, kept_as)], [kept, got])

    def over_chips(value, core0, core1):
        def target(i):
            z, y, c = i // 8, i // 2 % 4, i % 2
            return ((core0, core1)[c](z, y)) * 2 + c

        return move(value, SPACE, target)

    def along_y(partner):
        return lambda z, y: z * 4 + partner(y)

    def along_z(partner):
        return lambda z, y: partner(z) * 4 + y

    steps = (
        (along_y(y_pair), along_z(z_pair)),
        (along_z(z_pair), along_y(y_pair)),
        (along_y(y_other), along_z(z_other)),
        (along_z(z_other), along_y(y_other)),
        (along_z(z_far), along_z(z_far)),
    )
    got = near_row(dw_send)
    grad_far = far_row(far)
    send, keep = halve(dw_keep, got, BF)
    arrived = over_chips(send, *steps[0])

    piece = (2, ROW, WIDTH)
    pieces = call(
        input_kernel,
        "input_grad",
        [(piece, F32)] + [(piece, BF)] * 3,
        [att, gq, own, got, grad_far, wq, wk, wv, wo],
        flops=540_000_000,
        moved=4_000_000,
    )
    outs = [pieces[0]] + [across(pieces[s], s) for s in (1, 2, 3)]

    for step in steps[1:]:
        send, keep = halve(keep, arrived, F32)
        arrived = over_chips(send, *step)
    return call(
        last_sum_kernel,
        "last_sum",
        [(square, BF), (square, BF), ((4,) + block, F32)],
        [keep, arrived] + outs,
        keep=False,
    )


def solution(mesh):
    fine = Mesh(mesh.devices.reshape(8, 4, 2, 4), SPACE + ("mp",))
    in_specs = (
        P(SPACE, None),
        P(None, "mp"),
        P(None, "mp"),
        P(None, "mp"),
        P("mp", None),
        P(SPACE, "mp"),
        P(SPACE, None),
        P(SPACE, None),
    )
    out_specs = (P(SPACE, "mp"), P(SPACE, "mp"), P(None, SPACE, "mp"))
    return jax.shard_map(body, mesh=fine, in_specs=in_specs, out_specs=out_specs, check_vma=False)
```

```python
import jax
import jax.numpy as jnp
from jax import lax
from jax.experimental import pallas as pl
from jax.experimental.pallas import tpu as pltpu
from jax.sharding import Mesh
from jax.sharding import PartitionSpec as P

HD = 64
PATCH = 64
D = 1024
ROW = 256
WIDTH = 256
HEADS = WIDTH // HD
KEYS = 3 * ROW
LOG2E = 1.4426950408889634
BF = jnp.bfloat16
F32 = jnp.float32
SPACE = ("z", "y", "core")

NN = (((1,), (0,)), ((), ()))
NT = (((1,), (1,)), ((), ()))


def mm(a, b, dims=NN):
    return lax.dot_general(a, b, dims, preferred_element_type=F32)


def places():
    return [lax.axis_index(a) for a in ("core", "y", "z", "mp")]


def slot_bias(nb, mask, core, y, z):
    row = (z * 4 + y) * 2 + core
    sign = 1 - 2 * core
    patch_of_lane = lax.broadcasted_iota(jnp.int32, (16, ROW), 1) // PATCH
    patch_of_row = lax.broadcasted_iota(jnp.int32, (16, ROW), 0)
    count = jnp.zeros((16, ROW), F32)
    for slot in range(9):
        named = jnp.zeros((16, ROW), jnp.int32)
        for patch in range(4):
            number = nb[patch, slot]
            band = 1 + sign * (lax.div(number, 4) - row)
            place = jnp.where(mask[patch, slot] > 0, band * 4 + lax.rem(number, 4), -1)
            named = jnp.where(patch_of_lane == patch, place, named)
        count += jnp.where(named == patch_of_row, 1.0, 0.0)
    return jnp.where(count > 0, jnp.where(count > 1, jnp.log(count) * LOG2E, 0.0), -1e30)


def y_pair(y):
    return y + 1 - 2 * (y % 2)


def y_other(y):
    return 3 - y


def z_pair(z):
    return z + 1 - 2 * (z % 2)


def z_other(z):
    return (z + 7 + 2 * (z % 2)) % 8


def z_far(z):
    middle = (z % 4) * (3 - z % 4) // 2
    return (1 - middle) * (3 - 2 * (z % 4) + z) + middle * (7 - z)


def z_far_too(z):
    return z + 4 + (1 - 2 * (z % 2)) - 8 * (z // 4)


def target_row(z, y, path, core, stream):
    s1, s2, s3, s4, s5 = path
    first, second = (s1, s2) if stream == core else (s2, s1)
    if core == 0:
        y_steps, z_steps = ((y_pair, first), (y_other, s3)), ((z_other, second), (z_pair, s4), (z_far_too, s5))
    else:
        y_steps, z_steps = ((y_other, first), (y_pair, s4)), ((z_pair, second), (z_other, s3), (z_far, s5))
    for partner, sent in y_steps:
        y = partner(y) if sent else y
    for partner, sent in z_steps:
        z = partner(z) if sent else z
    return z * 4 + y


def columns(ref, x, step):
    return ref[:, pl.ds(pl.multiple_of((x ^ step) * WIDTH, WIDTH), WIDTH)]


def own_kernel(
    act, w_q, w_k, w_v, w_o, cot, slots, live,
    wq, wk, wv, wo, query_out, key_out, value_out, act_t, grad_out, cot_t, bias_out,
    act_s, cot_s, nb, mask, sems,
):
    core, y, z, x = places()
    pairs = (
        (act, act_s), (w_q, wq), (w_k, wk), (w_v, wv), (cot, cot_s), (w_o, wo), (slots, nb), (live, mask)
    )
    copies = [pltpu.make_async_copy(a, b, sems.at[i]) for i, (a, b) in enumerate(pairs)]
    for copy in copies:
        copy.start()
    copies[0].wait()
    act_t[...] = act_s[...].T
    for index, weight, out in ((1, wq, query_out), (2, wk, key_out), (3, wv, value_out)):
        copies[index].wait()
        out[...] = mm(act_s[...], weight[...]).astype(BF)
    copies[4].wait()
    cot_t[...] = cot_s[...].T
    copies[5].wait()
    grad_out[...] = mm(cot_s[...], columns(wo, x, 0), NT)
    copies[6].wait()
    copies[7].wait()
    bias_out[...] = slot_bias(nb, mask, core, y, z)


def forward_kernel(
    a_far, a_near, wk, wv, query, key_own, value_own, bias,
    keys, values, probs_out, att_out, far_t, near_t,
):
    keys[ROW : 2 * ROW, :] = key_own[...]
    values[ROW : 2 * ROW, :] = value_own[...]
    for band, block in ((0, a_far), (2, a_near)):
        rows = slice(band * ROW, (band + 1) * ROW)
        keys[rows, :] = mm(block[...], wk[...]).astype(BF)
        values[rows, :] = mm(block[...], wv[...]).astype(BF)
    values_t = values[...].T
    lane_head = lax.broadcasted_iota(jnp.int32, (ROW, WIDTH), 1) // HD
    bias_rows = jnp.concatenate(
        [jnp.broadcast_to(bias[patch : patch + 1, :], (PATCH, ROW)) for patch in range(KEYS // PATCH)],
        axis=0,
    )
    att_rows = []
    for head in range(HEADS):
        feats = slice(head * HD, (head + 1) * HD)
        q_head = jnp.where(lane_head == head, query[...], jnp.zeros((ROW, WIDTH), BF))
        scores = mm(keys[...], q_head, NT) * (LOG2E * HD**-0.5) + bias_rows
        peak = jnp.max(scores, axis=0, keepdims=True)
        weights = jnp.exp2(scores - peak)
        probs = weights * (1.0 / jnp.sum(weights, axis=0, keepdims=True))
        probs_out[head] = probs
        att_rows.append(mm(values_t[feats, :], probs.astype(BF)))
    att_out[...] = jnp.concatenate(att_rows, axis=0).astype(BF).T
    far_t[...] = a_far[...].T
    near_t[...] = a_near[...].T


def backward_kernel(
    keys, values, probs_in, att, far_t, near_t, wo, query, act_t, grad_in, cot_t, c1, c2, c3,
    gq_out, far_out, own_out, send_out, keep_out,
    dw_s,
):
    core, y, z, x = places()
    grad_att = grad_in[...]
    for step, block in ((1, c1), (2, c2), (3, c3)):
        grad_att += mm(block[...], columns(wo, x, step), NT)
    grad_att = grad_att.astype(BF)
    for step, block_t in ((0, cot_t[...]), (1, c1[...].T), (2, c2[...].T), (3, c3[...].T)):
        rows = pl.ds(pl.multiple_of((x ^ step) * WIDTH, WIDTH), WIDTH)
        dw_s[3, rows, :] = mm(block_t, att[...])

    keys_t = keys[...].T
    lane_head = lax.broadcasted_iota(jnp.int32, (ROW, WIDTH), 1) // HD
    grad_key = jnp.zeros((KEYS, WIDTH), F32)
    grad_value = jnp.zeros((KEYS, WIDTH), F32)
    gq_rows = []
    for head in range(HEADS):
        feats = slice(head * HD, (head + 1) * HD)
        q_head = jnp.where(lane_head == head, query[...], jnp.zeros((ROW, WIDTH), BF))
        g_head = jnp.where(lane_head == head, grad_att, jnp.zeros_like(grad_att))
        probs = probs_in[head]
        grad_probs = mm(values[...], g_head, NT)
        centre = jnp.sum(probs * grad_probs, axis=0, keepdims=True)
        grad_scores = (probs * (grad_probs - centre) * HD**-0.5).astype(BF)
        gq_rows.append(mm(keys_t[feats, :], grad_scores))
        grad_key += mm(grad_scores, q_head)
        grad_value += mm(probs.astype(BF), g_head)
    gq = jnp.concatenate(gq_rows, axis=0).astype(BF).T
    gq_out[...] = gq
    far_out[0], far_out[1] = grad_key[:ROW].astype(BF), grad_value[:ROW].astype(BF)
    own_out[0], own_out[1] = grad_key[ROW : 2 * ROW], grad_value[ROW : 2 * ROW]
    for part, grad in enumerate((grad_key, grad_value)):
        for block in range(16):
            rows = slice(2 * ROW + 16 * block, 2 * ROW + 16 * (block + 1))
            send_out[128 + 16 * part + block] = grad[rows].astype(BF)

    grad_key = grad_key.astype(BF)
    grad_value = grad_value.astype(BF)
    own = slice(ROW, 2 * ROW)
    dw_s[0] = mm(act_t[...], gq)
    for index, grad in ((1, grad_key), (2, grad_value)):
        dw_s[index] = (
            mm(act_t[...], grad[own]) + mm(far_t[...], grad[:ROW]) + mm(near_t[...], grad[2 * ROW :])
        )
    for c, out in ((1 - core, send_out), (core, keep_out)):
        for number in range(32):
            path = [(number >> (4 - step)) & 1 for step in range(5)]
            for stream in range(2):
                row0, row1 = (target_row(z, y, path, which, stream) for which in (0, 1))
                row = pl.multiple_of(jnp.where(c == 0, row0, row1) * 32 + c * 16, 16)
                block = 64 * stream + 2 * number
                out[block : block + 2] = dw_s[2 * stream : 2 * stream + 2, pl.ds(row, 16), :].astype(BF)


def core_sum_kernel(kept, got, send0, keep0, send1, keep1):
    for step, out in enumerate((keep0, send0, keep1, send1)):
        part = slice(32 * step, 32 * (step + 1))
        out[...] = (kept[part].astype(F32) + got[part].astype(F32)).astype(out.dtype)


def halve_kernel(kept, got, send, keep):
    half = send.shape[0]
    for part, out in ((slice(0, half), keep), (slice(half, 2 * half), send)):
        out[...] = (kept[part].astype(F32) + got[part].astype(F32)).astype(out.dtype)


def join_kernel(kept0, got0, kept1, got1, send, keep):
    for start, out in ((0, keep), (8, send)):
        for path in range(4):
            for stream, (kept, got) in enumerate(((kept0, got0), (kept1, got1))):
                here = slice(start + 2 * path, start + 2 * path + 2)
                there = slice(4 * path + 2 * stream, 4 * path + 2 * stream + 2)
                out[there] = (kept[here].astype(F32) + got[here].astype(F32)).astype(out.dtype)


def input_kernel(att, gq, own, near, far, wq, wk, wv, wo, p0, p1, p2, p3):
    x = places()[3]
    grads = []
    for part in range(2):
        from_near = near[128 + 16 * part : 144 + 16 * part].reshape(ROW, WIDTH)
        grads.append((own[part] + from_near.astype(F32) + far[part].astype(F32)).astype(BF))
    grad_key, grad_value = grads
    for step, out in enumerate((p0, p1, p2, p3)):
        block = pl.ds(pl.multiple_of((x ^ step) * WIDTH, WIDTH), WIDTH)
        out[0] = mm(att[...], wo[:, block]).astype(out.dtype)
        out[1] = (
            mm(gq[...], wq[block, :], NT)
            + mm(grad_key, wk[block, :], NT)
            + mm(grad_value, wv[block, :], NT)
        ).astype(out.dtype)


def mp_sum_kernel(p0, p1, p2, p3, out, grad):
    for part, ref in ((0, out), (1, grad)):
        total = (p0[part] + p1[part].astype(F32)) + (p2[part].astype(F32) + p3[part].astype(F32))
        ref[...] = total.astype(BF)


def last_sum_kernel(kept, got, dw):
    dw[...] = kept[...] + got[...].astype(F32)


def on_chip(*arrays):
    return [pltpu.with_memory_space_constraint(a, pltpu.VMEM) for a in arrays]


def call(
    kernel, name, outs, arrays, apart=(), scratch=(), limit=16, flops=0, moved=1_000_000, keep=True
):
    kept = [pltpu.VMEM(shape, dtype) if keep else jax.ShapeDtypeStruct(shape, dtype) for shape, dtype in outs]
    return pl.pallas_call(
        kernel,
        out_shape=tuple(kept),
        in_specs=[pl.BlockSpec(memory_space=pltpu.HBM)] * len(apart)
        + [pl.BlockSpec(memory_space=pltpu.VMEM)] * len(arrays),
        out_specs=(pl.BlockSpec(memory_space=pltpu.VMEM),) * len(kept),
        scratch_shapes=list(scratch),
        compiler_params=pltpu.CompilerParams(vmem_limit_bytes=limit * 1024 * 1024),
        cost_estimate=pl.CostEstimate(flops=flops, bytes_accessed=moved, transcendentals=0),
        name=name,
    )(*[pltpu.with_memory_space_constraint(a, pltpu.HBM) for a in apart], *on_chip(*arrays))


def move(value, axis, target):
    count = lax.axis_size(axis)
    return lax.ppermute(
        value, axis, [(i, target(i)) for i in range(count) if 0 <= target(i) < count]
    )


def across(value, step):
    return move(value, "mp", lambda i: i ^ step)


def near_row(value):
    return move(value, SPACE, lambda i: i ^ 1)


def far_row(value):
    return move(value, SPACE, lambda i: i + 1 if i % 2 else i - 1)


def body(activations, w_query, w_key, w_value, w_out, grad_output, neighbours, pad_mask):
    act_far = far_row(activations)
    cots = [across(grad_output, s) for s in (1, 2, 3)]
    act_near = near_row(activations)

    square = (ROW, WIDTH)
    wq, wk, wv, wo, *own_parts = call(
        own_kernel,
        "own_part",
        [((D, WIDTH), BF)] * 3 + [((WIDTH, D), BF)]
        + [(square, BF)] * 3 + [((D, ROW), BF), (square, F32), (square, BF), ((16, ROW), F32)],
        [],
        apart=(activations, w_query, w_key, w_value, w_out, grad_output, neighbours, pad_mask),
        scratch=[
            pltpu.VMEM((ROW, D), BF),
            pltpu.VMEM(square, BF),
            pltpu.SMEM((4, 9), jnp.int32),
            pltpu.SMEM((4, 9), jnp.int32),
            pltpu.SemaphoreType.DMA((8,)),
        ],
        flops=600_000_000,
        moved=6_000_000,
    )

    block = (16, WIDTH)
    query, key_own, value_own, act_t, grad_own, cot_t, bias = own_parts
    keys, values, probs, att, far_t, near_t = call(
        forward_kernel,
        "forward",
        [((KEYS, WIDTH), BF)] * 2
        + [((HEADS, KEYS, ROW), F32), (square, BF), ((D, ROW), BF), ((D, ROW), BF)],
        [act_far, act_near, wk, wv, query, key_own, value_own, bias],
        limit=20,
        flops=2_000_000_000,
        moved=6_000_000,
    )
    gq, far, own, dw_send, dw_keep = call(
        backward_kernel,
        "backward",
        [
            (square, BF),
            ((2, ROW, WIDTH), BF),
            ((2, ROW, WIDTH), F32),
            ((160,) + block, BF),
            ((128,) + block, BF),
        ],
        [keys, values, probs, att, far_t, near_t, wo, query, act_t, grad_own, cot_t, *cots],
        scratch=[pltpu.VMEM((4, D, WIDTH), F32)],
        limit=24,
        flops=3_000_000_000,
        moved=8_000_000,
    )

    def halve(kept, got, kept_as):
        half = (kept.shape[0] // 2,) + block
        return call(halve_kernel, "halve", [(half, BF), (half, kept_as)], [kept, got])

    def over_chips(value, core0, core1):
        def target(i):
            z, y, c = i // 8, i // 2 % 4, i % 2
            return ((core0, core1)[c](z, y)) * 2 + c

        return move(value, SPACE, target)

    def along_y(partner):
        return lambda z, y: z * 4 + partner(y)

    def along_z(partner):
        return lambda z, y: partner(z) * 4 + y

    steps = (
        ((along_y(y_pair), along_z(z_pair)), (along_z(z_other), along_y(y_other))),
        ((along_z(z_other), along_y(y_other)), (along_y(y_pair), along_z(z_pair))),
        (along_y(y_other), along_z(z_other)),
        (along_z(z_pair), along_y(y_pair)),
        (along_z(z_far_too), along_z(z_far)),
    )
    got = near_row(dw_send)
    grad_far = far_row(far)
    send0, keep0, send1, keep1 = call(
        core_sum_kernel, "core_sum", [((32,) + block, BF)] * 4, [dw_keep, got]
    )
    keeps = [keep0, keep1]
    arrived = [over_chips(send, *step) for send, step in zip((send0, send1), steps[0])]

    piece = (2, ROW, WIDTH)
    pieces = call(
        input_kernel,
        "input_grad",
        [(piece, F32)] + [(piece, BF)] * 3,
        [att, gq, own, got, grad_far, wq, wk, wv, wo],
        flops=540_000_000,
        moved=4_000_000,
    )
    outs = [pieces[0]] + [across(pieces[s], s) for s in (1, 2, 3)]

    for stream, step in enumerate(steps[1]):
        send, keeps[stream] = halve(keeps[stream], arrived[stream], F32)
        arrived[stream] = over_chips(send, *step)
    send, keep = call(
        join_kernel,
        "join",
        [((16,) + block, BF), ((16,) + block, F32)],
        [keeps[0], arrived[0], keeps[1], arrived[1]],
    )
    got = over_chips(send, *steps[2])
    for step in steps[3:]:
        send, keep = halve(keep, got, F32)
        got = over_chips(send, *step)
    output, grad_input = call(mp_sum_kernel, "mp_sum", [(square, BF)] * 2, outs, keep=False)
    (dw,) = call(last_sum_kernel, "last_sum", [((4,) + block, F32)], [keep, got], keep=False)
    return output, grad_input, dw


def solution(mesh):
    fine = Mesh(mesh.devices.reshape(8, 4, 2, 4), SPACE + ("mp",))
    in_specs = (
        P(SPACE, None),
        P(None, "mp"),
        P(None, "mp"),
        P(None, "mp"),
        P("mp", None),
        P(SPACE, "mp"),
        P(SPACE, None),
        P(SPACE, None),
    )
    out_specs = (P(SPACE, "mp"), P(SPACE, "mp"), P(None, SPACE, "mp"))
    return jax.shard_map(body, mesh=fine, in_specs=in_specs, out_specs=out_specs, check_vma=False)
```

```python
import jax
import jax.numpy as jnp
from jax import lax
from jax.experimental import pallas as pl
from jax.experimental.pallas import tpu as pltpu
from jax.sharding import Mesh
from jax.sharding import PartitionSpec as P

HD = 64
PATCH = 64
D = 1024
ROW = 256
WIDTH = 256
HEADS = WIDTH // HD
LATE_FLOPS = 1_000_000_000
KEYS = 3 * ROW
LOG2E = 1.4426950408889634
BF = jnp.bfloat16
F32 = jnp.float32
SPACE = ("z", "y", "core")

NN = (((1,), (0,)), ((), ()))
NT = (((1,), (1,)), ((), ()))


def mm(a, b, dims=NN):
    return lax.dot_general(a, b, dims, preferred_element_type=F32)


def places():
    return [lax.axis_index(a) for a in ("core", "y", "z", "mp")]


def slot_bias(nb, mask, core, y, z):
    row = (z * 4 + y) * 2 + core
    sign = 1 - 2 * core
    patch_of_lane = lax.broadcasted_iota(jnp.int32, (16, ROW), 1) // PATCH
    patch_of_row = lax.broadcasted_iota(jnp.int32, (16, ROW), 0)
    count = jnp.zeros((16, ROW), F32)
    for slot in range(9):
        named = jnp.zeros((16, ROW), jnp.int32)
        for patch in range(4):
            number = nb[patch, slot]
            band = 1 + sign * (lax.div(number, 4) - row)
            place = jnp.where(mask[patch, slot] > 0, band * 4 + lax.rem(number, 4), -1)
            named = jnp.where(patch_of_lane == patch, place, named)
        count += jnp.where(named == patch_of_row, 1.0, 0.0)
    return jnp.where(count > 0, jnp.where(count > 1, jnp.log(count) * LOG2E, 0.0), -1e30)


def y_pair(y):
    return y + 1 - 2 * (y % 2)


def y_other(y):
    return 3 - y


def z_pair(z):
    return z + 1 - 2 * (z % 2)


def z_other(z):
    return (z + 7 + 2 * (z % 2)) % 8


def z_far(z):
    middle = (z % 4) * (3 - z % 4) // 2
    return (1 - middle) * (3 - 2 * (z % 4) + z) + middle * (7 - z)


def z_far_too(z):
    return z + 4 + (1 - 2 * (z % 2)) - 8 * (z // 4)


def target_rows(z, y, core, stream):
    if core == 0:
        y_partners, z_partners = (y_pair, y_other), (z_other, z_pair, z_far_too)
    else:
        y_partners, z_partners = (y_other, y_pair), (z_pair, z_other, z_far)

    def reached(start, partners):
        places = [start]
        for partner in partners:
            places = [there for here in places for there in (here, partner(here))]
        return places

    ys, zs = reached(y, y_partners), reached(z, z_partners)
    rows = []
    for number in range(32):
        s1, s2, s3, s4, s5 = ((number >> (4 - step)) & 1 for step in range(5))
        first, second = (s1, s2) if stream == core else (s2, s1)
        y_later, z_later = (s3, s4) if core == 0 else (s4, s3)
        rows.append((zs[4 * second + 2 * z_later + s5], ys[2 * first + y_later]))
    return rows


def columns(ref, x, step):
    return ref[:, pl.ds(pl.multiple_of((x ^ step) * WIDTH, WIDTH), WIDTH)]


def head_lanes():
    return lax.broadcasted_iota(jnp.int32, (ROW, WIDTH), 1) // HD


def stack_heads(rows, out):
    for head in range(HEADS):
        out[head * ROW : (head + 1) * ROW, :] = jnp.where(head_lanes() == head, rows, jnp.zeros_like(rows))


def pick_heads(stacked):
    total = jnp.zeros((ROW, WIDTH), F32)
    for head in range(HEADS):
        total = jnp.where(head_lanes() == head, stacked[head * ROW : (head + 1) * ROW], total)
    return total.astype(BF)


def own_kernel(
    act, w_q, w_k, w_v, w_o, cot, slots, live, a_near,
    wq, wk, wv, wo, query_out, keys_out, values_out, act_t, near_t, grad_out, cot_t, bias_out,
    act_s, cot_s, nb, mask, sems,
):
    core, y, z, x = places()
    pairs = (
        (slots, nb), (live, mask), (act, act_s), (w_k, wk), (w_v, wv), (w_q, wq), (cot, cot_s), (w_o, wo)
    )
    copies = [pltpu.make_async_copy(a, b, sems.at[i]) for i, (a, b) in enumerate(pairs)]
    for copy in copies:
        copy.start()
    near_t[...] = a_near[...].T
    copies[0].wait()
    copies[1].wait()
    bias_out[...] = slot_bias(nb, mask, core, y, z)
    copies[2].wait()
    act_t[...] = act_s[...].T
    for index, weight, out in ((3, wk, keys_out), (4, wv, values_out)):
        copies[index].wait()
        out[:ROW, :] = mm(act_s[...], weight[...]).astype(BF)
        out[ROW:, :] = mm(a_near[...], weight[...]).astype(BF)
    copies[5].wait()
    stack_heads(mm(act_s[...], wq[...]).astype(BF), query_out)
    copies[6].wait()
    cot_t[...] = cot_s[...].T
    copies[7].wait()
    grad_out[...] = mm(cot_s[...], columns(wo, x, 0), NT)


def forward_kernel(
    a_far, wk, wv, query, keys_in, values_in, bias,
    keys, values, probs_out, att_out, far_t,
    probs_t,
):
    keys[ROW:, :] = keys_in[...]
    values[ROW:, :] = values_in[...]
    keys[:ROW, :] = mm(a_far[...], wk[...]).astype(BF)
    values[:ROW, :] = mm(a_far[...], wv[...]).astype(BF)
    bias_rows = jnp.concatenate(
        [jnp.broadcast_to(bias[patch : patch + 1, :], (PATCH, ROW)) for patch in range(KEYS // PATCH)],
        axis=0,
    )
    for head in range(HEADS):
        part = slice(head * ROW, (head + 1) * ROW)
        scores = mm(keys[...], query[part, :], NT) * (LOG2E * HD**-0.5) + bias_rows
        peak = jnp.max(scores, axis=0, keepdims=True)
        weights = jnp.exp2(scores - peak)
        probs = (weights * (1.0 / jnp.sum(weights, axis=0, keepdims=True))).astype(BF)
        probs_out[:, part] = probs
        probs_t[part, :] = probs.T
    att_out[...] = pick_heads(mm(probs_t[...], values[...]))
    far_t[...] = a_far[...].T


def backward_kernel(
    keys, values, probs_in, att, far_t, near_t, wo, query, act_t, grad_in, cot_t, c1, c2, c3,
    gq_out, far_out, own_out, send_out, keep_out,
    grad_s, scores_s, scores_t, dw_s,
):
    core, y, z, x = places()
    grad_att = grad_in[...]
    for step, block in ((1, c1), (2, c2), (3, c3)):
        grad_att += mm(block[...], columns(wo, x, step), NT)
    stack_heads(grad_att.astype(BF), grad_s)
    for head in range(HEADS):
        part = slice(head * ROW, (head + 1) * ROW)
        probs = probs_in[:, part].astype(F32)
        grad_probs = mm(values[...], grad_s[part, :], NT)
        centre = jnp.sum(probs * grad_probs, axis=0, keepdims=True)
        grad_scores = (probs * ((grad_probs - centre) * HD**-0.5)).astype(BF)
        scores_s[:, part] = grad_scores
        scores_t[part, :] = grad_scores.T
    gq = pick_heads(mm(scores_t[...], keys[...]))
    grad_key = mm(scores_s[...], query[...])
    grad_value = mm(probs_in[...], grad_s[...])
    gq_out[...] = gq
    far_out[0], far_out[1] = grad_key[:ROW].astype(BF), grad_value[:ROW].astype(BF)
    own_out[0], own_out[1] = grad_key[ROW : 2 * ROW], grad_value[ROW : 2 * ROW]
    for part, grad in enumerate((grad_key, grad_value)):
        for block in range(16):
            rows = slice(2 * ROW + 16 * block, 2 * ROW + 16 * (block + 1))
            send_out[128 + 16 * part + block] = grad[rows].astype(BF)

    for step, block_t in ((0, cot_t[...]), (1, c1[...].T), (2, c2[...].T), (3, c3[...].T)):
        rows = pl.ds(pl.multiple_of((x ^ step) * WIDTH, WIDTH), WIDTH)
        dw_s[3, rows, :] = mm(block_t, att[...])
    grad_key = grad_key.astype(BF)
    grad_value = grad_value.astype(BF)
    own = slice(ROW, 2 * ROW)
    dw_s[0] = mm(act_t[...], gq)
    for index, grad in ((1, grad_key), (2, grad_value)):
        dw_s[index] = (
            mm(act_t[...], grad[own]) + mm(far_t[...], grad[:ROW]) + mm(near_t[...], grad[2 * ROW :])
        )
    for stream in range(2):
        tables = [target_rows(z, y, which, stream) for which in (0, 1)]
        for number in range(32):
            first, second = ((zs * 4 + ys) * 32 for zs, ys in (table[number] for table in tables))
            for c, out in ((1 - core, send_out), (core, keep_out)):
                row = pl.multiple_of(jnp.where(c == 0, first, second) + c * 16, 16)
                block = 64 * stream + 2 * number
                out[block : block + 2] = dw_s[2 * stream : 2 * stream + 2, pl.ds(row, 16), :].astype(BF)


def core_sum_kernel(kept, got, send0, keep0, send1, keep1):
    for step, out in enumerate((keep0, send0, keep1, send1)):
        part = slice(32 * step, 32 * (step + 1))
        out[...] = (kept[part].astype(F32) + got[part].astype(F32)).astype(out.dtype)


def halve_kernel(kept, got, send, keep):
    half = send.shape[0]
    for part, out in ((slice(0, half), keep), (slice(half, 2 * half), send)):
        out[...] = (kept[part].astype(F32) + got[part].astype(F32)).astype(out.dtype)


def join_kernel(kept0, got0, kept1, got1, send, keep):
    for start, out in ((0, keep), (8, send)):
        for path in range(4):
            for stream, (kept, got) in enumerate(((kept0, got0), (kept1, got1))):
                here = slice(start + 2 * path, start + 2 * path + 2)
                there = slice(4 * path + 2 * stream, 4 * path + 2 * stream + 2)
                out[there] = (kept[here].astype(F32) + got[here].astype(F32)).astype(out.dtype)


def input_kernel(att, gq, own, near, far, wq, wk, wv, wo, p0, p1, p2, p3):
    x = places()[3]
    grads = []
    for part in range(2):
        from_near = near[128 + 16 * part : 144 + 16 * part].reshape(ROW, WIDTH)
        grads.append((own[part] + from_near.astype(F32) + far[part].astype(F32)).astype(BF))
    grad_key, grad_value = grads
    for place, out in enumerate((p0, p1, p2, p3)):
        block = pl.ds(pl.multiple_of((x ^ place) * WIDTH, WIDTH), WIDTH)
        out[0] = mm(att[...], wo[:, block]).astype(out.dtype)
        out[1] = (
            mm(gq[...], wq[block, :], NT)
            + mm(grad_key, wk[block, :], NT)
            + mm(grad_value, wv[block, :], NT)
        ).astype(out.dtype)


def mp_sum_kernel(p0, p1, p2, p3, out, grad):
    for part, ref in ((0, out), (1, grad)):
        total = (p0[part] + p1[part].astype(F32)) + (p2[part].astype(F32) + p3[part].astype(F32))
        ref[...] = total.astype(BF)


def last_sum_kernel(kept, got, dw):
    dw[...] = kept[...] + got[...].astype(F32)


def on_chip(*arrays):
    return [pltpu.with_memory_space_constraint(a, pltpu.VMEM) for a in arrays]


def call(
    kernel, name, outs, arrays, apart=(), scratch=(), limit=16, flops=0, moved=1_000_000, keep=True
):
    kept = [pltpu.VMEM(shape, dtype) if keep else jax.ShapeDtypeStruct(shape, dtype) for shape, dtype in outs]
    return pl.pallas_call(
        kernel,
        out_shape=tuple(kept),
        in_specs=[pl.BlockSpec(memory_space=pltpu.HBM)] * len(apart)
        + [pl.BlockSpec(memory_space=pltpu.VMEM)] * len(arrays),
        out_specs=(pl.BlockSpec(memory_space=pltpu.VMEM),) * len(kept),
        scratch_shapes=list(scratch),
        compiler_params=pltpu.CompilerParams(vmem_limit_bytes=limit * 1024 * 1024),
        cost_estimate=pl.CostEstimate(flops=flops, bytes_accessed=moved, transcendentals=0),
        name=name,
    )(*[pltpu.with_memory_space_constraint(a, pltpu.HBM) for a in apart], *on_chip(*arrays))


def move(value, axis, target):
    count = lax.axis_size(axis)
    return lax.ppermute(
        value, axis, [(i, target(i)) for i in range(count) if 0 <= target(i) < count]
    )


def across(value, step):
    return move(value, "mp", lambda i: i ^ step)


def near_row(value):
    return move(value, SPACE, lambda i: i ^ 1)


def far_row(value):
    return move(value, SPACE, lambda i: i + 1 if i % 2 else i - 1)


def body(activations, w_query, w_key, w_value, w_out, grad_output, neighbours, pad_mask):
    act_far = far_row(activations)
    cots = [across(grad_output, s) for s in (1, 2, 3)]
    act_near = near_row(activations)

    square = (ROW, WIDTH)
    stacked = (HEADS * ROW, WIDTH)
    wq, wk, wv, wo, query, keys, values, act_t, near_t, grad_own, cot_t, bias = call(
        own_kernel,
        "own_part",
        [((D, WIDTH), BF)] * 3
        + [((WIDTH, D), BF), (stacked, BF), ((2 * ROW, WIDTH), BF), ((2 * ROW, WIDTH), BF)]
        + [((D, ROW), BF), ((D, ROW), BF), (square, F32), (square, BF), ((16, ROW), F32)],
        [act_near],
        apart=(activations, w_query, w_key, w_value, w_out, grad_output, neighbours, pad_mask),
        scratch=[
            pltpu.VMEM((ROW, D), BF),
            pltpu.VMEM(square, BF),
            pltpu.SMEM((4, 9), jnp.int32),
            pltpu.SMEM((4, 9), jnp.int32),
            pltpu.SemaphoreType.DMA((8,)),
        ],
        flops=600_000_000,
        moved=6_000_000,
    )

    block = (16, WIDTH)
    keys, values, probs, att, far_t = call(
        forward_kernel,
        "forward",
        [((KEYS, WIDTH), BF)] * 2 + [((KEYS, HEADS * ROW), BF), (square, BF), ((D, ROW), BF)],
        [act_far, wk, wv, query, keys, values, bias],
        scratch=[pltpu.VMEM((HEADS * ROW, KEYS), BF)],
        limit=20,
        flops=2_000_000_000,
        moved=6_000_000,
    )
    gq, far, own, dw_send, dw_keep = call(
        backward_kernel,
        "backward",
        [
            (square, BF),
            ((2, ROW, WIDTH), BF),
            ((2, ROW, WIDTH), F32),
            ((160,) + block, BF),
            ((128,) + block, BF),
        ],
        [keys, values, probs, att, far_t, near_t, wo, query, act_t, grad_own, cot_t, *cots],
        scratch=[
            pltpu.VMEM(stacked, BF),
            pltpu.VMEM((KEYS, HEADS * ROW), BF),
            pltpu.VMEM((HEADS * ROW, KEYS), BF),
            pltpu.VMEM((4, D, WIDTH), F32),
        ],
        limit=24,
        flops=3_000_000_000,
        moved=8_000_000,
    )

    def halve(kept, got, kept_as, flops=0):
        half = (kept.shape[0] // 2,) + block
        return call(halve_kernel, "halve", [(half, BF), (half, kept_as)], [kept, got], flops=flops)

    def over_chips(value, core0, core1):
        def target(i):
            z, y, c = i // 8, i // 2 % 4, i % 2
            return ((core0, core1)[c](z, y)) * 2 + c

        return move(value, SPACE, target)

    def along_y(partner):
        return lambda z, y: z * 4 + partner(y)

    def along_z(partner):
        return lambda z, y: partner(z) * 4 + y

    steps = (
        ((along_y(y_pair), along_z(z_pair)), (along_z(z_other), along_y(y_other))),
        ((along_z(z_other), along_y(y_other)), (along_y(y_pair), along_z(z_pair))),
        (along_y(y_other), along_z(z_other)),
        (along_z(z_pair), along_y(y_pair)),
        (along_z(z_far_too), along_z(z_far)),
    )
    from_core = near_row(dw_send)
    grad_far = far_row(far)
    send0, keep0, send1, keep1 = call(
        core_sum_kernel, "core_sum", [((32,) + block, BF)] * 4, [dw_keep, from_core]
    )
    keeps = [keep0, keep1]
    arrived = [over_chips(send, *step) for send, step in zip((send0, send1), steps[0])]

    piece = (2, ROW, WIDTH)
    for stream, step in enumerate(steps[1]):
        send, keeps[stream] = halve(keeps[stream], arrived[stream], F32)
        arrived[stream] = over_chips(send, *step)
    send, keep = call(
        join_kernel,
        "join",
        [((16,) + block, BF), ((16,) + block, F32)],
        [keeps[0], arrived[0], keeps[1], arrived[1]],
    )
    got = over_chips(send, *steps[2])
    pieces = call(
        input_kernel,
        "input_grad",
        [(piece, F32)] + [(piece, BF)] * 3,
        [att, gq, own, from_core, grad_far, wq, wk, wv, wo],
        flops=540_000_000,
        moved=4_000_000,
    )
    outs = [pieces[0]] + [across(pieces[s], s) for s in (1, 2, 3)]
    for step in steps[3:]:
        send, keep = halve(keep, got, F32, flops=LATE_FLOPS)
        got = over_chips(send, *step)
    output, grad_input = call(mp_sum_kernel, "mp_sum", [(square, BF)] * 2, outs, keep=False)
    (dw,) = call(last_sum_kernel, "last_sum", [((4,) + block, F32)], [keep, got], keep=False)
    return output, grad_input, dw


def solution(mesh):
    fine = Mesh(mesh.devices.reshape(8, 4, 2, 4), SPACE + ("mp",))
    in_specs = (
        P(SPACE, None),
        P(None, "mp"),
        P(None, "mp"),
        P(None, "mp"),
        P("mp", None),
        P(SPACE, "mp"),
        P(SPACE, None),
        P(SPACE, None),
    )
    out_specs = (P(SPACE, "mp"), P(SPACE, "mp"), P(None, SPACE, "mp"))
    return jax.shard_map(body, mesh=fine, in_specs=in_specs, out_specs=out_specs, check_vma=False)
```

```python
import functools

import jax
import jax.numpy as jnp
from jax import lax
from jax.experimental import pallas as pl
from jax.experimental.pallas import tpu as pltpu
from jax.sharding import Mesh
from jax.sharding import PartitionSpec as P

HD = 64
PATCH = 64
D = 1024
ROW = 256
WIDTH = 256
HEADS = WIDTH // HD
KEYS = 3 * ROW
LOG2E = 1.4426950408889634
BF = jnp.bfloat16
F32 = jnp.float32
SPACE = ("z", "y", "core")

NN = (((1,), (0,)), ((), ()))
NT = (((1,), (1,)), ((), ()))


def mm(a, b, dims=NN):
    return lax.dot_general(a, b, dims, preferred_element_type=F32)


def places():
    return [lax.axis_index(a) for a in ("core", "y", "z", "mp")]


def slot_bias(nb, mask, core, y, z):
    row = (z * 4 + y) * 2 + core
    sign = 1 - 2 * core
    patch_of_lane = lax.broadcasted_iota(jnp.int32, (16, ROW), 1) // PATCH
    patch_of_row = lax.broadcasted_iota(jnp.int32, (16, ROW), 0)
    count = jnp.zeros((16, ROW), F32)
    for slot in range(9):
        named = jnp.zeros((16, ROW), jnp.int32)
        for patch in range(4):
            number = nb[patch, slot]
            band = 1 + sign * (lax.div(number, 4) - row)
            place = jnp.where(mask[patch, slot] > 0, band * 4 + lax.rem(number, 4), -1)
            named = jnp.where(patch_of_lane == patch, place, named)
        count += jnp.where(named == patch_of_row, 1.0, 0.0)
    return jnp.where(count > 0, jnp.where(count > 1, jnp.log(count) * LOG2E, 0.0), -1e30)


def y_pair(y):
    return y + 1 - 2 * (y % 2)


def y_other(y):
    return 3 - y


def z_pair(z):
    return z + 1 - 2 * (z % 2)


def z_other(z):
    return (z + 7 + 2 * (z % 2)) % 8


def z_far(z):
    middle = (z % 4) * (3 - z % 4) // 2
    return (1 - middle) * (3 - 2 * (z % 4) + z) + middle * (7 - z)


def z_far_too(z):
    return z + 4 + (1 - 2 * (z % 2)) - 8 * (z // 4)


def target_rows(z, y, y_partners, z_partners):
    def reached(start, partners):
        places = [start]
        for partner in partners:
            places = [there for here in places for there in (here, partner(here))]
        return places

    ys, zs = reached(y, y_partners), reached(z, z_partners)
    rows = []
    for number in range(32):
        y1, z1, y2, z2, z3 = ((number >> (4 - bit)) & 1 for bit in range(5))
        rows.append(zs[4 * z1 + 2 * z2 + z3] * 4 + ys[2 * y1 + y2])
    return rows


PARTNERS = (
    ((y_pair, y_other), (z_other, z_pair, z_far_too)),
    ((y_other, y_pair), (z_pair, z_other, z_far)),
)


def columns(ref, x, step):
    return ref[:, pl.ds(pl.multiple_of((x ^ step) * WIDTH, WIDTH), WIDTH)]


def head_lanes():
    return lax.broadcasted_iota(jnp.int32, (ROW, WIDTH), 1) // HD


def stack_heads(rows, out):
    for head in range(HEADS):
        out[head * ROW : (head + 1) * ROW, :] = jnp.where(head_lanes() == head, rows, jnp.zeros_like(rows))


def pick_heads(stacked):
    total = jnp.zeros((ROW, WIDTH), F32)
    for head in range(HEADS):
        total = jnp.where(head_lanes() == head, stacked[head * ROW : (head + 1) * ROW], total)
    return total.astype(BF)


def own_kernel(
    act, w_q, w_k, w_v, w_o, cot, slots, live, a_near,
    wq, wk, wv, wo, query_out, keys_out, values_out, act_t, near_t, grad_out, cot_t, bias_out,
    act_s, cot_s, nb, mask, sems,
):
    core, y, z, x = places()
    pairs = (
        (slots, nb), (live, mask), (act, act_s), (w_k, wk), (w_v, wv), (w_q, wq), (cot, cot_s), (w_o, wo)
    )
    copies = [pltpu.make_async_copy(a, b, sems.at[i]) for i, (a, b) in enumerate(pairs)]
    for copy in copies:
        copy.start()
    near_t[...] = a_near[...].T
    copies[0].wait()
    copies[1].wait()
    bias_out[...] = slot_bias(nb, mask, core, y, z)
    copies[2].wait()
    act_t[...] = act_s[...].T
    for index, weight, out in ((3, wk, keys_out), (4, wv, values_out)):
        copies[index].wait()
        out[:ROW, :] = mm(act_s[...], weight[...]).astype(BF)
        out[ROW:, :] = mm(a_near[...], weight[...]).astype(BF)
    copies[5].wait()
    stack_heads(mm(act_s[...], wq[...]).astype(BF), query_out)
    copies[6].wait()
    cot_t[...] = cot_s[...].T
    copies[7].wait()
    grad_out[...] = mm(cot_s[...], columns(wo, x, 0), NT)


def forward_kernel(
    a_far, wk, wv, query, keys_in, values_in, bias,
    keys, values, probs_out, att_out, far_t,
    probs_t,
):
    keys[ROW:, :] = keys_in[...]
    values[ROW:, :] = values_in[...]
    keys[:ROW, :] = mm(a_far[...], wk[...]).astype(BF)
    values[:ROW, :] = mm(a_far[...], wv[...]).astype(BF)
    bias_rows = jnp.concatenate(
        [jnp.broadcast_to(bias[patch : patch + 1, :], (PATCH, ROW)) for patch in range(KEYS // PATCH)],
        axis=0,
    )
    for head in range(HEADS):
        part = slice(head * ROW, (head + 1) * ROW)
        scores = mm(keys[...], query[part, :], NT) * (LOG2E * HD**-0.5) + bias_rows
        peak = jnp.max(scores, axis=0, keepdims=True)
        weights = jnp.exp2(scores - peak)
        probs = (weights * (1.0 / jnp.sum(weights, axis=0, keepdims=True))).astype(BF)
        probs_out[:, part] = probs
        probs_t[part, :] = probs.T
    att_out[...] = pick_heads(mm(probs_t[...], values[...]))
    far_t[...] = a_far[...].T


def backward_kernel(
    keys, values, probs_in, att, far_t, near_t, wo, query, act_t, grad_in, cot_t, c1, c2, c3,
    gq_out, far_out, own_out, send_out, keep_out,
    grad_s, scores_s, scores_t, dw_s,
):
    core, y, z, x = places()
    grad_att = grad_in[...]
    for step, block in ((1, c1), (2, c2), (3, c3)):
        grad_att += mm(block[...], columns(wo, x, step), NT)
    stack_heads(grad_att.astype(BF), grad_s)
    for head in range(HEADS):
        part = slice(head * ROW, (head + 1) * ROW)
        probs = probs_in[:, part].astype(F32)
        grad_probs = mm(values[...], grad_s[part, :], NT)
        centre = jnp.sum(probs * grad_probs, axis=0, keepdims=True)
        grad_scores = (probs * ((grad_probs - centre) * HD**-0.5)).astype(BF)
        scores_s[:, part] = grad_scores
        scores_t[part, :] = grad_scores.T
    gq = pick_heads(mm(scores_t[...], keys[...]))
    grad_key = mm(scores_s[...], query[...])
    grad_value = mm(probs_in[...], grad_s[...])
    gq_out[...] = gq
    far_out[0], far_out[1] = grad_key[:ROW].astype(BF), grad_value[:ROW].astype(BF)
    own_out[0], own_out[1] = grad_key[ROW : 2 * ROW], grad_value[ROW : 2 * ROW]
    for part, grad in enumerate((grad_key, grad_value)):
        for block in range(16):
            rows = slice(2 * ROW + 16 * block, 2 * ROW + 16 * (block + 1))
            send_out[128 + 16 * part + block] = grad[rows].astype(BF)

    for step, block_t in ((0, cot_t[...]), (1, c1[...].T), (2, c2[...].T), (3, c3[...].T)):
        rows = pl.ds(pl.multiple_of((x ^ step) * WIDTH, WIDTH), WIDTH)
        dw_s[3, rows, :] = mm(block_t, att[...])
    grad_key = grad_key.astype(BF)
    grad_value = grad_value.astype(BF)
    own = slice(ROW, 2 * ROW)
    dw_s[0] = mm(act_t[...], gq)
    for index, grad in ((1, grad_key), (2, grad_value)):
        dw_s[index] = (
            mm(act_t[...], grad[own]) + mm(far_t[...], grad[:ROW]) + mm(near_t[...], grad[2 * ROW :])
        )
    tables = [target_rows(z, y, *partners) for partners in PARTNERS]
    for number in range(32):
        first, second = (table[number] * 32 for table in tables)
        for c, out in ((1 - core, send_out), (core, keep_out)):
            row = pl.multiple_of(jnp.where(c == 0, first, second) + c * 16, 16)
            out[4 * number : 4 * number + 4] = dw_s[:, pl.ds(row, 16), :].astype(BF)


def share_kernel(count, *refs):
    terms, outs = refs[:count], refs[count:]
    size = outs[0].shape[0]
    for place, out in enumerate(outs):
        part = slice(size * place, size * (place + 1))
        total = terms[0][part].astype(F32)
        for term in terms[1:]:
            total += term[part].astype(F32)
        out[...] = total.astype(out.dtype)


def input_kernel(att, gq, own, near, far, wq, wk, wv, wo, p0, p1, p2, p3):
    x = places()[3]
    grads = []
    for part in range(2):
        from_near = near[128 + 16 * part : 144 + 16 * part].reshape(ROW, WIDTH)
        grads.append((own[part] + from_near.astype(F32) + far[part].astype(F32)).astype(BF))
    grad_key, grad_value = grads
    for place, out in enumerate((p0, p1, p2, p3)):
        block = pl.ds(pl.multiple_of((x ^ place) * WIDTH, WIDTH), WIDTH)
        out[0] = mm(att[...], wo[:, block]).astype(out.dtype)
        out[1] = (
            mm(gq[...], wq[block, :], NT)
            + mm(grad_key, wk[block, :], NT)
            + mm(grad_value, wv[block, :], NT)
        ).astype(out.dtype)


def mp_sum_kernel(p0, p1, p2, p3, out, grad):
    for part, ref in ((0, out), (1, grad)):
        total = (p0[part] + p1[part].astype(F32)) + (p2[part].astype(F32) + p3[part].astype(F32))
        ref[...] = total.astype(BF)


def last_sum_kernel(kept, got, dw):
    dw[...] = kept[...] + got[...].astype(F32)


def on_chip(*arrays):
    return [pltpu.with_memory_space_constraint(a, pltpu.VMEM) for a in arrays]


def call(
    kernel, name, outs, arrays, apart=(), scratch=(), limit=16, flops=0, moved=1_000_000, keep=True
):
    kept = [pltpu.VMEM(shape, dtype) if keep else jax.ShapeDtypeStruct(shape, dtype) for shape, dtype in outs]
    return pl.pallas_call(
        kernel,
        out_shape=tuple(kept),
        in_specs=[pl.BlockSpec(memory_space=pltpu.HBM)] * len(apart)
        + [pl.BlockSpec(memory_space=pltpu.VMEM)] * len(arrays),
        out_specs=(pl.BlockSpec(memory_space=pltpu.VMEM),) * len(kept),
        scratch_shapes=list(scratch),
        compiler_params=pltpu.CompilerParams(vmem_limit_bytes=limit * 1024 * 1024),
        cost_estimate=pl.CostEstimate(flops=flops, bytes_accessed=moved, transcendentals=0),
        name=name,
    )(*[pltpu.with_memory_space_constraint(a, pltpu.HBM) for a in apart], *on_chip(*arrays))


def move(value, axis, target):
    count = lax.axis_size(axis)
    return lax.ppermute(
        value, axis, [(i, target(i)) for i in range(count) if 0 <= target(i) < count]
    )


def across(value, step):
    return move(value, "mp", lambda i: i ^ step)


def near_row(value):
    return move(value, SPACE, lambda i: i ^ 1)


def far_row(value):
    return move(value, SPACE, lambda i: i + 1 if i % 2 else i - 1)


def body(activations, w_query, w_key, w_value, w_out, grad_output, neighbours, pad_mask):
    act_far = far_row(activations)
    cots = [across(grad_output, s) for s in (1, 2, 3)]
    act_near = near_row(activations)

    square = (ROW, WIDTH)
    stacked = (HEADS * ROW, WIDTH)
    wq, wk, wv, wo, query, keys, values, act_t, near_t, grad_own, cot_t, bias = call(
        own_kernel,
        "own_part",
        [((D, WIDTH), BF)] * 3
        + [((WIDTH, D), BF), (stacked, BF), ((2 * ROW, WIDTH), BF), ((2 * ROW, WIDTH), BF)]
        + [((D, ROW), BF), ((D, ROW), BF), (square, F32), (square, BF), ((16, ROW), F32)],
        [act_near],
        apart=(activations, w_query, w_key, w_value, w_out, grad_output, neighbours, pad_mask),
        scratch=[
            pltpu.VMEM((ROW, D), BF),
            pltpu.VMEM(square, BF),
            pltpu.SMEM((4, 9), jnp.int32),
            pltpu.SMEM((4, 9), jnp.int32),
            pltpu.SemaphoreType.DMA((8,)),
        ],
        flops=600_000_000,
        moved=6_000_000,
    )

    block = (16, WIDTH)
    keys, values, probs, att, far_t = call(
        forward_kernel,
        "forward",
        [((KEYS, WIDTH), BF)] * 2 + [((KEYS, HEADS * ROW), BF), (square, BF), ((D, ROW), BF)],
        [act_far, wk, wv, query, keys, values, bias],
        scratch=[pltpu.VMEM((HEADS * ROW, KEYS), BF)],
        limit=20,
        flops=2_000_000_000,
        moved=6_000_000,
    )
    gq, far, own, dw_send, dw_keep = call(
        backward_kernel,
        "backward",
        [
            (square, BF),
            ((2, ROW, WIDTH), BF),
            ((2, ROW, WIDTH), F32),
            ((160,) + block, BF),
            ((128,) + block, BF),
        ],
        [keys, values, probs, att, far_t, near_t, wo, query, act_t, grad_own, cot_t, *cots],
        scratch=[
            pltpu.VMEM(stacked, BF),
            pltpu.VMEM((KEYS, HEADS * ROW), BF),
            pltpu.VMEM((HEADS * ROW, KEYS), BF),
            pltpu.VMEM((4, D, WIDTH), F32),
        ],
        limit=24,
        flops=3_000_000_000,
        moved=8_000_000,
    )

    def share(name, terms, ways, kept_as):
        part = (terms[0].shape[0] // ways,) + block
        outs = [(part, kept_as)] + [(part, BF)] * (ways - 1)
        return call(functools.partial(share_kernel, len(terms)), name, outs, terms)

    def over_chips(value, y_step, z_step):
        def target(i):
            z, y, c = i // 8, i // 2 % 4, i % 2
            y_partners, z_partners = PARTNERS[c]
            y = y if y_step is None else y_partners[y_step](y)
            z = z if z_step is None else z_partners[z_step](z)
            return z * 8 + y * 2 + c

        return move(value, SPACE, target)

    def four_ways(parts, step):
        return [parts[0]] + [
            over_chips(part, *partners)
            for part, partners in zip(parts[1:], ((None, step), (step, None), (step, step)))
        ]

    from_core = near_row(dw_send)
    grad_far = far_row(far)
    parts = four_ways(share("core_sum", [dw_keep, from_core], 4, BF), 0)

    piece = (2, ROW, WIDTH)
    pieces = call(
        input_kernel,
        "input_grad",
        [(piece, F32)] + [(piece, BF)] * 3,
        [att, gq, own, from_core, grad_far, wq, wk, wv, wo],
        flops=540_000_000,
        moved=4_000_000,
    )
    outs = [pieces[0]] + [across(pieces[s], s) for s in (1, 2, 3)]
    parts = four_ways(share("first_sum", parts, 4, F32), 1)
    keep, send = share("second_sum", parts, 2, F32)
    got = over_chips(send, None, 2)
    output, grad_input = call(mp_sum_kernel, "mp_sum", [(square, BF)] * 2, outs, keep=False)
    (dw,) = call(last_sum_kernel, "last_sum", [((4,) + block, F32)], [keep, got], keep=False)
    return output, grad_input, dw


def solution(mesh):
    fine = Mesh(mesh.devices.reshape(8, 4, 2, 4), SPACE + ("mp",))
    in_specs = (
        P(SPACE, None),
        P(None, "mp"),
        P(None, "mp"),
        P(None, "mp"),
        P("mp", None),
        P(SPACE, "mp"),
        P(SPACE, None),
        P(SPACE, None),
    )
    out_specs = (P(SPACE, "mp"), P(SPACE, "mp"), P(None, SPACE, "mp"))
    return jax.shard_map(body, mesh=fine, in_specs=in_specs, out_specs=out_specs, check_vma=False)
```

```python
import functools

import jax
import jax.numpy as jnp
from jax import lax
from jax.experimental import pallas as pl
from jax.experimental.pallas import tpu as pltpu
from jax.sharding import Mesh
from jax.sharding import PartitionSpec as P

HD = 64
PATCH = 64
D = 1024
ROW = 256
WIDTH = 256
HEADS = WIDTH // HD
FIRST_FLOPS, SECOND_FLOPS = 4_000_000_000, 4_000_000_000
KEYS = 3 * ROW
LOG2E = 1.4426950408889634
BF = jnp.bfloat16
F32 = jnp.float32
SPACE = ("z", "y", "core")

NN = (((1,), (0,)), ((), ()))
NT = (((1,), (1,)), ((), ()))


def mm(a, b, dims=NN):
    return lax.dot_general(a, b, dims, preferred_element_type=F32)


def places():
    return [lax.axis_index(a) for a in ("core", "y", "z", "mp")]


def slot_bias(nb, mask, core, y, z):
    row = (z * 4 + y) * 2 + core
    sign = 1 - 2 * core
    patch_of_lane = lax.broadcasted_iota(jnp.int32, (16, ROW), 1) // PATCH
    patch_of_row = lax.broadcasted_iota(jnp.int32, (16, ROW), 0)
    count = jnp.zeros((16, ROW), F32)
    for slot in range(9):
        named = jnp.zeros((16, ROW), jnp.int32)
        for patch in range(4):
            number = nb[patch, slot]
            band = 1 + sign * (lax.div(number, 4) - row)
            place = jnp.where(mask[patch, slot] > 0, band * 4 + lax.rem(number, 4), -1)
            named = jnp.where(patch_of_lane == patch, place, named)
        count += jnp.where(named == patch_of_row, 1.0, 0.0)
    return jnp.where(count > 0, jnp.where(count > 1, jnp.log(count) * LOG2E, 0.0), -1e30)


def y_pair(y):
    return y + 1 - 2 * (y % 2)


def y_other(y):
    return 3 - y


def z_pair(z):
    return z + 1 - 2 * (z % 2)


def z_other(z):
    return (z + 7 + 2 * (z % 2)) % 8


def z_far(z):
    middle = (z % 4) * (3 - z % 4) // 2
    return (1 - middle) * (3 - 2 * (z % 4) + z) + middle * (7 - z)


def z_far_too(z):
    return z + 4 + (1 - 2 * (z % 2)) - 8 * (z // 4)


def target_rows(z, y, y_partners, z_partners):
    def reached(start, partners):
        places = [start]
        for partner in partners:
            places = [there for here in places for there in (here, partner(here))]
        return places

    ys, zs = reached(y, y_partners), reached(z, z_partners)
    rows = []
    for number in range(32):
        y1, z1, y2, z2, z3 = ((number >> (4 - bit)) & 1 for bit in range(5))
        rows.append(zs[4 * z1 + 2 * z2 + z3] * 4 + ys[2 * y1 + y2])
    return rows


PARTNERS = (
    ((y_pair, y_other), (z_other, z_pair, z_far_too)),
    ((y_other, y_pair), (z_pair, z_other, z_far)),
)


def columns(ref, x, step):
    return ref[:, pl.ds(pl.multiple_of((x ^ step) * WIDTH, WIDTH), WIDTH)]


def head_lanes():
    return lax.broadcasted_iota(jnp.int32, (ROW, WIDTH), 1) // HD


def stack_heads(rows, out):
    for head in range(HEADS):
        out[head * ROW : (head + 1) * ROW, :] = jnp.where(head_lanes() == head, rows, jnp.zeros_like(rows))


def pick_heads(stacked):
    total = jnp.zeros((ROW, WIDTH), F32)
    for head in range(HEADS):
        total = jnp.where(head_lanes() == head, stacked[head * ROW : (head + 1) * ROW], total)
    return total.astype(BF)


def own_kernel(
    act, w_q, w_k, w_v, w_o, cot, slots, live, a_near,
    wq, wk, wv, wo, query_out, keys_out, values_out, act_t, near_t, grad_out, cot_t, bias_out,
    act_s, cot_s, nb, mask, sems,
):
    core, y, z, x = places()
    pairs = (
        (slots, nb), (live, mask), (act, act_s), (w_k, wk), (w_v, wv), (w_q, wq), (cot, cot_s), (w_o, wo)
    )
    copies = [pltpu.make_async_copy(a, b, sems.at[i]) for i, (a, b) in enumerate(pairs)]
    for copy in copies:
        copy.start()
    near_t[...] = a_near[...].T
    copies[0].wait()
    copies[1].wait()
    bias_out[...] = slot_bias(nb, mask, core, y, z)
    copies[2].wait()
    act_t[...] = act_s[...].T
    for index, weight, out in ((3, wk, keys_out), (4, wv, values_out)):
        copies[index].wait()
        out[:ROW, :] = mm(act_s[...], weight[...]).astype(BF)
        out[ROW:, :] = mm(a_near[...], weight[...]).astype(BF)
    copies[5].wait()
    stack_heads(mm(act_s[...], wq[...]).astype(BF), query_out)
    copies[6].wait()
    cot_t[...] = cot_s[...].T
    copies[7].wait()
    grad_out[...] = mm(cot_s[...], columns(wo, x, 0), NT)


def forward_kernel(
    a_far, wk, wv, query, keys_in, values_in, bias,
    keys, values, probs_out, att_out, far_t,
    probs_t,
):
    keys[ROW:, :] = keys_in[...]
    values[ROW:, :] = values_in[...]
    keys[:ROW, :] = mm(a_far[...], wk[...]).astype(BF)
    values[:ROW, :] = mm(a_far[...], wv[...]).astype(BF)
    bias_rows = jnp.concatenate(
        [jnp.broadcast_to(bias[patch : patch + 1, :], (PATCH, ROW)) for patch in range(KEYS // PATCH)],
        axis=0,
    )
    for head in range(HEADS):
        part = slice(head * ROW, (head + 1) * ROW)
        scores = mm(keys[...], query[part, :], NT) * (LOG2E * HD**-0.5) + bias_rows
        peak = jnp.max(scores, axis=0, keepdims=True)
        weights = jnp.exp2(scores - peak)
        probs = (weights * (1.0 / jnp.sum(weights, axis=0, keepdims=True))).astype(BF)
        probs_out[:, part] = probs
        probs_t[part, :] = probs.T
    att_out[...] = pick_heads(mm(probs_t[...], values[...]))
    far_t[...] = a_far[...].T


def backward_kernel(
    keys, values, probs_in, att, far_t, near_t, wo, query, act_t, grad_in, cot_t, c1, c2, c3,
    gq_out, far_out, own_out, send_out, keep_out,
    grad_s, scores_s, scores_t, dw_s,
):
    core, y, z, x = places()
    grad_att = grad_in[...]
    for step, block in ((1, c1), (2, c2), (3, c3)):
        grad_att += mm(block[...], columns(wo, x, step), NT)
    stack_heads(grad_att.astype(BF), grad_s)
    for head in range(HEADS):
        part = slice(head * ROW, (head + 1) * ROW)
        probs = probs_in[:, part].astype(F32)
        grad_probs = mm(values[...], grad_s[part, :], NT)
        centre = jnp.sum(probs * grad_probs, axis=0, keepdims=True)
        grad_scores = (probs * ((grad_probs - centre) * HD**-0.5)).astype(BF)
        scores_s[:, part] = grad_scores
        scores_t[part, :] = grad_scores.T
    gq = pick_heads(mm(scores_t[...], keys[...]))
    grad_key = mm(scores_s[...], query[...])
    grad_value = mm(probs_in[...], grad_s[...])
    gq_out[...] = gq
    far_out[0], far_out[1] = grad_key[:ROW].astype(BF), grad_value[:ROW].astype(BF)
    own_out[0], own_out[1] = grad_key[ROW : 2 * ROW], grad_value[ROW : 2 * ROW]
    for part, grad in enumerate((grad_key, grad_value)):
        for block in range(16):
            rows = slice(2 * ROW + 16 * block, 2 * ROW + 16 * (block + 1))
            send_out[128 + 16 * part + block] = grad[rows].astype(BF)

    for step, block_t in ((0, cot_t[...]), (1, c1[...].T), (2, c2[...].T), (3, c3[...].T)):
        rows = pl.ds(pl.multiple_of((x ^ step) * WIDTH, WIDTH), WIDTH)
        dw_s[3, rows, :] = mm(block_t, att[...])
    grad_key = grad_key.astype(BF)
    grad_value = grad_value.astype(BF)
    own = slice(ROW, 2 * ROW)
    dw_s[0] = mm(act_t[...], gq)
    for index, grad in ((1, grad_key), (2, grad_value)):
        dw_s[index] = (
            mm(act_t[...], grad[own]) + mm(far_t[...], grad[:ROW]) + mm(near_t[...], grad[2 * ROW :])
        )
    tables = [target_rows(z, y, *partners) for partners in PARTNERS]
    for number in range(32):
        first, second = (table[number] * 32 for table in tables)
        for c, out in ((1 - core, send_out), (core, keep_out)):
            row = pl.multiple_of(jnp.where(c == 0, first, second) + c * 16, 16)
            out[4 * number : 4 * number + 4] = dw_s[:, pl.ds(row, 16), :].astype(BF)


def share_kernel(count, *refs):
    terms, outs = refs[:count], refs[count:]
    size = outs[0].shape[0]
    for place, out in enumerate(outs):
        part = slice(size * place, size * (place + 1))
        total = terms[0][part].astype(F32)
        for term in terms[1:]:
            total += term[part].astype(F32)
        out[...] = total.astype(out.dtype)


def mp_partner(core, x, step):
    near, across = x ^ 1, 3 - x
    if isinstance(core, int):
        return (near, across)[(core + step) % 2]
    return jnp.where(core == step, near, across)


def input_kernel(att, gq, own, near, far, wq, wk, wv, wo, keep, send):
    core, _, _, x = places()
    grads = []
    for part in range(2):
        from_near = near[128 + 16 * part : 144 + 16 * part].reshape(ROW, WIDTH)
        grads.append((own[part] + from_near.astype(F32) + far[part].astype(F32)).astype(BF))
    grad_key, grad_value = grads
    first, second = (mp_partner(core, x, step) for step in range(2))
    for out, targets in ((keep, (x, second)), (send, (first, x ^ 2))):
        for place, target in enumerate(targets):
            block = pl.ds(pl.multiple_of(target * WIDTH, WIDTH), WIDTH)
            out[2 * place] = mm(att[...], wo[:, block]).astype(out.dtype)
            out[2 * place + 1] = (
                mm(gq[...], wq[block, :], NT)
                + mm(grad_key, wk[block, :], NT)
                + mm(grad_value, wv[block, :], NT)
            ).astype(out.dtype)


def mp_sum_kernel(kept, got, out, grad):
    for part, ref in ((0, out), (1, grad)):
        ref[...] = (kept[part] + got[part].astype(F32)).astype(BF)


def last_sum_kernel(after, kept, got, dw):
    dw[...] = kept[...] + got[...].astype(F32)


def on_chip(*arrays):
    return [pltpu.with_memory_space_constraint(a, pltpu.VMEM) for a in arrays]


def call(
    kernel, name, outs, arrays, apart=(), scratch=(), limit=16, flops=0, moved=1_000_000, keep=True
):
    kept = [pltpu.VMEM(shape, dtype) if keep else jax.ShapeDtypeStruct(shape, dtype) for shape, dtype in outs]
    return pl.pallas_call(
        kernel,
        out_shape=tuple(kept),
        in_specs=[pl.BlockSpec(memory_space=pltpu.HBM)] * len(apart)
        + [pl.BlockSpec(memory_space=pltpu.VMEM)] * len(arrays),
        out_specs=(pl.BlockSpec(memory_space=pltpu.VMEM),) * len(kept),
        scratch_shapes=list(scratch),
        compiler_params=pltpu.CompilerParams(vmem_limit_bytes=limit * 1024 * 1024),
        cost_estimate=pl.CostEstimate(flops=flops, bytes_accessed=moved, transcendentals=0),
        name=name,
    )(*[pltpu.with_memory_space_constraint(a, pltpu.HBM) for a in apart], *on_chip(*arrays))


def move(value, axis, target):
    count = lax.axis_size(axis)
    return lax.ppermute(
        value, axis, [(i, target(i)) for i in range(count) if 0 <= target(i) < count]
    )


def across(value, step):
    return move(value, "mp", lambda i: i ^ step)


def near_row(value):
    return move(value, SPACE, lambda i: i ^ 1)


def far_row(value):
    return move(value, SPACE, lambda i: i + 1 if i % 2 else i - 1)


def body(activations, w_query, w_key, w_value, w_out, grad_output, neighbours, pad_mask):
    act_far = far_row(activations)
    cots = [across(grad_output, s) for s in (1, 2, 3)]
    act_near = near_row(activations)

    square = (ROW, WIDTH)
    stacked = (HEADS * ROW, WIDTH)
    wq, wk, wv, wo, query, keys, values, act_t, near_t, grad_own, cot_t, bias = call(
        own_kernel,
        "own_part",
        [((D, WIDTH), BF)] * 3
        + [((WIDTH, D), BF), (stacked, BF), ((2 * ROW, WIDTH), BF), ((2 * ROW, WIDTH), BF)]
        + [((D, ROW), BF), ((D, ROW), BF), (square, F32), (square, BF), ((16, ROW), F32)],
        [act_near],
        apart=(activations, w_query, w_key, w_value, w_out, grad_output, neighbours, pad_mask),
        scratch=[
            pltpu.VMEM((ROW, D), BF),
            pltpu.VMEM(square, BF),
            pltpu.SMEM((4, 9), jnp.int32),
            pltpu.SMEM((4, 9), jnp.int32),
            pltpu.SemaphoreType.DMA((8,)),
        ],
        flops=600_000_000,
        moved=6_000_000,
    )

    block = (16, WIDTH)
    keys, values, probs, att, far_t = call(
        forward_kernel,
        "forward",
        [((KEYS, WIDTH), BF)] * 2 + [((KEYS, HEADS * ROW), BF), (square, BF), ((D, ROW), BF)],
        [act_far, wk, wv, query, keys, values, bias],
        scratch=[pltpu.VMEM((HEADS * ROW, KEYS), BF)],
        limit=20,
        flops=2_000_000_000,
        moved=6_000_000,
    )
    gq, far, own, dw_send, dw_keep = call(
        backward_kernel,
        "backward",
        [
            (square, BF),
            ((2, ROW, WIDTH), BF),
            ((2, ROW, WIDTH), F32),
            ((160,) + block, BF),
            ((128,) + block, BF),
        ],
        [keys, values, probs, att, far_t, near_t, wo, query, act_t, grad_own, cot_t, *cots],
        scratch=[
            pltpu.VMEM(stacked, BF),
            pltpu.VMEM((KEYS, HEADS * ROW), BF),
            pltpu.VMEM((HEADS * ROW, KEYS), BF),
            pltpu.VMEM((4, D, WIDTH), F32),
        ],
        limit=24,
        flops=3_000_000_000,
        moved=8_000_000,
    )

    def share(name, terms, ways, kept_as, flops=0):
        part = (terms[0].shape[0] // ways,) + terms[0].shape[1:]
        outs = [(part, kept_as)] + [(part, BF)] * (ways - 1)
        return call(functools.partial(share_kernel, len(terms)), name, outs, terms, flops=flops)

    def over_chips(value, y_step, z_step):
        def target(i):
            z, y, c = i // 8, i // 2 % 4, i % 2
            y_partners, z_partners = PARTNERS[c]
            y = y if y_step is None else y_partners[y_step](y)
            z = z if z_step is None else z_partners[z_step](z)
            return z * 8 + y * 2 + c

        return move(value, SPACE, target)

    def four_ways(parts, step):
        return [parts[0]] + [
            over_chips(part, *partners)
            for part, partners in zip(parts[1:], ((None, step), (step, None), (step, step)))
        ]

    from_core = near_row(dw_send)
    grad_far = far_row(far)
    parts = four_ways(share("core_sum", [dw_keep, from_core], 4, BF), 0)

    def over_mp(value, step):
        def target(i):
            return i // 4 * 4 + mp_partner(i // 4 % 2, i % 4, step)

        return move(value, SPACE + ("mp",), target)

    mp_keep, mp_send = call(
        input_kernel,
        "input_grad",
        [((4, ROW, WIDTH), F32), ((4, ROW, WIDTH), BF)],
        [att, gq, own, from_core, grad_far, wq, wk, wv, wo],
        flops=540_000_000,
        moved=4_000_000,
    )
    mp_keep, mp_send = share("mp_share", [mp_keep, over_mp(mp_send, 0)], 2, F32)
    parts = four_ways(share("first_sum", parts, 4, F32, FIRST_FLOPS), 1)
    keep, send = share("second_sum", parts, 2, F32, SECOND_FLOPS)
    got = over_chips(send, None, 2)
    output, grad_input = call(
        mp_sum_kernel, "mp_sum", [(square, BF)] * 2, [mp_keep, over_mp(mp_send, 1)], keep=False
    )
    (dw,) = call(last_sum_kernel, "last_sum", [((4,) + block, F32)], [keep, got], apart=(output,), keep=False)
    return output, grad_input, dw


def solution(mesh):
    fine = Mesh(mesh.devices.reshape(8, 4, 2, 4), SPACE + ("mp",))
    in_specs = (
        P(SPACE, None),
        P(None, "mp"),
        P(None, "mp"),
        P(None, "mp"),
        P("mp", None),
        P(SPACE, "mp"),
        P(SPACE, None),
        P(SPACE, None),
    )
    out_specs = (P(SPACE, "mp"), P(SPACE, "mp"), P(None, SPACE, "mp"))
    return jax.shard_map(body, mesh=fine, in_specs=in_specs, out_specs=out_specs, check_vma=False)
```

```python
import functools

import jax
import jax.numpy as jnp
from jax import lax
from jax.experimental import pallas as pl
from jax.experimental.pallas import tpu as pltpu
from jax.sharding import Mesh
from jax.sharding import PartitionSpec as P

HD = 64
PATCH = 64
D = 1024
ROW = 256
WIDTH = 256
HEADS = WIDTH // HD
FIRST_FLOPS, SECOND_FLOPS = 4_000_000_000, 4_000_000_000
KEYS = 3 * ROW
LOG2E = 1.4426950408889634
BF = jnp.bfloat16
F32 = jnp.float32
SPACE = ("z", "y", "core")

NN = (((1,), (0,)), ((), ()))
NT = (((1,), (1,)), ((), ()))


def mm(a, b, dims=NN):
    return lax.dot_general(a, b, dims, preferred_element_type=F32)


def places():
    return [lax.axis_index(a) for a in ("core", "y", "z", "mp")]


def slot_bias(nb, mask, core, y, z):
    row = (z * 4 + y) * 2 + core
    sign = 1 - 2 * core
    patch_of_lane = lax.broadcasted_iota(jnp.int32, (16, ROW), 1) // PATCH
    patch_of_row = lax.broadcasted_iota(jnp.int32, (16, ROW), 0)
    count = jnp.zeros((16, ROW), F32)
    for slot in range(9):
        named = jnp.zeros((16, ROW), jnp.int32)
        for patch in range(4):
            number = nb[patch, slot]
            band = 1 + sign * (lax.div(number, 4) - row)
            place = jnp.where(mask[patch, slot] > 0, band * 4 + lax.rem(number, 4), -1)
            named = jnp.where(patch_of_lane == patch, place, named)
        count += jnp.where(named == patch_of_row, 1.0, 0.0)
    return jnp.where(count > 0, jnp.where(count > 1, jnp.log(count) * LOG2E, 0.0), -1e30)


def y_pair(y):
    return y + 1 - 2 * (y % 2)


def y_other(y):
    return 3 - y


def z_pair(z):
    return z + 1 - 2 * (z % 2)


def z_other(z):
    return (z + 7 + 2 * (z % 2)) % 8


def z_far(z):
    middle = (z % 4) * (3 - z % 4) // 2
    return (1 - middle) * (3 - 2 * (z % 4) + z) + middle * (7 - z)


def z_far_too(z):
    return z + 4 + (1 - 2 * (z % 2)) - 8 * (z // 4)


def target_rows(z, y, y_partners, z_partners):
    def reached(start, partners):
        places = [start]
        for partner in partners:
            places = [there for here in places for there in (here, partner(here))]
        return places

    ys, zs = reached(y, y_partners), reached(z, z_partners)
    rows = []
    for number in range(32):
        y1, z1, y2, z2, z3 = ((number >> (4 - bit)) & 1 for bit in range(5))
        rows.append(zs[4 * z1 + 2 * z2 + z3] * 4 + ys[2 * y1 + y2])
    return rows


PARTNERS = (
    ((y_pair, y_other), (z_other, z_pair, z_far_too)),
    ((y_other, y_pair), (z_pair, z_other, z_far)),
)


def mp_partner(core, x, step):
    near, across = x ^ 1, 3 - x
    if isinstance(core, int):
        return (near, across)[(core + step) % 2]
    return jnp.where(core == step, near, across)


def columns(ref, place):
    return ref[:, pl.ds(pl.multiple_of(place * WIDTH, WIDTH), WIDTH)]


def head_lanes():
    return lax.broadcasted_iota(jnp.int32, (ROW, WIDTH), 1) // HD


def stack_heads(rows, out):
    for head in range(HEADS):
        out[head * ROW : (head + 1) * ROW, :] = jnp.where(head_lanes() == head, rows, jnp.zeros_like(rows))


def pick_heads(stacked):
    total = jnp.zeros((ROW, WIDTH), F32)
    for head in range(HEADS):
        total = jnp.where(head_lanes() == head, stacked[head * ROW : (head + 1) * ROW], total)
    return total.astype(BF)


def own_kernel(
    act, w_q, w_k, w_v, w_o, cot, slots, live, a_near,
    wq, wk, wv, wo, query_out, keys_out, values_out, act_t, near_t, grad_out, cot_t, bias_out,
    act_s, cot_s, nb, mask, sems,
):
    core, y, z, x = places()
    pairs = (
        (slots, nb), (live, mask), (act, act_s), (w_k, wk), (w_v, wv), (w_q, wq), (cot, cot_s), (w_o, wo)
    )
    copies = [pltpu.make_async_copy(a, b, sems.at[i]) for i, (a, b) in enumerate(pairs)]
    for copy in copies:
        copy.start()
    near_t[...] = a_near[...].T
    copies[0].wait()
    copies[1].wait()
    bias_out[...] = slot_bias(nb, mask, core, y, z)
    copies[2].wait()
    act_t[...] = act_s[...].T
    for index, weight, out in ((3, wk, keys_out), (4, wv, values_out)):
        copies[index].wait()
        out[:ROW, :] = mm(act_s[...], weight[...]).astype(BF)
        out[ROW:, :] = mm(a_near[...], weight[...]).astype(BF)
    copies[5].wait()
    stack_heads(mm(act_s[...], wq[...]).astype(BF), query_out)
    copies[6].wait()
    cot_t[...] = cot_s[...].T
    copies[7].wait()
    grad_out[...] = mm(cot_s[...], columns(wo, x), NT)


def forward_kernel(
    a_far, wk, wv, query, keys_in, values_in, bias,
    keys, values, probs_out, att_out, far_t,
    probs_t,
):
    keys[ROW:, :] = keys_in[...]
    values[ROW:, :] = values_in[...]
    keys[:ROW, :] = mm(a_far[...], wk[...]).astype(BF)
    values[:ROW, :] = mm(a_far[...], wv[...]).astype(BF)
    bias_rows = jnp.concatenate(
        [jnp.broadcast_to(bias[patch : patch + 1, :], (PATCH, ROW)) for patch in range(KEYS // PATCH)],
        axis=0,
    )
    for head in range(HEADS):
        part = slice(head * ROW, (head + 1) * ROW)
        scores = mm(keys[...], query[part, :], NT) * (LOG2E * HD**-0.5) + bias_rows
        peak = jnp.max(scores, axis=0, keepdims=True)
        weights = jnp.exp2(scores - peak)
        probs = (weights * (1.0 / jnp.sum(weights, axis=0, keepdims=True))).astype(BF)
        probs_out[:, part] = probs
        probs_t[part, :] = probs.T
    att_out[...] = pick_heads(mm(probs_t[...], values[...]))
    far_t[...] = a_far[...].T


def backward_kernel(
    keys, values, probs_in, att, far_t, near_t, wo, query, act_t, grad_in, cot_t, c1, c2, c3,
    gq_out, far_out, own_out, send_out, keep_out,
    grad_s, scores_s, scores_t, dw_s,
):
    core, y, z, x = places()
    grad_att = grad_in[...]
    blocks = ((mp_partner(core, x, 0), c1), (mp_partner(core, x, 1), c2), (x ^ 2, c3))
    for place, block in blocks:
        grad_att += mm(block[...], columns(wo, place), NT)
    stack_heads(grad_att.astype(BF), grad_s)
    for head in range(HEADS):
        part = slice(head * ROW, (head + 1) * ROW)
        probs = probs_in[:, part].astype(F32)
        grad_probs = mm(values[...], grad_s[part, :], NT)
        centre = jnp.sum(probs * grad_probs, axis=0, keepdims=True)
        grad_scores = (probs * ((grad_probs - centre) * HD**-0.5)).astype(BF)
        scores_s[:, part] = grad_scores
        scores_t[part, :] = grad_scores.T
    gq = pick_heads(mm(scores_t[...], keys[...]))
    grad_key = mm(scores_s[...], query[...])
    grad_value = mm(probs_in[...], grad_s[...])
    gq_out[...] = gq
    far_out[0], far_out[1] = grad_key[:ROW].astype(BF), grad_value[:ROW].astype(BF)
    own_out[0], own_out[1] = grad_key[ROW : 2 * ROW], grad_value[ROW : 2 * ROW]
    for part, grad in enumerate((grad_key, grad_value)):
        for block in range(16):
            rows = slice(2 * ROW + 16 * block, 2 * ROW + 16 * (block + 1))
            send_out[128 + 16 * part + block] = grad[rows].astype(BF)

    for place, block_t in ((x, cot_t[...]), *((place, block[...].T) for place, block in blocks)):
        rows = pl.ds(pl.multiple_of(place * WIDTH, WIDTH), WIDTH)
        dw_s[3, rows, :] = mm(block_t, att[...])
    grad_key = grad_key.astype(BF)
    grad_value = grad_value.astype(BF)
    own = slice(ROW, 2 * ROW)
    dw_s[0] = mm(act_t[...], gq)
    for index, grad in ((1, grad_key), (2, grad_value)):
        dw_s[index] = (
            mm(act_t[...], grad[own]) + mm(far_t[...], grad[:ROW]) + mm(near_t[...], grad[2 * ROW :])
        )
    tables = [target_rows(z, y, *partners) for partners in PARTNERS]
    for number in range(32):
        first, second = (table[number] * 32 for table in tables)
        for c, out in ((1 - core, send_out), (core, keep_out)):
            row = pl.multiple_of(jnp.where(c == 0, first, second) + c * 16, 16)
            out[4 * number : 4 * number + 4] = dw_s[:, pl.ds(row, 16), :].astype(BF)


def share_kernel(count, *refs):
    terms, outs = refs[:count], refs[count:]
    size = outs[0].shape[0]
    for place, out in enumerate(outs):
        part = slice(size * place, size * (place + 1))
        total = terms[0][part].astype(F32)
        for term in terms[1:]:
            total += term[part].astype(F32)
        out[...] = total.astype(out.dtype)


def input_kernel(att, gq, own, near, far, wq, wk, wv, wo, keep, send):
    core, _, _, x = places()
    grads = []
    for part in range(2):
        from_near = near[128 + 16 * part : 144 + 16 * part].reshape(ROW, WIDTH)
        grads.append((own[part] + from_near.astype(F32) + far[part].astype(F32)).astype(BF))
    grad_key, grad_value = grads
    first, second = (mp_partner(core, x, step) for step in range(2))
    for out, targets in ((keep, (x, second)), (send, (first, x ^ 2))):
        for place, target in enumerate(targets):
            block = pl.ds(pl.multiple_of(target * WIDTH, WIDTH), WIDTH)
            out[2 * place] = mm(att[...], wo[:, block]).astype(out.dtype)
            out[2 * place + 1] = (
                mm(gq[...], wq[block, :], NT)
                + mm(grad_key, wk[block, :], NT)
                + mm(grad_value, wv[block, :], NT)
            ).astype(out.dtype)


def mp_sum_kernel(kept, got, out, grad):
    for part, ref in ((0, out), (1, grad)):
        ref[...] = (kept[part] + got[part].astype(F32)).astype(BF)


def last_sum_kernel(after, kept, got, dw):
    dw[...] = kept[...] + got[...].astype(F32)


def on_chip(*arrays):
    return [pltpu.with_memory_space_constraint(a, pltpu.VMEM) for a in arrays]


def call(
    kernel, name, outs, arrays, apart=(), scratch=(), limit=16, flops=0, moved=1_000_000, keep=True
):
    kept = [pltpu.VMEM(shape, dtype) if keep else jax.ShapeDtypeStruct(shape, dtype) for shape, dtype in outs]
    return pl.pallas_call(
        kernel,
        out_shape=tuple(kept),
        in_specs=[pl.BlockSpec(memory_space=pltpu.HBM)] * len(apart)
        + [pl.BlockSpec(memory_space=pltpu.VMEM)] * len(arrays),
        out_specs=(pl.BlockSpec(memory_space=pltpu.VMEM),) * len(kept),
        scratch_shapes=list(scratch),
        compiler_params=pltpu.CompilerParams(vmem_limit_bytes=limit * 1024 * 1024),
        cost_estimate=pl.CostEstimate(flops=flops, bytes_accessed=moved, transcendentals=0),
        name=name,
    )(*[pltpu.with_memory_space_constraint(a, pltpu.HBM) for a in apart], *on_chip(*arrays))


def hold_kernel(after, value, out):
    pass


def hold(value, after):
    return pl.pallas_call(
        hold_kernel,
        out_shape=pltpu.VMEM(value.shape, value.dtype),
        in_specs=[pl.BlockSpec(memory_space=pltpu.VMEM)] * 2,
        out_specs=pl.BlockSpec(memory_space=pltpu.VMEM),
        input_output_aliases={1: 0},
        name="hold",
    )(*on_chip(after, value))


def move(value, axis, target):
    count = lax.axis_size(axis)
    return lax.ppermute(
        value, axis, [(i, target(i)) for i in range(count) if 0 <= target(i) < count]
    )


def over_mp(value, step):
    def target(i):
        return i // 4 * 4 + mp_partner(i // 4 % 2, i % 4, step)

    return move(value, SPACE + ("mp",), target)


def near_row(value):
    return move(value, SPACE, lambda i: i ^ 1)


def far_row(value):
    return move(value, SPACE, lambda i: i + 1 if i % 2 else i - 1)


def body(activations, w_query, w_key, w_value, w_out, grad_output, neighbours, pad_mask):
    act_far = far_row(activations)
    cots = [over_mp(grad_output, 0), over_mp(grad_output, 1)]
    act_near = near_row(activations)

    square = (ROW, WIDTH)
    stacked = (HEADS * ROW, WIDTH)
    wq, wk, wv, wo, query, keys, values, act_t, near_t, grad_own, cot_t, bias = call(
        own_kernel,
        "own_part",
        [((D, WIDTH), BF)] * 3
        + [((WIDTH, D), BF), (stacked, BF), ((2 * ROW, WIDTH), BF), ((2 * ROW, WIDTH), BF)]
        + [((D, ROW), BF), ((D, ROW), BF), (square, F32), (square, BF), ((16, ROW), F32)],
        [act_near],
        apart=(activations, w_query, w_key, w_value, w_out, grad_output, neighbours, pad_mask),
        scratch=[
            pltpu.VMEM((ROW, D), BF),
            pltpu.VMEM(square, BF),
            pltpu.SMEM((4, 9), jnp.int32),
            pltpu.SMEM((4, 9), jnp.int32),
            pltpu.SemaphoreType.DMA((8,)),
        ],
        flops=600_000_000,
        moved=6_000_000,
    )

    cots[1] = hold(cots[1], bias)
    cots.append(over_mp(cots[1], 0))

    block = (16, WIDTH)
    keys, values, probs, att, far_t = call(
        forward_kernel,
        "forward",
        [((KEYS, WIDTH), BF)] * 2 + [((KEYS, HEADS * ROW), BF), (square, BF), ((D, ROW), BF)],
        [act_far, wk, wv, query, keys, values, bias],
        scratch=[pltpu.VMEM((HEADS * ROW, KEYS), BF)],
        limit=20,
        flops=2_000_000_000,
        moved=6_000_000,
    )
    gq, far, own, dw_send, dw_keep = call(
        backward_kernel,
        "backward",
        [
            (square, BF),
            ((2, ROW, WIDTH), BF),
            ((2, ROW, WIDTH), F32),
            ((160,) + block, BF),
            ((128,) + block, BF),
        ],
        [keys, values, probs, att, far_t, near_t, wo, query, act_t, grad_own, cot_t, *cots],
        scratch=[
            pltpu.VMEM(stacked, BF),
            pltpu.VMEM((KEYS, HEADS * ROW), BF),
            pltpu.VMEM((HEADS * ROW, KEYS), BF),
            pltpu.VMEM((4, D, WIDTH), F32),
        ],
        limit=24,
        flops=3_000_000_000,
        moved=8_000_000,
    )

    def share(name, terms, ways, kept_as, flops=0):
        part = (terms[0].shape[0] // ways,) + terms[0].shape[1:]
        outs = [(part, kept_as)] + [(part, BF)] * (ways - 1)
        return call(functools.partial(share_kernel, len(terms)), name, outs, terms, flops=flops)

    def over_chips(value, y_step, z_step):
        def target(i):
            z, y, c = i // 8, i // 2 % 4, i % 2
            y_partners, z_partners = PARTNERS[c]
            y = y if y_step is None else y_partners[y_step](y)
            z = z if z_step is None else z_partners[z_step](z)
            return z * 8 + y * 2 + c

        return move(value, SPACE, target)

    def four_ways(parts, step):
        along_z, along_y = over_chips(parts[1], None, step), over_chips(parts[2], step, None)
        return [parts[0], over_chips(parts[3], step, step), along_y, along_z]

    from_core = near_row(dw_send)
    grad_far = far_row(far)
    parts = four_ways(share("core_sum", [dw_keep, from_core], 4, BF), 0)

    mp_keep, mp_send = call(
        input_kernel,
        "input_grad",
        [((4, ROW, WIDTH), F32), ((4, ROW, WIDTH), BF)],
        [att, gq, own, from_core, grad_far, wq, wk, wv, wo],
        flops=540_000_000,
        moved=4_000_000,
    )
    mp_keep, mp_send = share("mp_share", [mp_keep, over_mp(mp_send, 0)], 2, F32)
    parts = four_ways(share("first_sum", parts, 4, F32, FIRST_FLOPS), 1)
    keep, send = share("second_sum", parts, 2, F32, SECOND_FLOPS)
    got = over_chips(send, None, 2)
    output, grad_input = call(
        mp_sum_kernel, "mp_sum", [(square, BF)] * 2, [mp_keep, over_mp(mp_send, 1)], keep=False
    )
    (dw,) = call(last_sum_kernel, "last_sum", [((4,) + block, F32)], [keep, got], apart=(output,), keep=False)
    return output, grad_input, dw


def solution(mesh):
    fine = Mesh(mesh.devices.reshape(8, 4, 2, 4), SPACE + ("mp",))
    in_specs = (
        P(SPACE, None),
        P(None, "mp"),
        P(None, "mp"),
        P(None, "mp"),
        P("mp", None),
        P(SPACE, "mp"),
        P(SPACE, None),
        P(SPACE, None),
    )
    out_specs = (P(SPACE, "mp"), P(SPACE, "mp"), P(None, SPACE, "mp"))
    return jax.shard_map(body, mesh=fine, in_specs=in_specs, out_specs=out_specs, check_vma=False)
```

```python
import functools

import jax
import jax.numpy as jnp
from jax import lax
from jax.experimental import pallas as pl
from jax.experimental.pallas import tpu as pltpu
from jax.sharding import Mesh
from jax.sharding import PartitionSpec as P

HD = 64
PATCH = 64
D = 1024
ROW = 256
WIDTH = 256
HEADS = WIDTH // HD
FIRST_FLOPS, SECOND_FLOPS = 4_000_000_000, 4_000_000_000
KEYS = 3 * ROW
LOG2E = 1.4426950408889634
BF = jnp.bfloat16
F32 = jnp.float32
SPACE = ("z", "y", "core")

NN = (((1,), (0,)), ((), ()))
NT = (((1,), (1,)), ((), ()))


def mm(a, b, dims=NN):
    return lax.dot_general(a, b, dims, preferred_element_type=F32)


def places():
    return [lax.axis_index(a) for a in ("core", "y", "z", "mp")]


def slot_bias(nb, mask, core, y, z):
    row = (z * 4 + y) * 2 + core
    sign = 1 - 2 * core
    patch_of_lane = lax.broadcasted_iota(jnp.int32, (16, ROW), 1) // PATCH
    patch_of_row = lax.broadcasted_iota(jnp.int32, (16, ROW), 0)
    count = jnp.zeros((16, ROW), F32)
    for slot in range(9):
        named = jnp.zeros((16, ROW), jnp.int32)
        for patch in range(4):
            number = nb[patch, slot]
            band = 1 + sign * (lax.div(number, 4) - row)
            place = jnp.where(mask[patch, slot] > 0, band * 4 + lax.rem(number, 4), -1)
            named = jnp.where(patch_of_lane == patch, place, named)
        count += jnp.where(named == patch_of_row, 1.0, 0.0)
    return jnp.where(count > 0, jnp.where(count > 1, jnp.log(count) * LOG2E, 0.0), -1e30)


def y_pair(y):
    return y + 1 - 2 * (y % 2)


def y_other(y):
    return 3 - y


def z_pair(z):
    return z + 1 - 2 * (z % 2)


def z_other(z):
    return (z + 7 + 2 * (z % 2)) % 8


def z_far(z):
    middle = (z % 4) * (3 - z % 4) // 2
    return (1 - middle) * (3 - 2 * (z % 4) + z) + middle * (7 - z)


def z_far_too(z):
    return z + 4 + (1 - 2 * (z % 2)) - 8 * (z // 4)


def target_rows(z, y, y_partners, z_partners):
    def reached(start, partners):
        places = [start]
        for partner in partners:
            places = [there for here in places for there in (here, partner(here))]
        return places

    ys, zs = reached(y, y_partners), reached(z, z_partners)
    rows = []
    for number in range(32):
        y1, z1, y2, z2, z3 = ((number >> (4 - bit)) & 1 for bit in range(5))
        rows.append(zs[4 * z1 + 2 * z2 + z3] * 4 + ys[2 * y1 + y2])
    return rows


PARTNERS = (
    ((y_pair, y_other), (z_other, z_pair, z_far_too)),
    ((y_other, y_pair), (z_pair, z_other, z_far)),
)


def mp_partner(core, x, step):
    near, across = x ^ 1, 3 - x
    if isinstance(core, int):
        return (near, across)[(core + step) % 2]
    return jnp.where(core == step, near, across)


def columns(ref, place):
    return ref[:, pl.ds(pl.multiple_of(place * WIDTH, WIDTH), WIDTH)]


def head_lanes():
    return lax.broadcasted_iota(jnp.int32, (ROW, WIDTH), 1) // HD


def stack_heads(rows, out):
    for head in range(HEADS):
        out[head * ROW : (head + 1) * ROW, :] = jnp.where(head_lanes() == head, rows, jnp.zeros_like(rows))


def pick_heads(stacked):
    total = jnp.zeros((ROW, WIDTH), F32)
    for head in range(HEADS):
        total = jnp.where(head_lanes() == head, stacked[head * ROW : (head + 1) * ROW], total)
    return total.astype(BF)


def own_kernel(
    act, w_q, w_k, w_v, w_o, cot, slots, live, a_near,
    wq, wk, wv, wo, query_out, keys_out, values_out, act_t, near_t, grad_out, cot_t, bias_out,
    act_s, cot_s, nb, mask, sems,
):
    core, y, z, x = places()
    pairs = (
        (slots, nb), (live, mask), (act, act_s), (w_k, wk), (w_v, wv), (w_q, wq), (cot, cot_s), (w_o, wo)
    )
    copies = [pltpu.make_async_copy(a, b, sems.at[i]) for i, (a, b) in enumerate(pairs)]
    for copy in copies:
        copy.start()
    near_t[...] = a_near[...].T
    copies[0].wait()
    copies[1].wait()
    bias_out[...] = slot_bias(nb, mask, core, y, z)
    copies[2].wait()
    act_t[...] = act_s[...].T
    for index, weight, out in ((3, wk, keys_out), (4, wv, values_out)):
        copies[index].wait()
        out[:ROW, :] = mm(act_s[...], weight[...]).astype(BF)
        out[ROW:, :] = mm(a_near[...], weight[...]).astype(BF)
    copies[5].wait()
    stack_heads(mm(act_s[...], wq[...]).astype(BF), query_out)
    copies[6].wait()
    cot_t[...] = cot_s[...].T
    copies[7].wait()
    grad_out[...] = mm(cot_s[...], columns(wo, x), NT)


def forward_kernel(
    a_far, wk, wv, query, keys_in, values_in, bias,
    keys, values, probs_out, att_out, far_t,
    probs_t,
):
    keys[ROW:, :] = keys_in[...]
    values[ROW:, :] = values_in[...]
    keys[:ROW, :] = mm(a_far[...], wk[...]).astype(BF)
    values[:ROW, :] = mm(a_far[...], wv[...]).astype(BF)
    bias_rows = jnp.concatenate(
        [jnp.broadcast_to(bias[patch : patch + 1, :], (PATCH, ROW)) for patch in range(KEYS // PATCH)],
        axis=0,
    )
    for head in range(HEADS):
        part = slice(head * ROW, (head + 1) * ROW)
        scores = mm(keys[...], query[part, :], NT) * (LOG2E * HD**-0.5) + bias_rows
        peak = jnp.max(scores, axis=0, keepdims=True)
        weights = jnp.exp2(scores - peak)
        probs = (weights * (1.0 / jnp.sum(weights, axis=0, keepdims=True))).astype(BF)
        probs_out[:, part] = probs
        probs_t[part, :] = probs.T
    att_out[...] = pick_heads(mm(probs_t[...], values[...]))
    far_t[...] = a_far[...].T


def backward_kernel(
    keys, values, probs_in, att, far_t, near_t, wo, query, act_t, grad_in, cot_t, c1, c2, c3,
    gq_out, far_out, own_out, send_out, keep_out,
    grad_s, scores_s, scores_t, dw_s,
):
    core, y, z, x = places()
    grad_att = grad_in[...]
    blocks = ((mp_partner(core, x, 0), c1), (mp_partner(core, x, 1), c2), (x ^ 2, c3))
    for place, block in blocks:
        grad_att += mm(block[...], columns(wo, place), NT)
    stack_heads(grad_att.astype(BF), grad_s)
    for head in range(HEADS):
        part = slice(head * ROW, (head + 1) * ROW)
        probs = probs_in[:, part].astype(F32)
        grad_probs = mm(values[...], grad_s[part, :], NT)
        centre = jnp.sum(probs * grad_probs, axis=0, keepdims=True)
        grad_scores = (probs * ((grad_probs - centre) * HD**-0.5)).astype(BF)
        scores_s[:, part] = grad_scores
        scores_t[part, :] = grad_scores.T
    gq = pick_heads(mm(scores_t[...], keys[...]))
    grad_key = mm(scores_s[...], query[...])
    grad_value = mm(probs_in[...], grad_s[...])
    gq_out[...] = gq
    far_out[0], far_out[1] = grad_key[:ROW].astype(BF), grad_value[:ROW].astype(BF)
    own_out[0], own_out[1] = grad_key[ROW : 2 * ROW], grad_value[ROW : 2 * ROW]
    for part, grad in enumerate((grad_key, grad_value)):
        for block in range(16):
            rows = slice(2 * ROW + 16 * block, 2 * ROW + 16 * (block + 1))
            send_out[128 + 16 * part + block] = grad[rows].astype(BF)

    for place, block_t in ((x, cot_t[...]), *((place, block[...].T) for place, block in blocks)):
        rows = pl.ds(pl.multiple_of(place * WIDTH, WIDTH), WIDTH)
        dw_s[3, rows, :] = mm(block_t, att[...])
    grad_key = grad_key.astype(BF)
    grad_value = grad_value.astype(BF)
    own = slice(ROW, 2 * ROW)
    dw_s[0] = mm(act_t[...], gq)
    for index, grad in ((1, grad_key), (2, grad_value)):
        dw_s[index] = (
            mm(act_t[...], grad[own]) + mm(far_t[...], grad[:ROW]) + mm(near_t[...], grad[2 * ROW :])
        )
    tables = [target_rows(z, y, *partners) for partners in PARTNERS]
    for number in range(32):
        first, second = (table[number] * 32 for table in tables)
        for c, out in ((1 - core, send_out), (core, keep_out)):
            row = pl.multiple_of(jnp.where(c == 0, first, second) + c * 16, 16)
            out[4 * number : 4 * number + 4] = dw_s[:, pl.ds(row, 16), :].astype(BF)


def share_kernel(count, *refs):
    terms, outs = refs[:count], refs[count:]
    size = outs[0].shape[0]
    for place, out in enumerate(outs):
        part = slice(size * place, size * (place + 1))
        total = terms[0][part].astype(F32)
        for term in terms[1:]:
            total += term[part].astype(F32)
        out[...] = total.astype(out.dtype)


def input_kernel(att, gq, own, near, far, wq, wk, wv, wo, keep, send):
    core, _, _, x = places()
    grads = []
    for part in range(2):
        from_near = near[128 + 16 * part : 144 + 16 * part].reshape(ROW, WIDTH)
        grads.append((own[part] + from_near.astype(F32) + far[part].astype(F32)).astype(BF))
    grad_key, grad_value = grads
    first, second = (mp_partner(core, x, step) for step in range(2))
    for out, targets in ((keep, (x, second)), (send, (first, x ^ 2))):
        for place, target in enumerate(targets):
            block = pl.ds(pl.multiple_of(target * WIDTH, WIDTH), WIDTH)
            out[2 * place] = mm(att[...], wo[:, block]).astype(out.dtype)
            out[2 * place + 1] = (
                mm(gq[...], wq[block, :], NT)
                + mm(grad_key, wk[block, :], NT)
                + mm(grad_value, wv[block, :], NT)
            ).astype(out.dtype)


def mp_sum_kernel(kept, got, out, grad):
    for part, ref in ((0, out), (1, grad)):
        ref[...] = (kept[part] + got[part].astype(F32)).astype(BF)


def last_sum_kernel(after, kept, got, dw):
    dw[...] = kept[...] + got[...].astype(F32)


def on_chip(*arrays):
    return [pltpu.with_memory_space_constraint(a, pltpu.VMEM) for a in arrays]


def call(
    kernel, name, outs, arrays, apart=(), scratch=(), limit=16, flops=0, moved=1_000_000, keep=True
):
    kept = [pltpu.VMEM(shape, dtype) if keep else jax.ShapeDtypeStruct(shape, dtype) for shape, dtype in outs]
    return pl.pallas_call(
        kernel,
        out_shape=tuple(kept),
        in_specs=[pl.BlockSpec(memory_space=pltpu.HBM)] * len(apart)
        + [pl.BlockSpec(memory_space=pltpu.VMEM)] * len(arrays),
        out_specs=(pl.BlockSpec(memory_space=pltpu.VMEM),) * len(kept),
        scratch_shapes=list(scratch),
        compiler_params=pltpu.CompilerParams(vmem_limit_bytes=limit * 1024 * 1024),
        cost_estimate=pl.CostEstimate(flops=flops, bytes_accessed=moved, transcendentals=0),
        name=name,
    )(*[pltpu.with_memory_space_constraint(a, pltpu.HBM) for a in apart], *on_chip(*arrays))


def hold_kernel(after, value, out):
    pass


def hold(value, after):
    return pl.pallas_call(
        hold_kernel,
        out_shape=pltpu.VMEM(value.shape, value.dtype),
        in_specs=[pl.BlockSpec(memory_space=pltpu.VMEM)] * 2,
        out_specs=pl.BlockSpec(memory_space=pltpu.VMEM),
        input_output_aliases={1: 0},
        compiler_params=pltpu.CompilerParams(vmem_limit_bytes=1024 * 1024),
        name="hold",
    )(*on_chip(after, value))


def move(value, axis, target):
    count = lax.axis_size(axis)
    return lax.ppermute(
        value, axis, [(i, target(i)) for i in range(count) if 0 <= target(i) < count]
    )


def over_mp(value, step):
    def target(i):
        return i // 4 * 4 + mp_partner(i // 4 % 2, i % 4, step)

    return move(value, SPACE + ("mp",), target)


def near_row(value):
    return move(value, SPACE, lambda i: i ^ 1)


def far_row(value):
    return move(value, SPACE, lambda i: i + 1 if i % 2 else i - 1)


def body(activations, w_query, w_key, w_value, w_out, grad_output, neighbours, pad_mask):
    act_far = far_row(activations)
    cots = [over_mp(grad_output, 0), over_mp(grad_output, 1)]
    act_near = near_row(activations)

    square = (ROW, WIDTH)
    stacked = (HEADS * ROW, WIDTH)
    wq, wk, wv, wo, query, keys, values, act_t, near_t, grad_own, cot_t, bias = call(
        own_kernel,
        "own_part",
        [((D, WIDTH), BF)] * 3
        + [((WIDTH, D), BF), (stacked, BF), ((2 * ROW, WIDTH), BF), ((2 * ROW, WIDTH), BF)]
        + [((D, ROW), BF), ((D, ROW), BF), (square, F32), (square, BF), ((16, ROW), F32)],
        [act_near],
        apart=(activations, w_query, w_key, w_value, w_out, grad_output, neighbours, pad_mask),
        scratch=[
            pltpu.VMEM((ROW, D), BF),
            pltpu.VMEM(square, BF),
            pltpu.SMEM((4, 9), jnp.int32),
            pltpu.SMEM((4, 9), jnp.int32),
            pltpu.SemaphoreType.DMA((8,)),
        ],
        flops=600_000_000,
        moved=6_000_000,
    )

    cots[1] = hold(cots[1], bias)
    cots.append(over_mp(cots[1], 0))

    block = (16, WIDTH)
    keys, values, probs, att, far_t = call(
        forward_kernel,
        "forward",
        [((KEYS, WIDTH), BF)] * 2 + [((KEYS, HEADS * ROW), BF), (square, BF), ((D, ROW), BF)],
        [act_far, wk, wv, query, keys, values, bias],
        scratch=[pltpu.VMEM((HEADS * ROW, KEYS), BF)],
        limit=20,
        flops=2_000_000_000,
        moved=6_000_000,
    )
    gq, far, own, dw_send, dw_keep = call(
        backward_kernel,
        "backward",
        [
            (square, BF),
            ((2, ROW, WIDTH), BF),
            ((2, ROW, WIDTH), F32),
            ((160,) + block, BF),
            ((128,) + block, BF),
        ],
        [keys, values, probs, att, far_t, near_t, wo, query, act_t, grad_own, cot_t, *cots],
        scratch=[
            pltpu.VMEM(stacked, BF),
            pltpu.VMEM((KEYS, HEADS * ROW), BF),
            pltpu.VMEM((HEADS * ROW, KEYS), BF),
            pltpu.VMEM((4, D, WIDTH), F32),
        ],
        limit=24,
        flops=3_000_000_000,
        moved=8_000_000,
    )

    def share(name, terms, ways, kept_as, flops=0):
        part = (terms[0].shape[0] // ways,) + terms[0].shape[1:]
        outs = [(part, kept_as)] + [(part, BF)] * (ways - 1)
        return call(functools.partial(share_kernel, len(terms)), name, outs, terms, flops=flops)

    def over_chips(value, y_step, z_step):
        def target(i):
            z, y, c = i // 8, i // 2 % 4, i % 2
            y_partners, z_partners = PARTNERS[c]
            y = y if y_step is None else y_partners[y_step](y)
            z = z if z_step is None else z_partners[z_step](z)
            return z * 8 + y * 2 + c

        return move(value, SPACE, target)

    def four_ways(parts, step):
        along_z, along_y = over_chips(parts[1], None, step), over_chips(parts[2], step, None)
        return [parts[0], over_chips(parts[3], step, step), along_y, along_z]

    from_core = near_row(dw_send)
    grad_far = far_row(far)
    parts = four_ways(share("core_sum", [dw_keep, from_core], 4, BF), 0)

    mp_keep, mp_send = call(
        input_kernel,
        "input_grad",
        [((4, ROW, WIDTH), F32), ((4, ROW, WIDTH), BF)],
        [att, gq, own, from_core, grad_far, wq, wk, wv, wo],
        flops=540_000_000,
        moved=4_000_000,
    )
    mp_keep, mp_send = share("mp_share", [mp_keep, over_mp(mp_send, 0)], 2, F32)
    parts = four_ways(share("first_sum", parts, 4, F32, FIRST_FLOPS), 1)
    keep, send = share("second_sum", parts, 2, F32, SECOND_FLOPS)
    got = over_chips(send, None, 2)
    output, grad_input = call(
        mp_sum_kernel, "mp_sum", [(square, BF)] * 2, [mp_keep, over_mp(mp_send, 1)], keep=False
    )
    (dw,) = call(last_sum_kernel, "last_sum", [((4,) + block, F32)], [keep, got], apart=(output,), keep=False)
    return output, grad_input, dw


def solution(mesh):
    fine = Mesh(mesh.devices.reshape(8, 4, 2, 4), SPACE + ("mp",))
    in_specs = (
        P(SPACE, None),
        P(None, "mp"),
        P(None, "mp"),
        P(None, "mp"),
        P("mp", None),
        P(SPACE, "mp"),
        P(SPACE, None),
        P(SPACE, None),
    )
    out_specs = (P(SPACE, "mp"), P(SPACE, "mp"), P(None, SPACE, "mp"))
    return jax.shard_map(body, mesh=fine, in_specs=in_specs, out_specs=out_specs, check_vma=False)
```

```python
import functools

import jax
import jax.numpy as jnp
from jax import lax
from jax.experimental import pallas as pl
from jax.experimental.pallas import tpu as pltpu
from jax.sharding import Mesh
from jax.sharding import PartitionSpec as P

HD = 64
PATCH = 64
D = 1024
ROW = 256
WIDTH = 256
HEADS = WIDTH // HD
FIRST_FLOPS, SECOND_FLOPS = 4_000_000_000, 4_000_000_000
KEYS = 3 * ROW
LOG2E = 1.4426950408889634
BF = jnp.bfloat16
F32 = jnp.float32
SPACE = ("z", "y", "core")

NN = (((1,), (0,)), ((), ()))
NT = (((1,), (1,)), ((), ()))


def mm(a, b, dims=NN):
    return lax.dot_general(a, b, dims, preferred_element_type=F32)


def places():
    return [lax.axis_index(a) for a in ("core", "y", "z", "mp")]


def slot_bias(nb, mask, core, y, z):
    row = (z * 4 + y) * 2 + core
    sign = 1 - 2 * core
    patch_of_lane = lax.broadcasted_iota(jnp.int32, (16, ROW), 1) // PATCH
    patch_of_row = lax.broadcasted_iota(jnp.int32, (16, ROW), 0)
    count = jnp.zeros((16, ROW), F32)
    for slot in range(9):
        named = jnp.zeros((16, ROW), jnp.int32)
        for patch in range(4):
            number = nb[patch, slot]
            band = 1 + sign * (lax.div(number, 4) - row)
            place = jnp.where(mask[patch, slot] > 0, band * 4 + lax.rem(number, 4), -1)
            named = jnp.where(patch_of_lane == patch, place, named)
        count += jnp.where(named == patch_of_row, 1.0, 0.0)
    return jnp.where(count > 0, jnp.where(count > 1, jnp.log(count) * LOG2E, 0.0), -1e30)


def y_pair(y):
    return y + 1 - 2 * (y % 2)


def y_other(y):
    return 3 - y


def z_pair(z):
    return z + 1 - 2 * (z % 2)


def z_other(z):
    return (z + 7 + 2 * (z % 2)) % 8


def z_far(z):
    middle = (z % 4) * (3 - z % 4) // 2
    return (1 - middle) * (3 - 2 * (z % 4) + z) + middle * (7 - z)


def z_far_too(z):
    return z + 4 + (1 - 2 * (z % 2)) - 8 * (z // 4)


def target_rows(z, y, y_partners, z_partners):
    def reached(start, partners):
        places = [start]
        for partner in partners:
            places = [there for here in places for there in (here, partner(here))]
        return places

    ys, zs = reached(y, y_partners), reached(z, z_partners)
    rows = []
    for number in range(32):
        y1, z1, y2, z2, z3 = ((number >> (4 - bit)) & 1 for bit in range(5))
        rows.append(zs[4 * z1 + 2 * z2 + z3] * 4 + ys[2 * y1 + y2])
    return rows


PARTNERS = (
    ((y_pair, y_other), (z_other, z_pair, z_far_too)),
    ((y_other, y_pair), (z_pair, z_other, z_far)),
)


def mp_partner(core, x, step):
    near, across = x ^ 1, 3 - x
    if isinstance(core, int):
        return (near, across)[(core + step) % 2]
    return jnp.where(core == step, near, across)


def columns(ref, place):
    return ref[:, pl.ds(pl.multiple_of(place * WIDTH, WIDTH), WIDTH)]


def head_lanes():
    return lax.broadcasted_iota(jnp.int32, (ROW, WIDTH), 1) // HD


def stack_heads(rows, out):
    for head in range(HEADS):
        out[head * ROW : (head + 1) * ROW, :] = jnp.where(head_lanes() == head, rows, jnp.zeros_like(rows))


def pick_heads(stacked):
    total = jnp.zeros((ROW, WIDTH), F32)
    for head in range(HEADS):
        total = jnp.where(head_lanes() == head, stacked[head * ROW : (head + 1) * ROW], total)
    return total.astype(BF)


def own_kernel(
    act, w_q, w_k, w_v, w_o, cot, slots, live, a_near,
    wq, wk, wv, wo, query_out, keys_out, values_out, act_t, near_t, grad_out, cot_t, bias_out,
    act_s, cot_s, nb, mask, sems,
):
    core, y, z, x = places()
    pairs = (
        (slots, nb), (live, mask), (act, act_s), (w_k, wk), (w_v, wv), (w_q, wq), (cot, cot_s), (w_o, wo)
    )
    copies = [pltpu.make_async_copy(a, b, sems.at[i]) for i, (a, b) in enumerate(pairs)]
    for copy in copies:
        copy.start()
    near_t[...] = a_near[...].T
    copies[0].wait()
    copies[1].wait()
    bias_out[...] = slot_bias(nb, mask, core, y, z)
    copies[2].wait()
    act_t[...] = act_s[...].T
    for index, weight, out in ((3, wk, keys_out), (4, wv, values_out)):
        copies[index].wait()
        out[:ROW, :] = mm(act_s[...], weight[...]).astype(BF)
        out[ROW:, :] = mm(a_near[...], weight[...]).astype(BF)
    copies[5].wait()
    stack_heads(mm(act_s[...], wq[...]).astype(BF), query_out)
    copies[6].wait()
    cot_t[...] = cot_s[...].T
    copies[7].wait()
    grad_out[...] = mm(cot_s[...], columns(wo, x), NT)


def forward_kernel(
    a_far, wk, wv, query, keys_in, values_in, bias,
    keys, values, probs_out, att_out, far_t,
    probs_t,
):
    keys[ROW:, :] = keys_in[...]
    values[ROW:, :] = values_in[...]
    keys[:ROW, :] = mm(a_far[...], wk[...]).astype(BF)
    values[:ROW, :] = mm(a_far[...], wv[...]).astype(BF)
    bias_rows = jnp.concatenate(
        [jnp.broadcast_to(bias[patch : patch + 1, :], (PATCH, ROW)) for patch in range(KEYS // PATCH)],
        axis=0,
    )
    for head in range(HEADS):
        part = slice(head * ROW, (head + 1) * ROW)
        scores = mm(keys[...], query[part, :], NT) * (LOG2E * HD**-0.5) + bias_rows
        peak = jnp.max(scores, axis=0, keepdims=True)
        weights = jnp.exp2(scores - peak)
        probs = (weights * (1.0 / jnp.sum(weights, axis=0, keepdims=True))).astype(BF)
        probs_out[:, part] = probs
        probs_t[part, :] = probs.T
    att_out[...] = pick_heads(mm(probs_t[...], values[...]))
    far_t[...] = a_far[...].T


def backward_kernel(
    keys, values, probs_in, att, far_t, near_t, wo, query, act_t, grad_in, cot_t, c2, c1, c3,
    gq_out, far_out, own_out, send_out, keep_out,
    grad_s, scores_s, scores_t, dw_s,
):
    core, y, z, x = places()
    grad_att = grad_in[...]
    blocks = ((x ^ 2, c2), (x ^ 1, c1), (x ^ 3, c3))
    for place, block in blocks:
        grad_att += mm(block[...], columns(wo, place), NT)
    stack_heads(grad_att.astype(BF), grad_s)
    for head in range(HEADS):
        part = slice(head * ROW, (head + 1) * ROW)
        probs = probs_in[:, part].astype(F32)
        grad_probs = mm(values[...], grad_s[part, :], NT)
        centre = jnp.sum(probs * grad_probs, axis=0, keepdims=True)
        grad_scores = (probs * ((grad_probs - centre) * HD**-0.5)).astype(BF)
        scores_s[:, part] = grad_scores
        scores_t[part, :] = grad_scores.T
    gq = pick_heads(mm(scores_t[...], keys[...]))
    grad_key = mm(scores_s[...], query[...])
    grad_value = mm(probs_in[...], grad_s[...])
    gq_out[...] = gq
    far_out[0], far_out[1] = grad_key[:ROW].astype(BF), grad_value[:ROW].astype(BF)
    own_out[0], own_out[1] = grad_key[ROW : 2 * ROW], grad_value[ROW : 2 * ROW]
    for part, grad in enumerate((grad_key, grad_value)):
        for block in range(16):
            rows = slice(2 * ROW + 16 * block, 2 * ROW + 16 * (block + 1))
            send_out[128 + 16 * part + block] = grad[rows].astype(BF)

    for place, block_t in ((x, cot_t[...]), *((place, block[...].T) for place, block in blocks)):
        rows = pl.ds(pl.multiple_of(place * WIDTH, WIDTH), WIDTH)
        dw_s[3, rows, :] = mm(block_t, att[...])
    grad_key = grad_key.astype(BF)
    grad_value = grad_value.astype(BF)
    own = slice(ROW, 2 * ROW)
    dw_s[0] = mm(act_t[...], gq)
    for index, grad in ((1, grad_key), (2, grad_value)):
        dw_s[index] = (
            mm(act_t[...], grad[own]) + mm(far_t[...], grad[:ROW]) + mm(near_t[...], grad[2 * ROW :])
        )
    tables = [target_rows(z, y, *partners) for partners in PARTNERS]
    for number in range(32):
        first, second = (table[number] * 32 for table in tables)
        for c, out in ((1 - core, send_out), (core, keep_out)):
            row = pl.multiple_of(jnp.where(c == 0, first, second) + c * 16, 16)
            out[4 * number : 4 * number + 4] = dw_s[:, pl.ds(row, 16), :].astype(BF)


def share_kernel(count, *refs):
    terms, outs = refs[:count], refs[count:]
    size = outs[0].shape[0]
    for place, out in enumerate(outs):
        part = slice(size * place, size * (place + 1))
        total = terms[0][part].astype(F32)
        for term in terms[1:]:
            total += term[part].astype(F32)
        out[...] = total.astype(out.dtype)


def input_kernel(att, gq, own, near, far, wq, wk, wv, wo, keep, send):
    core, _, _, x = places()
    grads = []
    for part in range(2):
        from_near = near[128 + 16 * part : 144 + 16 * part].reshape(ROW, WIDTH)
        grads.append((own[part] + from_near.astype(F32) + far[part].astype(F32)).astype(BF))
    grad_key, grad_value = grads
    first, second = (mp_partner(core, x, step) for step in range(2))
    for out, targets in ((keep, (x, second)), (send, (first, x ^ 2))):
        for place, target in enumerate(targets):
            block = pl.ds(pl.multiple_of(target * WIDTH, WIDTH), WIDTH)
            out[2 * place] = mm(att[...], wo[:, block]).astype(out.dtype)
            out[2 * place + 1] = (
                mm(gq[...], wq[block, :], NT)
                + mm(grad_key, wk[block, :], NT)
                + mm(grad_value, wv[block, :], NT)
            ).astype(out.dtype)


def mp_sum_kernel(kept, got, out, grad):
    for part, ref in ((0, out), (1, grad)):
        ref[...] = (kept[part] + got[part].astype(F32)).astype(BF)


def last_sum_kernel(after, kept, got, dw):
    dw[...] = kept[...] + got[...].astype(F32)


def on_chip(*arrays):
    return [pltpu.with_memory_space_constraint(a, pltpu.VMEM) for a in arrays]


def call(
    kernel, name, outs, arrays, apart=(), scratch=(), limit=16, flops=0, moved=1_000_000, keep=True
):
    kept = [pltpu.VMEM(shape, dtype) if keep else jax.ShapeDtypeStruct(shape, dtype) for shape, dtype in outs]
    return pl.pallas_call(
        kernel,
        out_shape=tuple(kept),
        in_specs=[pl.BlockSpec(memory_space=pltpu.HBM)] * len(apart)
        + [pl.BlockSpec(memory_space=pltpu.VMEM)] * len(arrays),
        out_specs=(pl.BlockSpec(memory_space=pltpu.VMEM),) * len(kept),
        scratch_shapes=list(scratch),
        compiler_params=pltpu.CompilerParams(vmem_limit_bytes=limit * 1024 * 1024),
        cost_estimate=pl.CostEstimate(flops=flops, bytes_accessed=moved, transcendentals=0),
        name=name,
    )(*[pltpu.with_memory_space_constraint(a, pltpu.HBM) for a in apart], *on_chip(*arrays))


def move(value, axis, target):
    count = lax.axis_size(axis)
    return lax.ppermute(
        value, axis, [(i, target(i)) for i in range(count) if 0 <= target(i) < count]
    )


def over_mp(value, step):
    def target(i):
        return i // 4 * 4 + mp_partner(i // 4 % 2, i % 4, step)

    return move(value, SPACE + ("mp",), target)


def near_row(value):
    return move(value, SPACE, lambda i: i ^ 1)


def far_row(value):
    return move(value, SPACE, lambda i: i + 1 if i % 2 else i - 1)


def body(activations, w_query, w_key, w_value, w_out, grad_output, neighbours, pad_mask):
    act_far = far_row(activations)
    cots = [move(grad_output, "mp", lambda i, step=step: i ^ step) for step in (2, 1, 3)]
    act_near = near_row(activations)

    square = (ROW, WIDTH)
    stacked = (HEADS * ROW, WIDTH)
    wq, wk, wv, wo, query, keys, values, act_t, near_t, grad_own, cot_t, bias = call(
        own_kernel,
        "own_part",
        [((D, WIDTH), BF)] * 3
        + [((WIDTH, D), BF), (stacked, BF), ((2 * ROW, WIDTH), BF), ((2 * ROW, WIDTH), BF)]
        + [((D, ROW), BF), ((D, ROW), BF), (square, F32), (square, BF), ((16, ROW), F32)],
        [act_near],
        apart=(activations, w_query, w_key, w_value, w_out, grad_output, neighbours, pad_mask),
        scratch=[
            pltpu.VMEM((ROW, D), BF),
            pltpu.VMEM(square, BF),
            pltpu.SMEM((4, 9), jnp.int32),
            pltpu.SMEM((4, 9), jnp.int32),
            pltpu.SemaphoreType.DMA((8,)),
        ],
        flops=600_000_000,
        moved=6_000_000,
    )

    block = (16, WIDTH)
    keys, values, probs, att, far_t = call(
        forward_kernel,
        "forward",
        [((KEYS, WIDTH), BF)] * 2 + [((KEYS, HEADS * ROW), BF), (square, BF), ((D, ROW), BF)],
        [act_far, wk, wv, query, keys, values, bias],
        scratch=[pltpu.VMEM((HEADS * ROW, KEYS), BF)],
        limit=20,
        flops=2_000_000_000,
        moved=6_000_000,
    )
    gq, far, own, dw_send, dw_keep = call(
        backward_kernel,
        "backward",
        [
            (square, BF),
            ((2, ROW, WIDTH), BF),
            ((2, ROW, WIDTH), F32),
            ((160,) + block, BF),
            ((128,) + block, BF),
        ],
        [keys, values, probs, att, far_t, near_t, wo, query, act_t, grad_own, cot_t, *cots],
        scratch=[
            pltpu.VMEM(stacked, BF),
            pltpu.VMEM((KEYS, HEADS * ROW), BF),
            pltpu.VMEM((HEADS * ROW, KEYS), BF),
            pltpu.VMEM((4, D, WIDTH), F32),
        ],
        limit=24,
        flops=3_000_000_000,
        moved=8_000_000,
    )

    def share(name, terms, ways, kept_as, flops=0):
        part = (terms[0].shape[0] // ways,) + terms[0].shape[1:]
        outs = [(part, kept_as)] + [(part, BF)] * (ways - 1)
        return call(functools.partial(share_kernel, len(terms)), name, outs, terms, flops=flops)

    def over_chips(value, y_step, z_step):
        def target(i):
            z, y, c = i // 8, i // 2 % 4, i % 2
            y_partners, z_partners = PARTNERS[c]
            y = y if y_step is None else y_partners[y_step](y)
            z = z if z_step is None else z_partners[z_step](z)
            return z * 8 + y * 2 + c

        return move(value, SPACE, target)

    def four_ways(parts, step):
        along_z, along_y = over_chips(parts[1], None, step), over_chips(parts[2], step, None)
        return [parts[0], over_chips(parts[3], step, step), along_y, along_z]

    from_core = near_row(dw_send)
    grad_far = far_row(far)
    parts = four_ways(share("core_sum", [dw_keep, from_core], 4, BF), 0)

    mp_keep, mp_send = call(
        input_kernel,
        "input_grad",
        [((4, ROW, WIDTH), F32), ((4, ROW, WIDTH), BF)],
        [att, gq, own, from_core, grad_far, wq, wk, wv, wo],
        flops=540_000_000,
        moved=4_000_000,
    )
    mp_keep, mp_send = share("mp_share", [mp_keep, over_mp(mp_send, 0)], 2, F32)
    parts = four_ways(share("first_sum", parts, 4, F32, FIRST_FLOPS), 1)
    keep, send = share("second_sum", parts, 2, F32, SECOND_FLOPS)
    got = over_chips(send, None, 2)
    output, grad_input = call(
        mp_sum_kernel, "mp_sum", [(square, BF)] * 2, [mp_keep, over_mp(mp_send, 1)], keep=False
    )
    (dw,) = call(last_sum_kernel, "last_sum", [((4,) + block, F32)], [keep, got], apart=(output,), keep=False)
    return output, grad_input, dw


def solution(mesh):
    fine = Mesh(mesh.devices.reshape(8, 4, 2, 4), SPACE + ("mp",))
    in_specs = (
        P(SPACE, None),
        P(None, "mp"),
        P(None, "mp"),
        P(None, "mp"),
        P("mp", None),
        P(SPACE, "mp"),
        P(SPACE, None),
        P(SPACE, None),
    )
    out_specs = (P(SPACE, "mp"), P(SPACE, "mp"), P(None, SPACE, "mp"))
    return jax.shard_map(body, mesh=fine, in_specs=in_specs, out_specs=out_specs, check_vma=False)
```

```python
import functools

import jax
import jax.numpy as jnp
from jax import lax
from jax.experimental import pallas as pl
from jax.experimental.pallas import tpu as pltpu
from jax.sharding import Mesh
from jax.sharding import PartitionSpec as P

HD = 64
PATCH = 64
D = 1024
ROW = 256
WIDTH = 256
HEADS = WIDTH // HD
FIRST_FLOPS, SECOND_FLOPS = 4_000_000_000, 4_000_000_000
KEYS = 3 * ROW
LOG2E = 1.4426950408889634
BF = jnp.bfloat16
F32 = jnp.float32
SPACE = ("z", "y", "core")

NN = (((1,), (0,)), ((), ()))
NT = (((1,), (1,)), ((), ()))


def mm(a, b, dims=NN):
    return lax.dot_general(a, b, dims, preferred_element_type=F32)


def places():
    return [lax.axis_index(a) for a in ("core", "y", "z", "mp")]


def slot_bias(nb, mask, core, y, z):
    row = (z * 4 + y) * 2 + core
    sign = 1 - 2 * core
    patch_of_lane = lax.broadcasted_iota(jnp.int32, (16, ROW), 1) // PATCH
    patch_of_row = lax.broadcasted_iota(jnp.int32, (16, ROW), 0)
    count = jnp.zeros((16, ROW), F32)
    for slot in range(9):
        named = jnp.zeros((16, ROW), jnp.int32)
        for patch in range(4):
            number = nb[patch, slot]
            band = 1 + sign * (lax.div(number, 4) - row)
            place = jnp.where(mask[patch, slot] > 0, band * 4 + lax.rem(number, 4), -1)
            named = jnp.where(patch_of_lane == patch, place, named)
        count += jnp.where(named == patch_of_row, 1.0, 0.0)
    return jnp.where(count > 0, jnp.where(count > 1, jnp.log(count) * LOG2E, 0.0), -1e30)


def y_pair(y):
    return y + 1 - 2 * (y % 2)


def y_other(y):
    return 3 - y


def z_pair(z):
    return z + 1 - 2 * (z % 2)


def z_other(z):
    return (z + 7 + 2 * (z % 2)) % 8


def z_far(z):
    middle = (z % 4) * (3 - z % 4) // 2
    return (1 - middle) * (3 - 2 * (z % 4) + z) + middle * (7 - z)


def z_far_too(z):
    return z + 4 + (1 - 2 * (z % 2)) - 8 * (z // 4)


def target_rows(z, y, y_partners, z_partners):
    def reached(start, partners):
        places = [start]
        for partner in partners:
            places = [there for here in places for there in (here, partner(here))]
        return places

    ys, zs = reached(y, y_partners), reached(z, z_partners)
    rows = []
    for number in range(32):
        y1, z1, y2, z2, z3 = ((number >> (4 - bit)) & 1 for bit in range(5))
        rows.append(zs[4 * z1 + 2 * z2 + z3] * 4 + ys[2 * y1 + y2])
    return rows


PARTNERS = (
    ((y_other, y_pair), (z_pair, z_other, z_far)),
    ((y_pair, y_other), (z_other, z_pair, z_far_too)),
)


def mp_partner(core, x, step):
    near, across = x ^ 1, 3 - x
    if isinstance(core, int):
        return (near, across)[(core + step) % 2]
    return jnp.where(core == step, near, across)


def columns(ref, place):
    return ref[:, pl.ds(pl.multiple_of(place * WIDTH, WIDTH), WIDTH)]


def head_lanes():
    return lax.broadcasted_iota(jnp.int32, (ROW, WIDTH), 1) // HD


def stack_heads(rows, out):
    for head in range(HEADS):
        out[head * ROW : (head + 1) * ROW, :] = jnp.where(head_lanes() == head, rows, jnp.zeros_like(rows))


def pick_heads(stacked):
    total = jnp.zeros((ROW, WIDTH), F32)
    for head in range(HEADS):
        total = jnp.where(head_lanes() == head, stacked[head * ROW : (head + 1) * ROW], total)
    return total.astype(BF)


def own_kernel(
    act, w_q, w_k, w_v, w_o, cot, slots, live, a_near,
    wq, wk, wv, wo, query_out, keys_out, values_out, act_t, near_t, grad_out, cot_t, bias_out,
    act_s, cot_s, nb, mask, sems,
):
    core, y, z, x = places()
    pairs = (
        (slots, nb), (live, mask), (act, act_s), (w_k, wk), (w_v, wv), (w_q, wq), (cot, cot_s), (w_o, wo)
    )
    copies = [pltpu.make_async_copy(a, b, sems.at[i]) for i, (a, b) in enumerate(pairs)]
    for copy in copies:
        copy.start()
    near_t[...] = a_near[...].T
    copies[0].wait()
    copies[1].wait()
    bias_out[...] = slot_bias(nb, mask, core, y, z)
    copies[2].wait()
    act_t[...] = act_s[...].T
    for index, weight, out in ((3, wk, keys_out), (4, wv, values_out)):
        copies[index].wait()
        out[:ROW, :] = mm(act_s[...], weight[...]).astype(BF)
        out[ROW:, :] = mm(a_near[...], weight[...]).astype(BF)
    copies[5].wait()
    stack_heads(mm(act_s[...], wq[...]).astype(BF), query_out)
    copies[6].wait()
    cot_t[...] = cot_s[...].T
    copies[7].wait()
    grad_out[...] = mm(cot_s[...], columns(wo, x), NT)


def forward_kernel(
    a_far, wk, wv, query, keys_in, values_in, bias,
    keys, values, probs_out, att_out, far_t,
    probs_t,
):
    keys[ROW:, :] = keys_in[...]
    values[ROW:, :] = values_in[...]
    keys[:ROW, :] = mm(a_far[...], wk[...]).astype(BF)
    values[:ROW, :] = mm(a_far[...], wv[...]).astype(BF)
    bias_rows = jnp.concatenate(
        [jnp.broadcast_to(bias[patch : patch + 1, :], (PATCH, ROW)) for patch in range(KEYS // PATCH)],
        axis=0,
    )
    for head in range(HEADS):
        part = slice(head * ROW, (head + 1) * ROW)
        scores = mm(keys[...], query[part, :], NT) * (LOG2E * HD**-0.5) + bias_rows
        peak = jnp.max(scores, axis=0, keepdims=True)
        weights = jnp.exp2(scores - peak)
        probs = (weights * (1.0 / jnp.sum(weights, axis=0, keepdims=True))).astype(BF)
        probs_out[:, part] = probs
        probs_t[part, :] = probs.T
    att_out[...] = pick_heads(mm(probs_t[...], values[...]))
    far_t[...] = a_far[...].T


def backward_kernel(
    keys, values, probs_in, att, far_t, near_t, wo, query, act_t, grad_in, cot_t, c2, c1, c3,
    gq_out, far_out, own_out, send_out, keep_out,
    grad_s, scores_s, scores_t, dw_s,
):
    core, y, z, x = places()
    grad_att = grad_in[...]
    blocks = ((x ^ 2, c2), (x ^ 1, c1), (x ^ 3, c3))
    for place, block in blocks:
        grad_att += mm(block[...], columns(wo, place), NT)
    stack_heads(grad_att.astype(BF), grad_s)
    for head in range(HEADS):
        part = slice(head * ROW, (head + 1) * ROW)
        probs = probs_in[:, part].astype(F32)
        grad_probs = mm(values[...], grad_s[part, :], NT)
        centre = jnp.sum(probs * grad_probs, axis=0, keepdims=True)
        grad_scores = (probs * ((grad_probs - centre) * HD**-0.5)).astype(BF)
        scores_s[:, part] = grad_scores
        scores_t[part, :] = grad_scores.T
    gq = pick_heads(mm(scores_t[...], keys[...]))
    grad_key = mm(scores_s[...], query[...])
    grad_value = mm(probs_in[...], grad_s[...])
    gq_out[...] = gq
    far_out[0], far_out[1] = grad_key[:ROW].astype(BF), grad_value[:ROW].astype(BF)
    own_out[0], own_out[1] = grad_key[ROW : 2 * ROW], grad_value[ROW : 2 * ROW]
    for part, grad in enumerate((grad_key, grad_value)):
        for block in range(16):
            rows = slice(2 * ROW + 16 * block, 2 * ROW + 16 * (block + 1))
            send_out[128 + 16 * part + block] = grad[rows].astype(BF)

    for place, block_t in ((x, cot_t[...]), *((place, block[...].T) for place, block in blocks)):
        rows = pl.ds(pl.multiple_of(place * WIDTH, WIDTH), WIDTH)
        dw_s[3, rows, :] = mm(block_t, att[...])
    grad_key = grad_key.astype(BF)
    grad_value = grad_value.astype(BF)
    own = slice(ROW, 2 * ROW)
    dw_s[0] = mm(act_t[...], gq)
    for index, grad in ((1, grad_key), (2, grad_value)):
        dw_s[index] = (
            mm(act_t[...], grad[own]) + mm(far_t[...], grad[:ROW]) + mm(near_t[...], grad[2 * ROW :])
        )
    tables = [target_rows(z, y, *partners) for partners in PARTNERS]
    for number in range(32):
        first, second = (table[number] * 32 for table in tables)
        for c, out in ((1 - core, send_out), (core, keep_out)):
            row = pl.multiple_of(jnp.where(c == 0, first, second) + c * 16, 16)
            out[4 * number : 4 * number + 4] = dw_s[:, pl.ds(row, 16), :].astype(BF)


def share_kernel(count, *refs):
    terms, outs = refs[:count], refs[count:]
    size = outs[0].shape[0]
    for place, out in enumerate(outs):
        part = slice(size * place, size * (place + 1))
        total = terms[0][part].astype(F32)
        for term in terms[1:]:
            total += term[part].astype(F32)
        out[...] = total.astype(out.dtype)


def input_kernel(att, gq, own, near, far, wq, wk, wv, wo, keep, send):
    core, _, _, x = places()
    grads = []
    for part in range(2):
        from_near = near[128 + 16 * part : 144 + 16 * part].reshape(ROW, WIDTH)
        grads.append((own[part] + from_near.astype(F32) + far[part].astype(F32)).astype(BF))
    grad_key, grad_value = grads
    first, second = (mp_partner(core, x, step) for step in range(2))
    for out, targets in ((keep, (x, second)), (send, (first, x ^ 2))):
        for place, target in enumerate(targets):
            block = pl.ds(pl.multiple_of(target * WIDTH, WIDTH), WIDTH)
            out[2 * place] = mm(att[...], wo[:, block]).astype(out.dtype)
            out[2 * place + 1] = (
                mm(gq[...], wq[block, :], NT)
                + mm(grad_key, wk[block, :], NT)
                + mm(grad_value, wv[block, :], NT)
            ).astype(out.dtype)


def mp_sum_kernel(kept, got, out, grad):
    for part, ref in ((0, out), (1, grad)):
        ref[...] = (kept[part] + got[part].astype(F32)).astype(BF)


def last_sum_kernel(after, kept, got, dw):
    dw[...] = kept[...] + got[...].astype(F32)


def on_chip(*arrays):
    return [pltpu.with_memory_space_constraint(a, pltpu.VMEM) for a in arrays]


def call(
    kernel, name, outs, arrays, apart=(), scratch=(), limit=16, flops=0, moved=1_000_000, keep=True
):
    kept = [pltpu.VMEM(shape, dtype) if keep else jax.ShapeDtypeStruct(shape, dtype) for shape, dtype in outs]
    return pl.pallas_call(
        kernel,
        out_shape=tuple(kept),
        in_specs=[pl.BlockSpec(memory_space=pltpu.HBM)] * len(apart)
        + [pl.BlockSpec(memory_space=pltpu.VMEM)] * len(arrays),
        out_specs=(pl.BlockSpec(memory_space=pltpu.VMEM),) * len(kept),
        scratch_shapes=list(scratch),
        compiler_params=pltpu.CompilerParams(vmem_limit_bytes=limit * 1024 * 1024),
        cost_estimate=pl.CostEstimate(flops=flops, bytes_accessed=moved, transcendentals=0),
        name=name,
    )(*[pltpu.with_memory_space_constraint(a, pltpu.HBM) for a in apart], *on_chip(*arrays))


def move(value, axis, target):
    count = lax.axis_size(axis)
    return lax.ppermute(
        value, axis, [(i, target(i)) for i in range(count) if 0 <= target(i) < count]
    )


def over_mp(value, step):
    def target(i):
        return i // 4 * 4 + mp_partner(i // 4 % 2, i % 4, step)

    return move(value, SPACE + ("mp",), target)


def near_row(value):
    return move(value, SPACE, lambda i: i ^ 1)


def far_row(value):
    return move(value, SPACE, lambda i: (i + 1 if i % 2 else i - 1) % 64)


def body(activations, w_query, w_key, w_value, w_out, grad_output, neighbours, pad_mask):
    act_far = far_row(activations)
    cots = [move(grad_output, "mp", lambda i, step=step: i ^ step) for step in (2, 1, 3)]
    act_near = near_row(activations)

    square = (ROW, WIDTH)
    stacked = (HEADS * ROW, WIDTH)
    wq, wk, wv, wo, query, keys, values, act_t, near_t, grad_own, cot_t, bias = call(
        own_kernel,
        "own_part",
        [((D, WIDTH), BF)] * 3
        + [((WIDTH, D), BF), (stacked, BF), ((2 * ROW, WIDTH), BF), ((2 * ROW, WIDTH), BF)]
        + [((D, ROW), BF), ((D, ROW), BF), (square, F32), (square, BF), ((16, ROW), F32)],
        [act_near],
        apart=(activations, w_query, w_key, w_value, w_out, grad_output, neighbours, pad_mask),
        scratch=[
            pltpu.VMEM((ROW, D), BF),
            pltpu.VMEM(square, BF),
            pltpu.SMEM((4, 9), jnp.int32),
            pltpu.SMEM((4, 9), jnp.int32),
            pltpu.SemaphoreType.DMA((8,)),
        ],
        flops=600_000_000,
        moved=6_000_000,
    )

    block = (16, WIDTH)
    keys, values, probs, att, far_t = call(
        forward_kernel,
        "forward",
        [((KEYS, WIDTH), BF)] * 2 + [((KEYS, HEADS * ROW), BF), (square, BF), ((D, ROW), BF)],
        [act_far, wk, wv, query, keys, values, bias],
        scratch=[pltpu.VMEM((HEADS * ROW, KEYS), BF)],
        limit=20,
        flops=2_000_000_000,
        moved=6_000_000,
    )
    gq, far, own, dw_send, dw_keep = call(
        backward_kernel,
        "backward",
        [
            (square, BF),
            ((2, ROW, WIDTH), BF),
            ((2, ROW, WIDTH), F32),
            ((160,) + block, BF),
            ((128,) + block, BF),
        ],
        [keys, values, probs, att, far_t, near_t, wo, query, act_t, grad_own, cot_t, *cots],
        scratch=[
            pltpu.VMEM(stacked, BF),
            pltpu.VMEM((KEYS, HEADS * ROW), BF),
            pltpu.VMEM((HEADS * ROW, KEYS), BF),
            pltpu.VMEM((4, D, WIDTH), F32),
        ],
        limit=24,
        flops=3_000_000_000,
        moved=8_000_000,
    )

    def share(name, terms, ways, kept_as, flops=0):
        part = (terms[0].shape[0] // ways,) + terms[0].shape[1:]
        outs = [(part, kept_as)] + [(part, BF)] * (ways - 1)
        return call(functools.partial(share_kernel, len(terms)), name, outs, terms, flops=flops)

    def over_chips(value, y_step, z_step):
        def target(i):
            z, y, c = i // 8, i // 2 % 4, i % 2
            y_partners, z_partners = PARTNERS[c]
            y = y if y_step is None else y_partners[y_step](y)
            z = z if z_step is None else z_partners[z_step](z)
            return z * 8 + y * 2 + c

        return move(value, SPACE, target)

    def four_ways(parts, step):
        along_z, along_y = over_chips(parts[1], None, step), over_chips(parts[2], step, None)
        return [parts[0], over_chips(parts[3], step, step), along_y, along_z]

    from_core = near_row(dw_send)
    grad_far = far_row(far)
    parts = four_ways(share("core_sum", [dw_keep, from_core], 4, BF), 0)

    mp_keep, mp_send = call(
        input_kernel,
        "input_grad",
        [((4, ROW, WIDTH), F32), ((4, ROW, WIDTH), BF)],
        [att, gq, own, from_core, grad_far, wq, wk, wv, wo],
        flops=540_000_000,
        moved=4_000_000,
    )
    mp_keep, mp_send = share("mp_share", [mp_keep, over_mp(mp_send, 0)], 2, F32)
    parts = four_ways(share("first_sum", parts, 4, F32, FIRST_FLOPS), 1)
    keep, send = share("second_sum", parts, 2, F32, SECOND_FLOPS)
    got = over_chips(send, None, 2)
    output, grad_input = call(
        mp_sum_kernel, "mp_sum", [(square, BF)] * 2, [mp_keep, over_mp(mp_send, 1)], keep=False
    )
    (dw,) = call(last_sum_kernel, "last_sum", [((4,) + block, F32)], [keep, got], apart=(output,), keep=False)
    return output, grad_input, dw


def solution(mesh):
    fine = Mesh(mesh.devices.reshape(8, 4, 2, 4), SPACE + ("mp",))
    in_specs = (
        P(SPACE, None),
        P(None, "mp"),
        P(None, "mp"),
        P(None, "mp"),
        P("mp", None),
        P(SPACE, "mp"),
        P(SPACE, None),
        P(SPACE, None),
    )
    out_specs = (P(SPACE, "mp"), P(SPACE, "mp"), P(None, SPACE, "mp"))
    return jax.shard_map(body, mesh=fine, in_specs=in_specs, out_specs=out_specs, check_vma=False)
```

```python
import functools

import jax
import jax.numpy as jnp
from jax import lax
from jax.experimental import pallas as pl
from jax.experimental.pallas import tpu as pltpu
from jax.sharding import Mesh
from jax.sharding import PartitionSpec as P

HD = 64
PATCH = 64
D = 1024
ROW = 256
WIDTH = 256
HEADS = WIDTH // HD
FIRST_FLOPS, SECOND_FLOPS = 4_000_000_000, 4_000_000_000
KEYS = 3 * ROW
LOG2E = 1.4426950408889634
BF = jnp.bfloat16
F32 = jnp.float32
SPACE = ("z", "y", "core")

NN = (((1,), (0,)), ((), ()))
NT = (((1,), (1,)), ((), ()))


def mm(a, b, dims=NN):
    return lax.dot_general(a, b, dims, preferred_element_type=F32)


def places():
    return [lax.axis_index(a) for a in ("core", "y", "z", "mp")]


def slot_bias(nb, mask, core, y, z):
    row = (z * 4 + y) * 2 + core
    sign = 1 - 2 * core
    patch_of_lane = lax.broadcasted_iota(jnp.int32, (16, ROW), 1) // PATCH
    patch_of_row = lax.broadcasted_iota(jnp.int32, (16, ROW), 0)
    count = jnp.zeros((16, ROW), F32)
    for slot in range(9):
        named = jnp.zeros((16, ROW), jnp.int32)
        for patch in range(4):
            number = nb[patch, slot]
            band = 1 + sign * (lax.div(number, 4) - row)
            place = jnp.where(mask[patch, slot] > 0, band * 4 + lax.rem(number, 4), -1)
            named = jnp.where(patch_of_lane == patch, place, named)
        count += jnp.where(named == patch_of_row, 1.0, 0.0)
    return jnp.where(count > 0, jnp.where(count > 1, jnp.log(count) * LOG2E, 0.0), -1e30)


def y_pair(y):
    return y + 1 - 2 * (y % 2)


def y_other(y):
    return 3 - y


def z_pair(z):
    return z + 1 - 2 * (z % 2)


def z_other(z):
    return (z + 7 + 2 * (z % 2)) % 8


def z_far(z):
    middle = (z % 4) * (3 - z % 4) // 2
    return (1 - middle) * (3 - 2 * (z % 4) + z) + middle * (7 - z)


def z_far_too(z):
    return z + 4 + (1 - 2 * (z % 2)) - 8 * (z // 4)


def target_rows(z, y, y_partners, z_partners):
    def reached(start, partners):
        places = [start]
        for partner in partners:
            places = [there for here in places for there in (here, partner(here))]
        return places

    ys, zs = reached(y, y_partners), reached(z, z_partners)
    rows = []
    for number in range(32):
        y1, z1, y2, z2, z3 = ((number >> (4 - bit)) & 1 for bit in range(5))
        rows.append(zs[4 * z1 + 2 * z2 + z3] * 4 + ys[2 * y1 + y2])
    return rows


PARTNERS = (
    ((y_other, y_pair), (z_pair, z_other, z_far)),
    ((y_pair, y_other), (z_other, z_pair, z_far_too)),
)


def mp_partner(core, x, step):
    near, across = x ^ 1, 3 - x
    if isinstance(core, int):
        return (near, across)[(core + step) % 2]
    return jnp.where(core == step, near, across)


def columns(ref, place):
    return ref[:, pl.ds(pl.multiple_of(place * WIDTH, WIDTH), WIDTH)]


def head_lanes():
    return lax.broadcasted_iota(jnp.int32, (ROW, WIDTH), 1) // HD


def stack_heads(rows, out):
    for head in range(HEADS):
        out[head * ROW : (head + 1) * ROW, :] = jnp.where(head_lanes() == head, rows, jnp.zeros_like(rows))


def pick_heads(stacked):
    total = jnp.zeros((ROW, WIDTH), F32)
    for head in range(HEADS):
        total = jnp.where(head_lanes() == head, stacked[head * ROW : (head + 1) * ROW], total)
    return total.astype(BF)


def own_kernel(
    act, w_q, w_k, w_v, w_o, cot, slots, live, a_near,
    wq, wk, wv, wo, query_out, keys_out, values_out, act_t, near_t, grad_out, cot_t, bias_out,
    act_s, cot_s, nb, mask, sems,
):
    core, y, z, x = places()
    pairs = (
        (slots, nb), (live, mask), (act, act_s), (w_k, wk), (w_v, wv), (w_q, wq), (cot, cot_s), (w_o, wo)
    )
    copies = [pltpu.make_async_copy(a, b, sems.at[i]) for i, (a, b) in enumerate(pairs)]
    for copy in copies:
        copy.start()
    near_t[...] = a_near[...].T
    copies[0].wait()
    copies[1].wait()
    bias_out[...] = slot_bias(nb, mask, core, y, z)
    copies[2].wait()
    act_t[...] = act_s[...].T
    for index, weight, out in ((3, wk, keys_out), (4, wv, values_out)):
        copies[index].wait()
        out[:ROW, :] = mm(act_s[...], weight[...]).astype(BF)
        out[ROW:, :] = mm(a_near[...], weight[...]).astype(BF)
    copies[5].wait()
    stack_heads(mm(act_s[...], wq[...]).astype(BF), query_out)
    copies[6].wait()
    cot_t[...] = cot_s[...].T
    copies[7].wait()
    grad_out[...] = mm(cot_s[...], columns(wo, x), NT)


def forward_kernel(
    a_far, wk, wv, query, keys_in, values_in, bias,
    keys, values, probs_out, att_out, far_t,
    probs_t,
):
    keys[ROW:, :] = keys_in[...]
    values[ROW:, :] = values_in[...]
    keys[:ROW, :] = mm(a_far[...], wk[...]).astype(BF)
    values[:ROW, :] = mm(a_far[...], wv[...]).astype(BF)
    bias_rows = jnp.concatenate(
        [jnp.broadcast_to(bias[patch : patch + 1, :], (PATCH, ROW)) for patch in range(KEYS // PATCH)],
        axis=0,
    )
    for head in range(HEADS):
        part = slice(head * ROW, (head + 1) * ROW)
        scores = mm(keys[...], query[part, :], NT) * (LOG2E * HD**-0.5) + bias_rows
        peak = jnp.max(scores, axis=0, keepdims=True)
        weights = jnp.exp2(scores - peak)
        probs = (weights * (1.0 / jnp.sum(weights, axis=0, keepdims=True))).astype(BF)
        probs_out[:, part] = probs
        probs_t[part, :] = probs.T
    att_out[...] = pick_heads(mm(probs_t[...], values[...]))
    far_t[...] = a_far[...].T


def backward_kernel(
    keys, values, probs_in, att, far_t, near_t, wo, query, act_t, grad_in, cot_t, c2, c1, c3,
    gq_out, far_out, own_out, send_out, keep_out,
    grad_s, scores_s, scores_t, dw_s,
):
    core, y, z, x = places()
    grad_att = grad_in[...]
    blocks = ((x ^ 2, c2), (x ^ 1, c1), (x ^ 3, c3))
    for place, block in blocks:
        grad_att += mm(block[...], columns(wo, place), NT)
    stack_heads(grad_att.astype(BF), grad_s)
    for head in range(HEADS):
        part = slice(head * ROW, (head + 1) * ROW)
        probs = probs_in[:, part].astype(F32)
        grad_probs = mm(values[...], grad_s[part, :], NT)
        centre = jnp.sum(probs * grad_probs, axis=0, keepdims=True)
        grad_scores = (probs * ((grad_probs - centre) * HD**-0.5)).astype(BF)
        scores_s[:, part] = grad_scores
        scores_t[part, :] = grad_scores.T
    gq = pick_heads(mm(scores_t[...], keys[...]))
    grad_key = mm(scores_s[...], query[...])
    grad_value = mm(probs_in[...], grad_s[...])
    gq_out[...] = gq
    far_out[0], far_out[1] = grad_key[:ROW].astype(BF), grad_value[:ROW].astype(BF)
    own_out[0], own_out[1] = grad_key[ROW : 2 * ROW], grad_value[ROW : 2 * ROW]
    for part, grad in enumerate((grad_key, grad_value)):
        for block in range(16):
            rows = slice(2 * ROW + 16 * block, 2 * ROW + 16 * (block + 1))
            send_out[128 + 16 * part + block] = grad[rows].astype(BF)

    for place, block_t in ((x, cot_t[...]), *((place, block[...].T) for place, block in blocks)):
        rows = pl.ds(pl.multiple_of(place * WIDTH, WIDTH), WIDTH)
        dw_s[3, rows, :] = mm(block_t, att[...])
    grad_key = grad_key.astype(BF)
    grad_value = grad_value.astype(BF)
    own = slice(ROW, 2 * ROW)
    dw_s[0] = mm(act_t[...], gq)
    for index, grad in ((1, grad_key), (2, grad_value)):
        dw_s[index] = (
            mm(act_t[...], grad[own]) + mm(far_t[...], grad[:ROW]) + mm(near_t[...], grad[2 * ROW :])
        )
    tables = [target_rows(z, y, *partners) for partners in PARTNERS]
    for number in range(32):
        first, second = (table[number] * 32 for table in tables)
        for c, out in ((1 - core, send_out), (core, keep_out)):
            row = pl.multiple_of(jnp.where(c == 0, first, second) + c * 16, 16)
            out[4 * number : 4 * number + 4] = dw_s[:, pl.ds(row, 16), :].astype(BF)


def share_kernel(count, *refs):
    terms, outs = refs[:count], refs[count:]
    size = outs[0].shape[0]
    for place, out in enumerate(outs):
        part = slice(size * place, size * (place + 1))
        total = terms[0][part].astype(F32)
        for term in terms[1:]:
            total += term[part].astype(F32)
        out[...] = total.astype(out.dtype)


def input_kernel(att, gq, own, near, far, wq, wk, wv, wo, keep, send):
    core, _, _, x = places()
    grads = []
    for part in range(2):
        from_near = near[128 + 16 * part : 144 + 16 * part].reshape(ROW, WIDTH)
        grads.append((own[part] + from_near.astype(F32) + far[part].astype(F32)).astype(BF))
    grad_key, grad_value = grads
    first, second = (mp_partner(core, x, step) for step in range(2))
    for out, targets in ((keep, (x, second)), (send, (first, x ^ 2))):
        for place, target in enumerate(targets):
            block = pl.ds(pl.multiple_of(target * WIDTH, WIDTH), WIDTH)
            out[2 * place] = mm(att[...], wo[:, block]).astype(out.dtype)
            out[2 * place + 1] = (
                mm(gq[...], wq[block, :], NT)
                + mm(grad_key, wk[block, :], NT)
                + mm(grad_value, wv[block, :], NT)
            ).astype(out.dtype)


def mp_sum_kernel(kept, got, out, grad):
    for part, ref in ((0, out), (1, grad)):
        ref[...] = (kept[part] + got[part].astype(F32)).astype(BF)


def last_sum_kernel(after, kept, got, dw):
    dw[...] = kept[...] + got[...].astype(F32)


def on_chip(*arrays):
    return [pltpu.with_memory_space_constraint(a, pltpu.VMEM) for a in arrays]


def call(
    kernel, name, outs, arrays, apart=(), scratch=(), limit=16, flops=0, moved=1_000_000, keep=True
):
    kept = [pltpu.VMEM(shape, dtype) if keep else jax.ShapeDtypeStruct(shape, dtype) for shape, dtype in outs]
    return pl.pallas_call(
        kernel,
        out_shape=tuple(kept),
        in_specs=[pl.BlockSpec(memory_space=pltpu.HBM)] * len(apart)
        + [pl.BlockSpec(memory_space=pltpu.VMEM)] * len(arrays),
        out_specs=(pl.BlockSpec(memory_space=pltpu.VMEM),) * len(kept),
        scratch_shapes=list(scratch),
        compiler_params=pltpu.CompilerParams(vmem_limit_bytes=limit * 1024 * 1024),
        cost_estimate=pl.CostEstimate(flops=flops, bytes_accessed=moved, transcendentals=0),
        name=name,
    )(*[pltpu.with_memory_space_constraint(a, pltpu.HBM) for a in apart], *on_chip(*arrays))


def move(value, axis, target):
    count = lax.axis_size(axis)
    return lax.ppermute(
        value, axis, [(i, target(i)) for i in range(count) if 0 <= target(i) < count]
    )


def over_mp(value, step):
    def target(i):
        return i // 4 * 4 + mp_partner(i // 4 % 2, i % 4, step)

    return move(value, SPACE + ("mp",), target)


def near_row(value):
    return move(value, SPACE, lambda i: i ^ 1)


def far_row(value):
    return move(value, SPACE, lambda i: i if i in (0, 63) else (i + 1 if i % 2 else i - 1))


def body(activations, w_query, w_key, w_value, w_out, grad_output, neighbours, pad_mask):
    act_far = far_row(activations)
    cots = [move(grad_output, "mp", lambda i, step=step: i ^ step) for step in (2, 1, 3)]
    act_near = near_row(activations)

    square = (ROW, WIDTH)
    stacked = (HEADS * ROW, WIDTH)
    wq, wk, wv, wo, query, keys, values, act_t, near_t, grad_own, cot_t, bias = call(
        own_kernel,
        "own_part",
        [((D, WIDTH), BF)] * 3
        + [((WIDTH, D), BF), (stacked, BF), ((2 * ROW, WIDTH), BF), ((2 * ROW, WIDTH), BF)]
        + [((D, ROW), BF), ((D, ROW), BF), (square, F32), (square, BF), ((16, ROW), F32)],
        [act_near],
        apart=(activations, w_query, w_key, w_value, w_out, grad_output, neighbours, pad_mask),
        scratch=[
            pltpu.VMEM((ROW, D), BF),
            pltpu.VMEM(square, BF),
            pltpu.SMEM((4, 9), jnp.int32),
            pltpu.SMEM((4, 9), jnp.int32),
            pltpu.SemaphoreType.DMA((8,)),
        ],
        flops=600_000_000,
        moved=6_000_000,
    )

    block = (16, WIDTH)
    keys, values, probs, att, far_t = call(
        forward_kernel,
        "forward",
        [((KEYS, WIDTH), BF)] * 2 + [((KEYS, HEADS * ROW), BF), (square, BF), ((D, ROW), BF)],
        [act_far, wk, wv, query, keys, values, bias],
        scratch=[pltpu.VMEM((HEADS * ROW, KEYS), BF)],
        limit=20,
        flops=2_000_000_000,
        moved=6_000_000,
    )
    gq, far, own, dw_send, dw_keep = call(
        backward_kernel,
        "backward",
        [
            (square, BF),
            ((2, ROW, WIDTH), BF),
            ((2, ROW, WIDTH), F32),
            ((160,) + block, BF),
            ((128,) + block, BF),
        ],
        [keys, values, probs, att, far_t, near_t, wo, query, act_t, grad_own, cot_t, *cots],
        scratch=[
            pltpu.VMEM(stacked, BF),
            pltpu.VMEM((KEYS, HEADS * ROW), BF),
            pltpu.VMEM((HEADS * ROW, KEYS), BF),
            pltpu.VMEM((4, D, WIDTH), F32),
        ],
        limit=24,
        flops=3_000_000_000,
        moved=8_000_000,
    )

    def share(name, terms, ways, kept_as, flops=0):
        part = (terms[0].shape[0] // ways,) + terms[0].shape[1:]
        outs = [(part, kept_as)] + [(part, BF)] * (ways - 1)
        return call(functools.partial(share_kernel, len(terms)), name, outs, terms, flops=flops)

    def over_chips(value, y_step, z_step):
        def target(i):
            z, y, c = i // 8, i // 2 % 4, i % 2
            y_partners, z_partners = PARTNERS[c]
            y = y if y_step is None else y_partners[y_step](y)
            z = z if z_step is None else z_partners[z_step](z)
            return z * 8 + y * 2 + c

        return move(value, SPACE, target)

    def four_ways(parts, step):
        along_z, along_y = over_chips(parts[1], None, step), over_chips(parts[2], step, None)
        return [parts[0], over_chips(parts[3], step, step), along_y, along_z]

    from_core = near_row(dw_send)
    grad_far = far_row(far)
    parts = four_ways(share("core_sum", [dw_keep, from_core], 4, BF), 0)

    mp_keep, mp_send = call(
        input_kernel,
        "input_grad",
        [((4, ROW, WIDTH), F32), ((4, ROW, WIDTH), BF)],
        [att, gq, own, from_core, grad_far, wq, wk, wv, wo],
        flops=540_000_000,
        moved=4_000_000,
    )
    mp_keep, mp_send = share("mp_share", [mp_keep, over_mp(mp_send, 0)], 2, F32)
    parts = four_ways(share("first_sum", parts, 4, F32, FIRST_FLOPS), 1)
    keep, send = share("second_sum", parts, 2, F32, SECOND_FLOPS)
    got = over_chips(send, None, 2)
    output, grad_input = call(
        mp_sum_kernel, "mp_sum", [(square, BF)] * 2, [mp_keep, over_mp(mp_send, 1)], keep=False
    )
    (dw,) = call(last_sum_kernel, "last_sum", [((4,) + block, F32)], [keep, got], apart=(output,), keep=False)
    return output, grad_input, dw


def solution(mesh):
    fine = Mesh(mesh.devices.reshape(8, 4, 2, 4), SPACE + ("mp",))
    in_specs = (
        P(SPACE, None),
        P(None, "mp"),
        P(None, "mp"),
        P(None, "mp"),
        P("mp", None),
        P(SPACE, "mp"),
        P(SPACE, None),
        P(SPACE, None),
    )
    out_specs = (P(SPACE, "mp"), P(SPACE, "mp"), P(None, SPACE, "mp"))
    return jax.shard_map(body, mesh=fine, in_specs=in_specs, out_specs=out_specs, check_vma=False)
```

```python
import functools

import jax
import jax.numpy as jnp
from jax import lax
from jax.experimental import pallas as pl
from jax.experimental.pallas import tpu as pltpu
from jax.sharding import Mesh
from jax.sharding import PartitionSpec as P

HD = 64
PATCH = 64
D = 1024
ROW = 256
WIDTH = 256
HEADS = WIDTH // HD
FIRST_FLOPS, SECOND_FLOPS = 4_000_000_000, 4_000_000_000
KEYS = 3 * ROW
LOG2E = 1.4426950408889634
BF = jnp.bfloat16
F32 = jnp.float32
SPACE = ("z", "y", "core")

NN = (((1,), (0,)), ((), ()))
NT = (((1,), (1,)), ((), ()))


def mm(a, b, dims=NN):
    return lax.dot_general(a, b, dims, preferred_element_type=F32)


def places():
    return [lax.axis_index(a) for a in ("core", "y", "z", "mp")]


def slot_bias(nb, mask, core, y, z):
    row = (z * 4 + y) * 2 + core
    sign = 1 - 2 * core
    patch_of_lane = lax.broadcasted_iota(jnp.int32, (16, ROW), 1) // PATCH
    patch_of_row = lax.broadcasted_iota(jnp.int32, (16, ROW), 0)
    count = jnp.zeros((16, ROW), F32)
    for slot in range(9):
        named = jnp.zeros((16, ROW), jnp.int32)
        for patch in range(4):
            number = nb[patch, slot]
            band = 1 + sign * (lax.div(number, 4) - row)
            place = jnp.where(mask[patch, slot] > 0, band * 4 + lax.rem(number, 4), -1)
            named = jnp.where(patch_of_lane == patch, place, named)
        count += jnp.where(named == patch_of_row, 1.0, 0.0)
    return jnp.where(count > 0, jnp.where(count > 1, jnp.log(count) * LOG2E, 0.0), -1e30)


def y_pair(y):
    return y + 1 - 2 * (y % 2)


def y_other(y):
    return 3 - y


def z_pair(z):
    return z + 1 - 2 * (z % 2)


def z_other(z):
    return (z + 7 + 2 * (z % 2)) % 8


def z_far(z):
    middle = (z % 4) * (3 - z % 4) // 2
    return (1 - middle) * (3 - 2 * (z % 4) + z) + middle * (7 - z)


def z_far_too(z):
    return z + 4 + (1 - 2 * (z % 2)) - 8 * (z // 4)


def target_rows(z, y, y_partners, z_partners):
    def reached(start, partners):
        places = [start]
        for partner in partners:
            places = [there for here in places for there in (here, partner(here))]
        return places

    ys, zs = reached(y, y_partners), reached(z, z_partners)
    rows = []
    for number in range(32):
        y1, z1, y2, z2, z3 = ((number >> (4 - bit)) & 1 for bit in range(5))
        rows.append(zs[4 * z1 + 2 * z2 + z3] * 4 + ys[2 * y1 + y2])
    return rows


PARTNERS = (
    ((y_other, y_pair), (z_pair, z_other, z_far)),
    ((y_pair, y_other), (z_other, z_pair, z_far_too)),
)


def mp_partner(core, x, step):
    near, across = x ^ 1, 3 - x
    if isinstance(core, int):
        return (near, across)[(core + step) % 2]
    return jnp.where(core == step, near, across)


def columns(ref, place):
    return ref[:, pl.ds(pl.multiple_of(place * WIDTH, WIDTH), WIDTH)]


def head_lanes():
    return lax.broadcasted_iota(jnp.int32, (ROW, WIDTH), 1) // HD


def stack_heads(rows, out):
    for head in range(HEADS):
        out[head * ROW : (head + 1) * ROW, :] = jnp.where(head_lanes() == head, rows, jnp.zeros_like(rows))


def pick_heads(stacked):
    total = jnp.zeros((ROW, WIDTH), F32)
    for head in range(HEADS):
        total = jnp.where(head_lanes() == head, stacked[head * ROW : (head + 1) * ROW], total)
    return total.astype(BF)


def own_kernel(
    act, w_q, w_k, w_v, w_o, cot, slots, live, a_near,
    wq, wk, wv, wo, query_out, keys_out, values_out, act_t, near_t, grad_out, cot_t, bias_out,
    act_s, cot_s, nb, mask, sems,
):
    core, y, z, x = places()
    pairs = (
        (slots, nb), (live, mask), (act, act_s), (w_k, wk), (w_v, wv), (w_q, wq), (cot, cot_s), (w_o, wo)
    )
    copies = [pltpu.make_async_copy(a, b, sems.at[i]) for i, (a, b) in enumerate(pairs)]
    for copy in copies:
        copy.start()
    near_t[...] = a_near[...].T
    copies[0].wait()
    copies[1].wait()
    bias_out[...] = slot_bias(nb, mask, core, y, z)
    copies[2].wait()
    act_t[...] = act_s[...].T
    for index, weight, out in ((3, wk, keys_out), (4, wv, values_out)):
        copies[index].wait()
        out[:ROW, :] = mm(act_s[...], weight[...]).astype(BF)
        out[ROW:, :] = mm(a_near[...], weight[...]).astype(BF)
    copies[5].wait()
    stack_heads(mm(act_s[...], wq[...]).astype(BF), query_out)
    copies[6].wait()
    cot_t[...] = cot_s[...].T
    copies[7].wait()
    grad_out[...] = mm(cot_s[...], columns(wo, x), NT)


def forward_kernel(
    a_far, wk, wv, query, keys_in, values_in, bias,
    keys, values, probs_out, att_out, far_t,
    probs_t,
):
    keys[ROW:, :] = keys_in[...]
    values[ROW:, :] = values_in[...]
    keys[:ROW, :] = mm(a_far[...], wk[...]).astype(BF)
    values[:ROW, :] = mm(a_far[...], wv[...]).astype(BF)
    bias_rows = jnp.concatenate(
        [jnp.broadcast_to(bias[patch : patch + 1, :], (PATCH, ROW)) for patch in range(KEYS // PATCH)],
        axis=0,
    )
    for head in range(HEADS):
        part = slice(head * ROW, (head + 1) * ROW)
        scores = mm(keys[...], query[part, :], NT) * (LOG2E * HD**-0.5) + bias_rows
        peak = jnp.max(scores, axis=0, keepdims=True)
        weights = jnp.exp2(scores - peak)
        probs = (weights * (1.0 / jnp.sum(weights, axis=0, keepdims=True))).astype(BF)
        probs_out[:, part] = probs
        probs_t[part, :] = probs.T
    att_out[...] = pick_heads(mm(probs_t[...], values[...]))
    far_t[...] = a_far[...].T


def backward_kernel(
    keys, values, probs_in, att, far_t, near_t, wo, query, act_t, grad_in, cot_t, c2, c1, c3,
    gq_out, far_out, own_out, send_out, keep_out,
    grad_s, scores_s, scores_t, dw_s,
):
    core, y, z, x = places()
    grad_att = grad_in[...]
    blocks = ((x ^ 2, c2), (x ^ 1, c1), (x ^ 3, c3))
    for place, block in blocks:
        grad_att += mm(block[...], columns(wo, place), NT)
    stack_heads(grad_att.astype(BF), grad_s)
    for head in range(HEADS):
        part = slice(head * ROW, (head + 1) * ROW)
        probs = probs_in[:, part].astype(F32)
        grad_probs = mm(values[...], grad_s[part, :], NT)
        centre = jnp.sum(probs * grad_probs, axis=0, keepdims=True)
        grad_scores = (probs * ((grad_probs - centre) * HD**-0.5)).astype(BF)
        scores_s[:, part] = grad_scores
        scores_t[part, :] = grad_scores.T
    gq = pick_heads(mm(scores_t[...], keys[...]))
    grad_key = mm(scores_s[...], query[...])
    grad_value = mm(probs_in[...], grad_s[...])
    gq_out[...] = gq
    far_out[0], far_out[1] = grad_key[:ROW].astype(BF), grad_value[:ROW].astype(BF)
    own_out[0], own_out[1] = grad_key[ROW : 2 * ROW], grad_value[ROW : 2 * ROW]
    for part, grad in enumerate((grad_key, grad_value)):
        for block in range(16):
            rows = slice(2 * ROW + 16 * block, 2 * ROW + 16 * (block + 1))
            send_out[128 + 16 * part + block] = grad[rows].astype(BF)

    for place, block_t in ((x, cot_t[...]), *((place, block[...].T) for place, block in blocks)):
        rows = pl.ds(pl.multiple_of(place * WIDTH, WIDTH), WIDTH)
        dw_s[3, rows, :] = mm(block_t, att[...])
    grad_key = grad_key.astype(BF)
    grad_value = grad_value.astype(BF)
    own = slice(ROW, 2 * ROW)
    dw_s[0] = mm(act_t[...], gq)
    for index, grad in ((1, grad_key), (2, grad_value)):
        dw_s[index] = (
            mm(act_t[...], grad[own]) + mm(far_t[...], grad[:ROW]) + mm(near_t[...], grad[2 * ROW :])
        )
    tables = [target_rows(z, y, *partners) for partners in PARTNERS]
    for number in range(32):
        first, second = (table[number] * 32 for table in tables)
        for c, out in ((1 - core, send_out), (core, keep_out)):
            row = pl.multiple_of(jnp.where(c == 0, first, second) + c * 16, 16)
            out[4 * number : 4 * number + 4] = dw_s[:, pl.ds(row, 16), :].astype(BF)


def share_kernel(count, *refs):
    terms, outs = refs[:count], refs[count:]
    size = outs[0].shape[0]
    for place, out in enumerate(outs):
        part = slice(size * place, size * (place + 1))
        total = terms[0][part].astype(F32)
        for term in terms[1:]:
            total += term[part].astype(F32)
        out[...] = total.astype(out.dtype)


def input_kernel(att, gq, own, near, far, wq, wk, wv, wo, keep, send):
    core, _, _, x = places()
    grads = []
    for part in range(2):
        from_near = near[128 + 16 * part : 144 + 16 * part].reshape(ROW, WIDTH)
        grads.append((own[part] + from_near.astype(F32) + far[part].astype(F32)).astype(BF))
    grad_key, grad_value = grads
    first, second = (mp_partner(core, x, step) for step in range(2))
    for out, targets in ((keep, (x, second)), (send, (first, x ^ 2))):
        for place, target in enumerate(targets):
            block = pl.ds(pl.multiple_of(target * WIDTH, WIDTH), WIDTH)
            out[2 * place] = mm(att[...], wo[:, block]).astype(out.dtype)
            out[2 * place + 1] = (
                mm(gq[...], wq[block, :], NT)
                + mm(grad_key, wk[block, :], NT)
                + mm(grad_value, wv[block, :], NT)
            ).astype(out.dtype)


def mp_sum_kernel(kept, got, out, grad):
    for part, ref in ((0, out), (1, grad)):
        ref[...] = (kept[part] + got[part].astype(F32)).astype(BF)


def last_sum_kernel(after, kept, got, dw):
    dw[...] = kept[...] + got[...].astype(F32)


def on_chip(*arrays):
    return [pltpu.with_memory_space_constraint(a, pltpu.VMEM) for a in arrays]


def call(
    kernel, name, outs, arrays, apart=(), scratch=(), limit=16, flops=0, moved=1_000_000, keep=True
):
    kept = [pltpu.VMEM(shape, dtype) if keep else jax.ShapeDtypeStruct(shape, dtype) for shape, dtype in outs]
    return pl.pallas_call(
        kernel,
        out_shape=tuple(kept),
        in_specs=[pl.BlockSpec(memory_space=pltpu.HBM)] * len(apart)
        + [pl.BlockSpec(memory_space=pltpu.VMEM)] * len(arrays),
        out_specs=(pl.BlockSpec(memory_space=pltpu.VMEM),) * len(kept),
        scratch_shapes=list(scratch),
        compiler_params=pltpu.CompilerParams(vmem_limit_bytes=limit * 1024 * 1024),
        cost_estimate=pl.CostEstimate(flops=flops, bytes_accessed=moved, transcendentals=0),
        name=name,
    )(*[pltpu.with_memory_space_constraint(a, pltpu.HBM) for a in apart], *on_chip(*arrays))


def move(value, axis, target):
    count = lax.axis_size(axis)
    return lax.ppermute(
        value, axis, [(i, target(i)) for i in range(count) if 0 <= target(i) < count]
    )


def over_mp(value, step):
    def target(i):
        return i // 4 * 4 + mp_partner(i // 4 % 2, i % 4, step)

    return move(value, SPACE + ("mp",), target)


def near_row(value):
    return move(value, SPACE, lambda i: i ^ 1)


def far_row(value):
    def target(i):
        row, x = i // 4, i % 4
        if row in (0, 63):
            return row * 4 + (x ^ 1)
        return (row + 1 if row % 2 else row - 1) * 4 + x

    return move(value, SPACE + ("mp",), target)


def body(activations, w_query, w_key, w_value, w_out, grad_output, neighbours, pad_mask):
    act_far = far_row(activations)
    cots = [move(grad_output, "mp", lambda i, step=step: i ^ step) for step in (2, 1, 3)]
    act_near = near_row(activations)

    square = (ROW, WIDTH)
    stacked = (HEADS * ROW, WIDTH)
    wq, wk, wv, wo, query, keys, values, act_t, near_t, grad_own, cot_t, bias = call(
        own_kernel,
        "own_part",
        [((D, WIDTH), BF)] * 3
        + [((WIDTH, D), BF), (stacked, BF), ((2 * ROW, WIDTH), BF), ((2 * ROW, WIDTH), BF)]
        + [((D, ROW), BF), ((D, ROW), BF), (square, F32), (square, BF), ((16, ROW), F32)],
        [act_near],
        apart=(activations, w_query, w_key, w_value, w_out, grad_output, neighbours, pad_mask),
        scratch=[
            pltpu.VMEM((ROW, D), BF),
            pltpu.VMEM(square, BF),
            pltpu.SMEM((4, 9), jnp.int32),
            pltpu.SMEM((4, 9), jnp.int32),
            pltpu.SemaphoreType.DMA((8,)),
        ],
        flops=600_000_000,
        moved=6_000_000,
    )

    block = (16, WIDTH)
    keys, values, probs, att, far_t = call(
        forward_kernel,
        "forward",
        [((KEYS, WIDTH), BF)] * 2 + [((KEYS, HEADS * ROW), BF), (square, BF), ((D, ROW), BF)],
        [act_far, wk, wv, query, keys, values, bias],
        scratch=[pltpu.VMEM((HEADS * ROW, KEYS), BF)],
        limit=20,
        flops=2_000_000_000,
        moved=6_000_000,
    )
    gq, far, own, dw_send, dw_keep = call(
        backward_kernel,
        "backward",
        [
            (square, BF),
            ((2, ROW, WIDTH), BF),
            ((2, ROW, WIDTH), F32),
            ((160,) + block, BF),
            ((128,) + block, BF),
        ],
        [keys, values, probs, att, far_t, near_t, wo, query, act_t, grad_own, cot_t, *cots],
        scratch=[
            pltpu.VMEM(stacked, BF),
            pltpu.VMEM((KEYS, HEADS * ROW), BF),
            pltpu.VMEM((HEADS * ROW, KEYS), BF),
            pltpu.VMEM((4, D, WIDTH), F32),
        ],
        limit=24,
        flops=3_000_000_000,
        moved=8_000_000,
    )

    def share(name, terms, ways, kept_as, flops=0):
        part = (terms[0].shape[0] // ways,) + terms[0].shape[1:]
        outs = [(part, kept_as)] + [(part, BF)] * (ways - 1)
        return call(functools.partial(share_kernel, len(terms)), name, outs, terms, flops=flops)

    def over_chips(value, y_step, z_step):
        def target(i):
            z, y, c = i // 8, i // 2 % 4, i % 2
            y_partners, z_partners = PARTNERS[c]
            y = y if y_step is None else y_partners[y_step](y)
            z = z if z_step is None else z_partners[z_step](z)
            return z * 8 + y * 2 + c

        return move(value, SPACE, target)

    def four_ways(parts, step):
        along_z, along_y = over_chips(parts[1], None, step), over_chips(parts[2], step, None)
        return [parts[0], over_chips(parts[3], step, step), along_y, along_z]

    from_core = near_row(dw_send)
    grad_far = far_row(far)
    parts = four_ways(share("core_sum", [dw_keep, from_core], 4, BF), 0)

    mp_keep, mp_send = call(
        input_kernel,
        "input_grad",
        [((4, ROW, WIDTH), F32), ((4, ROW, WIDTH), BF)],
        [att, gq, own, from_core, grad_far, wq, wk, wv, wo],
        flops=540_000_000,
        moved=4_000_000,
    )
    mp_keep, mp_send = share("mp_share", [mp_keep, over_mp(mp_send, 0)], 2, F32)
    parts = four_ways(share("first_sum", parts, 4, F32, FIRST_FLOPS), 1)
    keep, send = share("second_sum", parts, 2, F32, SECOND_FLOPS)
    got = over_chips(send, None, 2)
    output, grad_input = call(
        mp_sum_kernel, "mp_sum", [(square, BF)] * 2, [mp_keep, over_mp(mp_send, 1)], keep=False
    )
    (dw,) = call(last_sum_kernel, "last_sum", [((4,) + block, F32)], [keep, got], apart=(output,), keep=False)
    return output, grad_input, dw


def solution(mesh):
    fine = Mesh(mesh.devices.reshape(8, 4, 2, 4), SPACE + ("mp",))
    in_specs = (
        P(SPACE, None),
        P(None, "mp"),
        P(None, "mp"),
        P(None, "mp"),
        P("mp", None),
        P(SPACE, "mp"),
        P(SPACE, None),
        P(SPACE, None),
    )
    out_specs = (P(SPACE, "mp"), P(SPACE, "mp"), P(None, SPACE, "mp"))
    return jax.shard_map(body, mesh=fine, in_specs=in_specs, out_specs=out_specs, check_vma=False)
```

```python
import functools

import jax
import jax.numpy as jnp
from jax import lax
from jax.experimental import pallas as pl
from jax.experimental.pallas import tpu as pltpu
from jax.sharding import Mesh
from jax.sharding import PartitionSpec as P

HD = 64
PATCH = 64
D = 1024
ROW = 256
WIDTH = 256
HEADS = WIDTH // HD
FIRST_FLOPS, SECOND_FLOPS = 4_000_000_000, 4_000_000_000
KEYS = 3 * ROW
LOG2E = 1.4426950408889634
BF = jnp.bfloat16
F32 = jnp.float32
SPACE = ("z", "y", "core")

NN = (((1,), (0,)), ((), ()))
NT = (((1,), (1,)), ((), ()))


def mm(a, b, dims=NN):
    return lax.dot_general(a, b, dims, preferred_element_type=F32)


def places():
    return [lax.axis_index(a) for a in ("core", "y", "z", "mp")]


def slot_bias(nb, mask, core, y, z):
    row = (z * 4 + y) * 2 + core
    sign = 1 - 2 * core
    patch_of_lane = lax.broadcasted_iota(jnp.int32, (16, ROW), 1) // PATCH
    patch_of_row = lax.broadcasted_iota(jnp.int32, (16, ROW), 0)
    count = jnp.zeros((16, ROW), F32)
    for slot in range(9):
        named = jnp.zeros((16, ROW), jnp.int32)
        for patch in range(4):
            number = nb[patch, slot]
            band = 1 + sign * (lax.div(number, 4) - row)
            place = jnp.where(mask[patch, slot] > 0, band * 4 + lax.rem(number, 4), -1)
            named = jnp.where(patch_of_lane == patch, place, named)
        count += jnp.where(named == patch_of_row, 1.0, 0.0)
    return jnp.where(count > 0, jnp.where(count > 1, jnp.log(count) * LOG2E, 0.0), -1e30)


def y_pair(y):
    return y + 1 - 2 * (y % 2)


def y_other(y):
    return 3 - y


def z_pair(z):
    return z + 1 - 2 * (z % 2)


def z_other(z):
    return (z + 7 + 2 * (z % 2)) % 8


def z_far(z):
    middle = (z % 4) * (3 - z % 4) // 2
    return (1 - middle) * (3 - 2 * (z % 4) + z) + middle * (7 - z)


def z_far_too(z):
    return z + 4 + (1 - 2 * (z % 2)) - 8 * (z // 4)


def target_rows(z, y, y_partners, z_partners):
    def reached(start, partners):
        places = [start]
        for partner in partners:
            places = [there for here in places for there in (here, partner(here))]
        return places

    ys, zs = reached(y, y_partners), reached(z, z_partners)
    rows = []
    for number in range(32):
        y1, z1, y2, z2, z3 = ((number >> (4 - bit)) & 1 for bit in range(5))
        rows.append(zs[4 * z1 + 2 * z2 + z3] * 4 + ys[2 * y1 + y2])
    return rows


PARTNERS = (
    ((y_other, y_pair), (z_pair, z_other, z_far)),
    ((y_pair, y_other), (z_other, z_pair, z_far_too)),
)


def mp_partner(core, x, step):
    near, across = x ^ 1, 3 - x
    if isinstance(core, int):
        return (near, across)[(core + step) % 2]
    return jnp.where(core == step, near, across)


def columns(ref, place):
    return ref[:, pl.ds(pl.multiple_of(place * WIDTH, WIDTH), WIDTH)]


def head_lanes():
    return lax.broadcasted_iota(jnp.int32, (ROW, WIDTH), 1) // HD


def stack_heads(rows, out):
    for head in range(HEADS):
        out[head * ROW : (head + 1) * ROW, :] = jnp.where(head_lanes() == head, rows, jnp.zeros_like(rows))


def pick_heads(stacked):
    total = jnp.zeros((ROW, WIDTH), F32)
    for head in range(HEADS):
        total = jnp.where(head_lanes() == head, stacked[head * ROW : (head + 1) * ROW], total)
    return total.astype(BF)


def store_halves(out, rows, start, core):
    for block in range(rows.shape[0] // 32):
        for c in range(2):
            half = jnp.where(core == c, D // 2, 0)
            there = pl.ds(pl.multiple_of(half + start + 16 * block, 16), 16)
            out[there, :] = rows[32 * block + 16 * c : 32 * block + 16 * (c + 1)]


def spread_bias(bias, patches):
    return jnp.concatenate(
        [jnp.broadcast_to(bias[patch : patch + 1, :], (PATCH, ROW)) for patch in patches], axis=0
    )


def own_kernel(
    act, w_q, w_k, w_v, w_o, cot, slots, live, a_near,
    wq, wk, wv, wo, query_out, keys_out, values_out, exps_out, peaks_out, act_t, near_t, grad_out, cot_t, bias_out,
    act_s, cot_s, nb, mask, sems,
):
    core, y, z, x = places()
    pairs = (
        (slots, nb), (live, mask), (act, act_s), (w_k, wk), (w_v, wv), (w_q, wq), (cot, cot_s), (w_o, wo)
    )
    copies = [pltpu.make_async_copy(a, b, sems.at[i]) for i, (a, b) in enumerate(pairs)]
    for copy in copies:
        copy.start()
    store_halves(near_t, a_near[...].T, 0, core)
    copies[0].wait()
    copies[1].wait()
    bias = slot_bias(nb, mask, core, y, z)
    bias_out[...] = bias
    copies[2].wait()
    store_halves(act_t, act_s[...].T, 0, core)
    for index, weight, out in ((3, wk, keys_out), (4, wv, values_out)):
        copies[index].wait()
        out[:ROW, :] = mm(act_s[...], weight[...]).astype(BF)
        out[ROW:, :] = mm(a_near[...], weight[...]).astype(BF)
    copies[5].wait()
    stack_heads(mm(act_s[...], wq[...]).astype(BF), query_out)
    bias_rows = spread_bias(bias, range(4, 12))
    for head in range(HEADS):
        scores = mm(keys_out[...], query_out[head * ROW : (head + 1) * ROW, :], NT)
        scores = scores * (LOG2E * HD**-0.5) + bias_rows
        peak = jnp.max(scores, axis=0, keepdims=True)
        exps = jnp.exp2(scores - peak)
        exps_out[head] = exps
        peaks_out[head : head + 1, :] = peak
        peaks_out[HEADS + head : HEADS + head + 1, :] = jnp.sum(exps, axis=0, keepdims=True)
    copies[6].wait()
    cot_t[...] = cot_s[...].T
    copies[7].wait()
    grad_out[...] = mm(cot_s[...], columns(wo, x), NT)


def forward_kernel(
    a_far, wk, wv, query, keys_in, values_in, exps, peaks, bias,
    keys, values, probs_out, att_out, far_t,
    probs_t,
):
    core = places()[0]
    keys[ROW:, :] = keys_in[...]
    values[ROW:, :] = values_in[...]
    keys[:ROW, :] = mm(a_far[...], wk[...]).astype(BF)
    values[:ROW, :] = mm(a_far[...], wv[...]).astype(BF)
    bias_rows = spread_bias(bias, range(4))
    for head in range(HEADS):
        part = slice(head * ROW, (head + 1) * ROW)
        scores = mm(keys[:ROW, :], query[part, :], NT) * (LOG2E * HD**-0.5) + bias_rows
        peak_before = peaks[head : head + 1, :]
        peak = jnp.maximum(peak_before, jnp.max(scores, axis=0, keepdims=True))
        weights = jnp.exp2(scores - peak)
        before = jnp.exp2(peak_before - peak)
        total = before * peaks[HEADS + head : HEADS + head + 1, :] + jnp.sum(weights, axis=0, keepdims=True)
        scale = 1.0 / total
        far_probs = (weights * scale).astype(BF)
        other_probs = (exps[head] * (before * scale)).astype(BF)
        probs_out[:ROW, part] = far_probs
        probs_out[ROW:, part] = other_probs
        probs_t[part, :ROW] = far_probs.T
        probs_t[part, ROW:] = other_probs.T
    att_out[...] = pick_heads(mm(probs_t[...], values[...]))
    store_halves(far_t, a_far[...].T, 0, core)


def weight_terms(half, partners, act_t, far_t, near_t, cot_t, gq, grad_key, grad_value, att, out, dw_s):
    rows = slice(half * (D // 2), (half + 1) * (D // 2))
    dw_s[0] = mm(act_t[rows, :], gq[...])
    for index, grad in ((1, grad_key), (2, grad_value)):
        dw_s[index] = (
            mm(act_t[rows, :], grad[ROW : 2 * ROW, :])
            + mm(far_t[rows, :], grad[:ROW, :])
            + mm(near_t[rows, :], grad[2 * ROW :, :])
        )
    dw_s[3] = mm(cot_t[rows, :], att[...])
    core, y, z, _ = places()
    tables = [target_rows(z, y, *pair) for pair in PARTNERS]
    for number in range(32):
        zero, one = (table[number] * 16 for table in tables)
        row = pl.multiple_of(jnp.where(partners == 0, zero, one), 16)
        out[4 * number : 4 * number + 4] = dw_s[:, pl.ds(row, 16), :].astype(BF)


def backward_kernel(
    keys, values, probs_in, att, far_t, near_t, wo, query, act_t, grad_in, cot_own, c2, c1, c3,
    gq, far_out, own_out, grad_key, grad_value, cot_t, send_out,
    grad_s, scores_s, scores_t, dw_s,
):
    core, y, z, x = places()
    grad_att = grad_in[...]
    blocks = ((x ^ 2, c2), (x ^ 1, c1), (x ^ 3, c3))
    for place, block in blocks:
        grad_att += mm(block[...], columns(wo, place), NT)
    stack_heads(grad_att.astype(BF), grad_s)
    for head in range(HEADS):
        part = slice(head * ROW, (head + 1) * ROW)
        probs = probs_in[:, part].astype(F32)
        grad_probs = mm(values[...], grad_s[part, :], NT)
        centre = jnp.sum(probs * grad_probs, axis=0, keepdims=True)
        grad_scores = (probs * ((grad_probs - centre) * HD**-0.5)).astype(BF)
        scores_s[:, part] = grad_scores
        scores_t[part, :] = grad_scores.T
    gq[...] = pick_heads(mm(scores_t[...], keys[...]))
    for index, (grad, out) in enumerate(
        ((mm(scores_s[...], query[...]), grad_key), (mm(probs_in[...], grad_s[...]), grad_value))
    ):
        low = grad.astype(BF)
        out[...] = low
        far_out[index] = low[:ROW]
        own_out[index] = grad[ROW : 2 * ROW]
        for block in range(16):
            rows = slice(2 * ROW + 16 * block, 2 * ROW + 16 * (block + 1))
            send_out[128 + 16 * index + block] = low[rows]
    for place, block_t in ((x, cot_own[...]), *((place, block[...].T) for place, block in blocks)):
        store_halves(cot_t, block_t, place * (WIDTH // 2), core)
    weight_terms(
        0, 1 - core, act_t, far_t, near_t, cot_t, gq, grad_key, grad_value, att, send_out, dw_s
    )


def keep_kernel(act_t, far_t, near_t, cot_t, gq, grad_key, grad_value, att, keep_out, dw_s):
    core = places()[0]
    weight_terms(
        1, core, act_t, far_t, near_t, cot_t, gq, grad_key, grad_value, att, keep_out, dw_s
    )


def share_kernel(count, *refs):
    terms, outs = refs[:count], refs[count:]
    size = outs[0].shape[0]
    for place, out in enumerate(outs):
        part = slice(size * place, size * (place + 1))
        total = terms[0][part].astype(F32)
        for term in terms[1:]:
            total += term[part].astype(F32)
        out[...] = total.astype(out.dtype)


def input_kernel(att, gq, own, near, far, wq, wk, wv, wo, keep, send):
    core, _, _, x = places()
    grads = []
    for part in range(2):
        from_near = near[128 + 16 * part : 144 + 16 * part].reshape(ROW, WIDTH)
        grads.append((own[part] + from_near.astype(F32) + far[part].astype(F32)).astype(BF))
    grad_key, grad_value = grads
    first, second = (mp_partner(core, x, step) for step in range(2))
    for out, targets in ((keep, (x, second)), (send, (first, x ^ 2))):
        for place, target in enumerate(targets):
            block = pl.ds(pl.multiple_of(target * WIDTH, WIDTH), WIDTH)
            out[2 * place] = mm(att[...], wo[:, block]).astype(out.dtype)
            out[2 * place + 1] = (
                mm(gq[...], wq[block, :], NT)
                + mm(grad_key, wk[block, :], NT)
                + mm(grad_value, wv[block, :], NT)
            ).astype(out.dtype)


def mp_sum_kernel(kept, got, out, grad):
    for part, ref in ((0, out), (1, grad)):
        ref[...] = (kept[part] + got[part].astype(F32)).astype(BF)


def last_sum_kernel(after, kept, got, dw):
    dw[...] = kept[...] + got[...].astype(F32)


def on_chip(*arrays):
    return [pltpu.with_memory_space_constraint(a, pltpu.VMEM) for a in arrays]


def call(
    kernel, name, outs, arrays, apart=(), scratch=(), limit=16, flops=0, moved=1_000_000, keep=True
):
    kept = [pltpu.VMEM(shape, dtype) if keep else jax.ShapeDtypeStruct(shape, dtype) for shape, dtype in outs]
    return pl.pallas_call(
        kernel,
        out_shape=tuple(kept),
        in_specs=[pl.BlockSpec(memory_space=pltpu.HBM)] * len(apart)
        + [pl.BlockSpec(memory_space=pltpu.VMEM)] * len(arrays),
        out_specs=(pl.BlockSpec(memory_space=pltpu.VMEM),) * len(kept),
        scratch_shapes=list(scratch),
        compiler_params=pltpu.CompilerParams(vmem_limit_bytes=limit * 1024 * 1024),
        cost_estimate=pl.CostEstimate(flops=flops, bytes_accessed=moved, transcendentals=0),
        name=name,
    )(*[pltpu.with_memory_space_constraint(a, pltpu.HBM) for a in apart], *on_chip(*arrays))


def move(value, axis, target):
    count = lax.axis_size(axis)
    return lax.ppermute(
        value, axis, [(i, target(i)) for i in range(count) if 0 <= target(i) < count]
    )


def over_mp(value, step):
    def target(i):
        return i // 4 * 4 + mp_partner(i // 4 % 2, i % 4, step)

    return move(value, SPACE + ("mp",), target)


def near_row(value):
    return move(value, SPACE, lambda i: i ^ 1)


def far_row(value):
    def target(i):
        row, x = i // 4, i % 4
        if row in (0, 63):
            return row * 4 + (x ^ 1)
        return (row + 1 if row % 2 else row - 1) * 4 + x

    return move(value, SPACE + ("mp",), target)


def body(activations, w_query, w_key, w_value, w_out, grad_output, neighbours, pad_mask):
    act_far = far_row(activations)
    cots = [move(grad_output, "mp", lambda i, step=step: i ^ step) for step in (2, 1, 3)]
    act_near = near_row(activations)

    square = (ROW, WIDTH)
    stacked = (HEADS * ROW, WIDTH)
    wq, wk, wv, wo, query, keys, values, exps, peaks, act_t, near_t, grad_own, cot_own, bias = call(
        own_kernel,
        "own_part",
        [((D, WIDTH), BF)] * 3
        + [((WIDTH, D), BF), (stacked, BF), ((2 * ROW, WIDTH), BF), ((2 * ROW, WIDTH), BF)]
        + [((HEADS, 2 * ROW, ROW), F32), ((2 * HEADS, ROW), F32)]
        + [((D, ROW), BF), ((D, ROW), BF), (square, F32), (square, BF), ((16, ROW), F32)],
        [act_near],
        apart=(activations, w_query, w_key, w_value, w_out, grad_output, neighbours, pad_mask),
        scratch=[
            pltpu.VMEM((ROW, D), BF),
            pltpu.VMEM(square, BF),
            pltpu.SMEM((4, 9), jnp.int32),
            pltpu.SMEM((4, 9), jnp.int32),
            pltpu.SemaphoreType.DMA((8,)),
        ],
        flops=600_000_000,
        moved=6_000_000,
    )

    block = (16, WIDTH)
    keys, values, probs, att, far_t = call(
        forward_kernel,
        "forward",
        [((KEYS, WIDTH), BF)] * 2 + [((KEYS, HEADS * ROW), BF), (square, BF), ((D, ROW), BF)],
        [act_far, wk, wv, query, keys, values, exps, peaks, bias],
        scratch=[pltpu.VMEM((HEADS * ROW, KEYS), BF)],
        limit=20,
        flops=2_000_000_000,
        moved=6_000_000,
    )
    gq, far, own, grad_key, grad_value, cot_t, dw_send = call(
        backward_kernel,
        "backward",
        [
            (square, BF),
            ((2, ROW, WIDTH), BF),
            ((2, ROW, WIDTH), F32),
            ((KEYS, WIDTH), BF),
            ((KEYS, WIDTH), BF),
            ((D, ROW), BF),
            ((160,) + block, BF),
        ],
        [keys, values, probs, att, far_t, near_t, wo, query, act_t, grad_own, cot_own, *cots],
        scratch=[
            pltpu.VMEM(stacked, BF),
            pltpu.VMEM((KEYS, HEADS * ROW), BF),
            pltpu.VMEM((HEADS * ROW, KEYS), BF),
            pltpu.VMEM((4, D // 2, WIDTH), F32),
        ],
        limit=24,
        flops=2_000_000_000,
        moved=8_000_000,
    )
    (dw_keep,) = call(
        keep_kernel,
        "keep_terms",
        [((128,) + block, BF)],
        [act_t, far_t, near_t, cot_t, gq, grad_key, grad_value, att],
        scratch=[pltpu.VMEM((4, D // 2, WIDTH), F32)],
        flops=1_000_000_000,
        moved=4_000_000,
    )

    def share(name, terms, ways, kept_as, flops=0):
        part = (terms[0].shape[0] // ways,) + terms[0].shape[1:]
        outs = [(part, kept_as)] + [(part, BF)] * (ways - 1)
        return call(functools.partial(share_kernel, len(terms)), name, outs, terms, flops=flops)

    def over_chips(value, y_step, z_step):
        def target(i):
            z, y, c = i // 8, i // 2 % 4, i % 2
            y_partners, z_partners = PARTNERS[c]
            y = y if y_step is None else y_partners[y_step](y)
            z = z if z_step is None else z_partners[z_step](z)
            return z * 8 + y * 2 + c

        return move(value, SPACE, target)

    def four_ways(parts, step):
        along_z, along_y = over_chips(parts[1], None, step), over_chips(parts[2], step, None)
        return [parts[0], over_chips(parts[3], step, step), along_y, along_z]

    from_core = near_row(dw_send)
    grad_far = far_row(far)
    parts = four_ways(share("core_sum", [dw_keep, from_core], 4, BF), 0)

    mp_keep, mp_send = call(
        input_kernel,
        "input_grad",
        [((4, ROW, WIDTH), F32), ((4, ROW, WIDTH), BF)],
        [att, gq, own, from_core, grad_far, wq, wk, wv, wo],
        flops=540_000_000,
        moved=4_000_000,
    )
    mp_keep, mp_send = share("mp_share", [mp_keep, over_mp(mp_send, 0)], 2, F32)
    parts = four_ways(share("first_sum", parts, 4, F32, FIRST_FLOPS), 1)
    keep, send = share("second_sum", parts, 2, F32, SECOND_FLOPS)
    got = over_chips(send, None, 2)
    output, grad_input = call(
        mp_sum_kernel, "mp_sum", [(square, BF)] * 2, [mp_keep, over_mp(mp_send, 1)], keep=False
    )
    (dw,) = call(last_sum_kernel, "last_sum", [((4,) + block, F32)], [keep, got], apart=(output,), keep=False)
    return output, grad_input, dw


def solution(mesh):
    fine = Mesh(mesh.devices.reshape(8, 4, 2, 4), SPACE + ("mp",))
    in_specs = (
        P(SPACE, None),
        P(None, "mp"),
        P(None, "mp"),
        P(None, "mp"),
        P("mp", None),
        P(SPACE, "mp"),
        P(SPACE, None),
        P(SPACE, None),
    )
    out_specs = (P(SPACE, "mp"), P(SPACE, "mp"), P(None, SPACE, "mp"))
    return jax.shard_map(body, mesh=fine, in_specs=in_specs, out_specs=out_specs, check_vma=False)
```

```python
import functools

import jax
import jax.numpy as jnp
from jax import lax
from jax.experimental import pallas as pl
from jax.experimental.pallas import tpu as pltpu
from jax.sharding import Mesh
from jax.sharding import PartitionSpec as P

HD = 64
PATCH = 64
D = 1024
ROW = 256
WIDTH = 256
HEADS = WIDTH // HD
FIRST_FLOPS, SECOND_FLOPS = 4_000_000_000, 4_000_000_000
KEYS = 3 * ROW
LOG2E = 1.4426950408889634
BF = jnp.bfloat16
F32 = jnp.float32
SPACE = ("z", "y", "core")

NN = (((1,), (0,)), ((), ()))
NT = (((1,), (1,)), ((), ()))


def mm(a, b, dims=NN):
    return lax.dot_general(a, b, dims, preferred_element_type=F32)


def places():
    return [lax.axis_index(a) for a in ("core", "y", "z", "mp")]


def slot_bias(nb, mask, core, y, z):
    row = (z * 4 + y) * 2 + core
    sign = 1 - 2 * core
    patch_of_lane = lax.broadcasted_iota(jnp.int32, (16, ROW), 1) // PATCH
    patch_of_row = lax.broadcasted_iota(jnp.int32, (16, ROW), 0)
    count = jnp.zeros((16, ROW), F32)
    for slot in range(9):
        named = jnp.zeros((16, ROW), jnp.int32)
        for patch in range(4):
            number = nb[patch, slot]
            band = 1 + sign * (lax.div(number, 4) - row)
            place = jnp.where(mask[patch, slot] > 0, band * 4 + lax.rem(number, 4), -1)
            named = jnp.where(patch_of_lane == patch, place, named)
        count += jnp.where(named == patch_of_row, 1.0, 0.0)
    return jnp.where(count > 0, jnp.where(count > 1, jnp.log(count) * LOG2E, 0.0), -1e30)


def y_pair(y):
    return y + 1 - 2 * (y % 2)


def y_other(y):
    return 3 - y


def z_pair(z):
    return z + 1 - 2 * (z % 2)


def z_other(z):
    return (z + 7 + 2 * (z % 2)) % 8


def z_far(z):
    middle = (z % 4) * (3 - z % 4) // 2
    return (1 - middle) * (3 - 2 * (z % 4) + z) + middle * (7 - z)


def z_far_too(z):
    return z + 4 + (1 - 2 * (z % 2)) - 8 * (z // 4)


def target_rows(z, y, y_partners, z_partners):
    def reached(start, partners):
        places = [start]
        for partner in partners:
            places = [there for here in places for there in (here, partner(here))]
        return places

    ys, zs = reached(y, y_partners), reached(z, z_partners)
    rows = []
    for number in range(32):
        y1, z1, y2, z2, z3 = ((number >> (4 - bit)) & 1 for bit in range(5))
        rows.append(zs[4 * z1 + 2 * z2 + z3] * 4 + ys[2 * y1 + y2])
    return rows


PARTNERS = (
    ((y_other, y_pair), (z_pair, z_other, z_far)),
    ((y_pair, y_other), (z_other, z_pair, z_far_too)),
)


def mp_partner(core, x, step):
    near, across = x ^ 1, 3 - x
    if isinstance(core, int):
        return (near, across)[(core + step) % 2]
    return jnp.where(core == step, near, across)


def columns(ref, place):
    return ref[:, pl.ds(pl.multiple_of(place * WIDTH, WIDTH), WIDTH)]


def head_lanes():
    return lax.broadcasted_iota(jnp.int32, (ROW, WIDTH), 1) // HD


def stack_heads(rows, out):
    for head in range(HEADS):
        out[head * ROW : (head + 1) * ROW, :] = jnp.where(head_lanes() == head, rows, jnp.zeros_like(rows))


def pick_heads(stacked):
    total = jnp.zeros((ROW, WIDTH), F32)
    for head in range(HEADS):
        total = jnp.where(head_lanes() == head, stacked[head * ROW : (head + 1) * ROW], total)
    return total.astype(BF)


def store_halves(out, rows, start, core):
    for block in range(rows.shape[0] // 32):
        for c in range(2):
            half = jnp.where(core == c, D // 2, 0)
            there = pl.ds(pl.multiple_of(half + start + 16 * block, 16), 16)
            out[there, :] = rows[32 * block + 16 * c : 32 * block + 16 * (c + 1)]


def spread_bias(bias, patches):
    return jnp.concatenate(
        [jnp.broadcast_to(bias[patch : patch + 1, :], (PATCH, ROW)) for patch in patches], axis=0
    )


def own_kernel(
    act, w_q, w_k, w_v, w_o, cot, slots, live, a_near,
    wq, wk, wv, wo, query_out, keys_out, values_out, exps_out, peaks_out, act_t, near_t, grad_out, cot_t, bias_out,
    act_s, cot_s, nb, mask, sems,
):
    core, y, z, x = places()
    pairs = (
        (slots, nb), (live, mask), (act, act_s), (w_k, wk), (w_v, wv), (w_q, wq), (cot, cot_s), (w_o, wo)
    )
    copies = [pltpu.make_async_copy(a, b, sems.at[i]) for i, (a, b) in enumerate(pairs)]
    for copy in copies:
        copy.start()
    store_halves(near_t, a_near[...].T, 0, core)
    copies[0].wait()
    copies[1].wait()
    bias = slot_bias(nb, mask, core, y, z)
    bias_out[...] = bias
    copies[2].wait()
    store_halves(act_t, act_s[...].T, 0, core)
    for index, weight, out in ((3, wk, keys_out), (4, wv, values_out)):
        copies[index].wait()
        out[:ROW, :] = mm(act_s[...], weight[...]).astype(BF)
        out[ROW:, :] = mm(a_near[...], weight[...]).astype(BF)
    copies[5].wait()
    stack_heads(mm(act_s[...], wq[...]).astype(BF), query_out)
    bias_rows = spread_bias(bias, range(4, 12))
    for head in range(HEADS):
        scores = mm(keys_out[...], query_out[head * ROW : (head + 1) * ROW, :], NT)
        scores = scores * (LOG2E * HD**-0.5) + bias_rows
        peak = jnp.max(scores, axis=0, keepdims=True)
        exps = jnp.exp2(scores - peak)
        exps_out[head] = exps
        peaks_out[head : head + 1, :] = peak
        peaks_out[HEADS + head : HEADS + head + 1, :] = jnp.sum(exps, axis=0, keepdims=True)
    copies[6].wait()
    cot_t[...] = cot_s[...].T
    copies[7].wait()
    grad_out[...] = mm(cot_s[...], columns(wo, x), NT)


def forward_kernel(
    a_far, wk, wv, wo, query, keys_in, values_in, exps, peaks, bias,
    keys, values, probs_out, att_out, far_t, out_keep, out_send,
    probs_t,
):
    core, _, _, x = places()
    keys[ROW:, :] = keys_in[...]
    values[ROW:, :] = values_in[...]
    keys[:ROW, :] = mm(a_far[...], wk[...]).astype(BF)
    values[:ROW, :] = mm(a_far[...], wv[...]).astype(BF)
    bias_rows = spread_bias(bias, range(4))
    for head in range(HEADS):
        part = slice(head * ROW, (head + 1) * ROW)
        scores = mm(keys[:ROW, :], query[part, :], NT) * (LOG2E * HD**-0.5) + bias_rows
        peak_before = peaks[head : head + 1, :]
        peak = jnp.maximum(peak_before, jnp.max(scores, axis=0, keepdims=True))
        weights = jnp.exp2(scores - peak)
        before = jnp.exp2(peak_before - peak)
        total = before * peaks[HEADS + head : HEADS + head + 1, :] + jnp.sum(weights, axis=0, keepdims=True)
        scale = 1.0 / total
        far_probs = (weights * scale).astype(BF)
        other_probs = (exps[head] * (before * scale)).astype(BF)
        probs_out[:ROW, part] = far_probs
        probs_out[ROW:, part] = other_probs
        probs_t[part, :ROW] = far_probs.T
        probs_t[part, ROW:] = other_probs.T
    att = pick_heads(mm(probs_t[...], values[...]))
    att_out[...] = att
    first, second = (mp_partner(core, x, step) for step in range(2))
    for out, targets in ((out_keep, (x, second)), (out_send, (first, x ^ 2))):
        for place, target in enumerate(targets):
            out[place] = mm(att, columns(wo, target)).astype(out.dtype)
    store_halves(far_t, a_far[...].T, 0, core)


def weight_terms(half, partners, act_t, far_t, near_t, cot_t, gq, grad_key, grad_value, att, out, dw_s):
    rows = slice(half * (D // 2), (half + 1) * (D // 2))
    dw_s[0] = mm(act_t[rows, :], gq[...])
    for index, grad in ((1, grad_key), (2, grad_value)):
        dw_s[index] = (
            mm(act_t[rows, :], grad[ROW : 2 * ROW, :])
            + mm(far_t[rows, :], grad[:ROW, :])
            + mm(near_t[rows, :], grad[2 * ROW :, :])
        )
    dw_s[3] = mm(cot_t[rows, :], att[...])
    core, y, z, _ = places()
    tables = [target_rows(z, y, *pair) for pair in PARTNERS]
    for number in range(32):
        zero, one = (table[number] * 16 for table in tables)
        row = pl.multiple_of(jnp.where(partners == 0, zero, one), 16)
        out[4 * number : 4 * number + 4] = dw_s[:, pl.ds(row, 16), :].astype(BF)


def backward_kernel(
    keys, values, probs_in, att, far_t, near_t, wo, query, act_t, grad_in, cot_own, c2, c1, c3,
    gq, far_out, own_out, grad_key, grad_value, cot_t, send_out,
    grad_s, scores_s, scores_t, dw_s,
):
    core, y, z, x = places()
    grad_att = grad_in[...]
    blocks = ((x ^ 2, c2), (x ^ 1, c1), (x ^ 3, c3))
    for place, block in blocks:
        grad_att += mm(block[...], columns(wo, place), NT)
    stack_heads(grad_att.astype(BF), grad_s)
    for head in range(HEADS):
        part = slice(head * ROW, (head + 1) * ROW)
        probs = probs_in[:, part].astype(F32)
        grad_probs = mm(values[...], grad_s[part, :], NT)
        centre = jnp.sum(probs * grad_probs, axis=0, keepdims=True)
        grad_scores = (probs * ((grad_probs - centre) * HD**-0.5)).astype(BF)
        scores_s[:, part] = grad_scores
        scores_t[part, :] = grad_scores.T
    gq[...] = pick_heads(mm(scores_t[...], keys[...]))
    for index, (grad, out) in enumerate(
        ((mm(scores_s[...], query[...]), grad_key), (mm(probs_in[...], grad_s[...]), grad_value))
    ):
        low = grad.astype(BF)
        out[...] = low
        far_out[index] = low[:ROW]
        own_out[index] = grad[ROW : 2 * ROW]
        for block in range(16):
            rows = slice(2 * ROW + 16 * block, 2 * ROW + 16 * (block + 1))
            send_out[128 + 16 * index + block] = low[rows]
    for place, block_t in ((x, cot_own[...]), *((place, block[...].T) for place, block in blocks)):
        store_halves(cot_t, block_t, place * (WIDTH // 2), core)
    weight_terms(
        0, 1 - core, act_t, far_t, near_t, cot_t, gq, grad_key, grad_value, att, send_out, dw_s
    )


def keep_kernel(act_t, far_t, near_t, cot_t, gq, grad_key, grad_value, att, keep_out, dw_s):
    core = places()[0]
    weight_terms(
        1, core, act_t, far_t, near_t, cot_t, gq, grad_key, grad_value, att, keep_out, dw_s
    )


def share_kernel(count, *refs):
    terms, outs = refs[:count], refs[count:]
    size = outs[0].shape[0]
    for place, out in enumerate(outs):
        part = slice(size * place, size * (place + 1))
        total = terms[0][part].astype(F32)
        for term in terms[1:]:
            total += term[part].astype(F32)
        out[...] = total.astype(out.dtype)


def input_kernel(gq, own, near, far, wq, wk, wv, out_kept, out_got, keep, send):
    core, _, _, x = places()
    grads = []
    for part in range(2):
        from_near = near[128 + 16 * part : 144 + 16 * part].reshape(ROW, WIDTH)
        grads.append((own[part] + from_near.astype(F32) + far[part].astype(F32)).astype(BF))
    grad_key, grad_value = grads
    first, second = (mp_partner(core, x, step) for step in range(2))
    for out, targets in ((keep, (x, first)), (send, (second, x ^ 2))):
        for place, target in enumerate(targets):
            block = pl.ds(pl.multiple_of(target * WIDTH, WIDTH), WIDTH)
            out[place] = (
                mm(gq[...], wq[block, :], NT)
                + mm(grad_key, wk[block, :], NT)
                + mm(grad_value, wv[block, :], NT)
            ).astype(out.dtype)
    for place, out in ((0, keep), (1, send)):
        out[2] = (out_kept[place] + out_got[place].astype(F32)).astype(out.dtype)


def mp_share_kernel(kept, got, out, keep, send):
    out[...] = (kept[2] + got[2].astype(F32)).astype(BF)
    keep[...] = kept[0] + got[0].astype(F32)
    send[...] = (kept[1] + got[1].astype(F32)).astype(BF)


def mp_sum_kernel(kept, got, grad):
    grad[...] = (kept[...] + got[...].astype(F32)).astype(BF)


def last_sum_kernel(after, kept, got, dw):
    dw[...] = kept[...] + got[...].astype(F32)


def on_chip(*arrays):
    return [pltpu.with_memory_space_constraint(a, pltpu.VMEM) for a in arrays]


def call(
    kernel, name, outs, arrays, apart=(), scratch=(), limit=16, flops=0, moved=1_000_000, apart_outs=0
):
    kept = [jax.ShapeDtypeStruct(shape, dtype) for shape, dtype in outs[:apart_outs]]
    kept += [pltpu.VMEM(shape, dtype) for shape, dtype in outs[apart_outs:]]
    return pl.pallas_call(
        kernel,
        out_shape=tuple(kept),
        in_specs=[pl.BlockSpec(memory_space=pltpu.HBM)] * len(apart)
        + [pl.BlockSpec(memory_space=pltpu.VMEM)] * len(arrays),
        out_specs=(pl.BlockSpec(memory_space=pltpu.VMEM),) * len(kept),
        scratch_shapes=list(scratch),
        compiler_params=pltpu.CompilerParams(vmem_limit_bytes=limit * 1024 * 1024),
        cost_estimate=pl.CostEstimate(flops=flops, bytes_accessed=moved, transcendentals=0),
        name=name,
    )(*[pltpu.with_memory_space_constraint(a, pltpu.HBM) for a in apart], *on_chip(*arrays))


def move(value, axis, target):
    count = lax.axis_size(axis)
    return lax.ppermute(
        value, axis, [(i, target(i)) for i in range(count) if 0 <= target(i) < count]
    )


def over_mp(value, step):
    def target(i):
        return i // 4 * 4 + mp_partner(i // 4 % 2, i % 4, step)

    return move(value, SPACE + ("mp",), target)


def near_row(value):
    return move(value, SPACE, lambda i: i ^ 1)


def far_row(value):
    def target(i):
        row, x = i // 4, i % 4
        if row in (0, 63):
            return row * 4 + (x ^ 1)
        return (row + 1 if row % 2 else row - 1) * 4 + x

    return move(value, SPACE + ("mp",), target)


def body(activations, w_query, w_key, w_value, w_out, grad_output, neighbours, pad_mask):
    act_far = far_row(activations)
    cots = [move(grad_output, "mp", lambda i, step=step: i ^ step) for step in (2, 1, 3)]
    act_near = near_row(activations)

    square = (ROW, WIDTH)
    stacked = (HEADS * ROW, WIDTH)
    wq, wk, wv, wo, query, keys, values, exps, peaks, act_t, near_t, grad_own, cot_own, bias = call(
        own_kernel,
        "own_part",
        [((D, WIDTH), BF)] * 3
        + [((WIDTH, D), BF), (stacked, BF), ((2 * ROW, WIDTH), BF), ((2 * ROW, WIDTH), BF)]
        + [((HEADS, 2 * ROW, ROW), F32), ((2 * HEADS, ROW), F32)]
        + [((D, ROW), BF), ((D, ROW), BF), (square, F32), (square, BF), ((16, ROW), F32)],
        [act_near],
        apart=(activations, w_query, w_key, w_value, w_out, grad_output, neighbours, pad_mask),
        scratch=[
            pltpu.VMEM((ROW, D), BF),
            pltpu.VMEM(square, BF),
            pltpu.SMEM((4, 9), jnp.int32),
            pltpu.SMEM((4, 9), jnp.int32),
            pltpu.SemaphoreType.DMA((8,)),
        ],
        flops=600_000_000,
        moved=6_000_000,
    )

    block = (16, WIDTH)
    pair = (2, ROW, WIDTH)
    keys, values, probs, att, far_t, out_keep, out_send = call(
        forward_kernel,
        "forward",
        [((KEYS, WIDTH), BF)] * 2
        + [((KEYS, HEADS * ROW), BF), (square, BF), ((D, ROW), BF), (pair, F32), (pair, BF)],
        [act_far, wk, wv, wo, query, keys, values, exps, peaks, bias],
        scratch=[pltpu.VMEM((HEADS * ROW, KEYS), BF)],
        limit=20,
        flops=2_000_000_000,
        moved=6_000_000,
    )
    out_got = over_mp(out_send, 0)
    gq, far, own, grad_key, grad_value, cot_t, dw_send = call(
        backward_kernel,
        "backward",
        [
            (square, BF),
            ((2, ROW, WIDTH), BF),
            ((2, ROW, WIDTH), F32),
            ((KEYS, WIDTH), BF),
            ((KEYS, WIDTH), BF),
            ((D, ROW), BF),
            ((160,) + block, BF),
        ],
        [keys, values, probs, att, far_t, near_t, wo, query, act_t, grad_own, cot_own, *cots],
        scratch=[
            pltpu.VMEM(stacked, BF),
            pltpu.VMEM((KEYS, HEADS * ROW), BF),
            pltpu.VMEM((HEADS * ROW, KEYS), BF),
            pltpu.VMEM((4, D // 2, WIDTH), F32),
        ],
        limit=24,
        flops=2_000_000_000,
        moved=8_000_000,
    )
    (dw_keep,) = call(
        keep_kernel,
        "keep_terms",
        [((128,) + block, BF)],
        [act_t, far_t, near_t, cot_t, gq, grad_key, grad_value, att],
        scratch=[pltpu.VMEM((4, D // 2, WIDTH), F32)],
        flops=1_000_000_000,
        moved=4_000_000,
    )

    def share(name, terms, ways, kept_as, flops=0):
        part = (terms[0].shape[0] // ways,) + terms[0].shape[1:]
        outs = [(part, kept_as)] + [(part, BF)] * (ways - 1)
        return call(functools.partial(share_kernel, len(terms)), name, outs, terms, flops=flops)

    def over_chips(value, y_step, z_step):
        def target(i):
            z, y, c = i // 8, i // 2 % 4, i % 2
            y_partners, z_partners = PARTNERS[c]
            y = y if y_step is None else y_partners[y_step](y)
            z = z if z_step is None else z_partners[z_step](z)
            return z * 8 + y * 2 + c

        return move(value, SPACE, target)

    def four_ways(parts, step):
        along_z, along_y = over_chips(parts[1], None, step), over_chips(parts[2], step, None)
        return [parts[0], over_chips(parts[3], step, step), along_y, along_z]

    from_core = near_row(dw_send)
    grad_far = far_row(far)
    parts = four_ways(share("core_sum", [dw_keep, from_core], 4, BF), 0)

    mp_keep, mp_send = call(
        input_kernel,
        "input_grad",
        [((3, ROW, WIDTH), F32), ((3, ROW, WIDTH), BF)],
        [gq, own, from_core, grad_far, wq, wk, wv, out_keep, out_got],
        flops=540_000_000,
        moved=4_000_000,
    )
    output, mp_keep, mp_send = call(
        mp_share_kernel,
        "mp_share",
        [(square, BF), (square, F32), (square, BF)],
        [mp_keep, over_mp(mp_send, 1)],
        apart_outs=1,
    )
    parts = four_ways(share("first_sum", parts, 4, F32, FIRST_FLOPS), 1)
    keep, send = share("second_sum", parts, 2, F32, SECOND_FLOPS)
    got = over_chips(send, None, 2)
    (grad_input,) = call(
        mp_sum_kernel, "mp_sum", [(square, BF)], [mp_keep, over_mp(mp_send, 0)], apart_outs=1
    )
    (dw,) = call(last_sum_kernel, "last_sum", [((4,) + block, F32)], [keep, got], apart=(grad_input,), apart_outs=1)
    return output, grad_input, dw


def solution(mesh):
    fine = Mesh(mesh.devices.reshape(8, 4, 2, 4), SPACE + ("mp",))
    in_specs = (
        P(SPACE, None),
        P(None, "mp"),
        P(None, "mp"),
        P(None, "mp"),
        P("mp", None),
        P(SPACE, "mp"),
        P(SPACE, None),
        P(SPACE, None),
    )
    out_specs = (P(SPACE, "mp"), P(SPACE, "mp"), P(None, SPACE, "mp"))
    return jax.shard_map(body, mesh=fine, in_specs=in_specs, out_specs=out_specs, check_vma=False)
```

```python
import functools

import jax
import jax.numpy as jnp
from jax import lax
from jax.experimental import pallas as pl
from jax.experimental.pallas import tpu as pltpu
from jax.sharding import Mesh
from jax.sharding import PartitionSpec as P

HD = 64
PATCH = 64
D = 1024
ROW = 256
WIDTH = 256
HEADS = WIDTH // HD
FIRST_FLOPS, SECOND_FLOPS = 4_000_000_000, 4_000_000_000
KEYS = 3 * ROW
LOG2E = 1.4426950408889634
BF = jnp.bfloat16
F32 = jnp.float32
SPACE = ("z", "y", "core")

NN = (((1,), (0,)), ((), ()))
NT = (((1,), (1,)), ((), ()))


def mm(a, b, dims=NN):
    return lax.dot_general(a, b, dims, preferred_element_type=F32)


def places():
    return [lax.axis_index(a) for a in ("core", "y", "z", "mp")]


def slot_bias(nb, mask, core, y, z):
    row = (z * 4 + y) * 2 + core
    sign = 1 - 2 * core
    patch_of_lane = lax.broadcasted_iota(jnp.int32, (16, ROW), 1) // PATCH
    patch_of_row = lax.broadcasted_iota(jnp.int32, (16, ROW), 0)
    count = jnp.zeros((16, ROW), F32)
    for slot in range(9):
        named = jnp.zeros((16, ROW), jnp.int32)
        for patch in range(4):
            number = nb[patch, slot]
            band = 1 + sign * (lax.div(number, 4) - row)
            place = jnp.where(mask[patch, slot] > 0, band * 4 + lax.rem(number, 4), -1)
            named = jnp.where(patch_of_lane == patch, place, named)
        count += jnp.where(named == patch_of_row, 1.0, 0.0)
    return jnp.where(count > 0, jnp.where(count > 1, jnp.log(count) * LOG2E, 0.0), -1e30)


def y_pair(y):
    return y + 1 - 2 * (y % 2)


def y_other(y):
    return 3 - y


def z_pair(z):
    return z + 1 - 2 * (z % 2)


def z_other(z):
    return (z + 7 + 2 * (z % 2)) % 8


def z_far(z):
    middle = (z % 4) * (3 - z % 4) // 2
    return (1 - middle) * (3 - 2 * (z % 4) + z) + middle * (7 - z)


def z_far_too(z):
    return z + 4 + (1 - 2 * (z % 2)) - 8 * (z // 4)


def target_rows(z, y, y_partners, z_partners):
    def reached(start, partners):
        places = [start]
        for partner in partners:
            places = [there for here in places for there in (here, partner(here))]
        return places

    ys, zs = reached(y, y_partners), reached(z, z_partners)
    rows = []
    for number in range(32):
        y1, z1, y2, z2, z3 = ((number >> (4 - bit)) & 1 for bit in range(5))
        rows.append(zs[4 * z1 + 2 * z2 + z3] * 4 + ys[2 * y1 + y2])
    return rows


PARTNERS = (
    ((y_other, y_pair), (z_pair, z_other, z_far)),
    ((y_pair, y_other), (z_other, z_pair, z_far_too)),
)


def mp_partner(core, x, step):
    near, across = x ^ 1, 3 - x
    if isinstance(core, int):
        return (near, across)[(core + step) % 2]
    return jnp.where(core == step, near, across)


def columns(ref, place):
    return ref[:, pl.ds(pl.multiple_of(place * WIDTH, WIDTH), WIDTH)]


def head_lanes():
    return lax.broadcasted_iota(jnp.int32, (ROW, WIDTH), 1) // HD


def stack_heads(rows, out):
    for head in range(HEADS):
        out[head * ROW : (head + 1) * ROW, :] = jnp.where(head_lanes() == head, rows, jnp.zeros_like(rows))


def pick_heads(stacked):
    total = jnp.zeros((ROW, WIDTH), F32)
    for head in range(HEADS):
        total = jnp.where(head_lanes() == head, stacked[head * ROW : (head + 1) * ROW], total)
    return total.astype(BF)


def store_halves(out, rows, start, core):
    for block in range(rows.shape[0] // 32):
        for c in range(2):
            half = jnp.where(core == c, D // 2, 0)
            there = pl.ds(pl.multiple_of(half + start + 16 * block, 16), 16)
            out[there, :] = rows[32 * block + 16 * c : 32 * block + 16 * (c + 1)]


def spread_bias(bias, patches):
    return jnp.concatenate(
        [jnp.broadcast_to(bias[patch : patch + 1, :], (PATCH, ROW)) for patch in patches], axis=0
    )


def own_kernel(
    act, w_q, w_k, w_v, w_o, cot, slots, live, a_near,
    wq, wk, wv, wo, query_out, keys_out, values_out, exps_out, peaks_out, act_t, near_t, grad_out, cot_t, bias_out,
    act_s, cot_s, nb, mask, sems,
):
    core, y, z, x = places()
    pairs = (
        (slots, nb), (live, mask), (act, act_s), (w_k, wk), (w_v, wv), (w_q, wq), (cot, cot_s), (w_o, wo)
    )
    copies = [pltpu.make_async_copy(a, b, sems.at[i]) for i, (a, b) in enumerate(pairs)]
    for copy in copies:
        copy.start()
    store_halves(near_t, a_near[...].T, 0, core)
    copies[0].wait()
    copies[1].wait()
    bias = slot_bias(nb, mask, core, y, z)
    bias_out[...] = bias
    copies[2].wait()
    store_halves(act_t, act_s[...].T, 0, core)
    for index, weight, out in ((3, wk, keys_out), (4, wv, values_out)):
        copies[index].wait()
        out[:ROW, :] = mm(act_s[...], weight[...]).astype(BF)
        out[ROW:, :] = mm(a_near[...], weight[...]).astype(BF)
    copies[5].wait()
    stack_heads(mm(act_s[...], wq[...]).astype(BF), query_out)
    bias_rows = spread_bias(bias, range(4, 12))
    for head in range(HEADS):
        scores = mm(keys_out[...], query_out[head * ROW : (head + 1) * ROW, :], NT)
        scores = scores * (LOG2E * HD**-0.5) + bias_rows
        peak = jnp.max(scores, axis=0, keepdims=True)
        exps = jnp.exp2(scores - peak)
        exps_out[head] = exps
        peaks_out[head : head + 1, :] = peak
        peaks_out[HEADS + head : HEADS + head + 1, :] = jnp.sum(exps, axis=0, keepdims=True)
    copies[6].wait()
    cot_t[...] = cot_s[...].T
    copies[7].wait()
    grad_out[...] = mm(cot_s[...], columns(wo, x), NT)


def forward_kernel(
    a_far, wk, wv, query, keys_in, values_in, exps, peaks, bias,
    keys, values, probs_out, att_out, far_t,
    probs_t,
):
    core = places()[0]
    keys[ROW:, :] = keys_in[...]
    values[ROW:, :] = values_in[...]
    keys[:ROW, :] = mm(a_far[...], wk[...]).astype(BF)
    values[:ROW, :] = mm(a_far[...], wv[...]).astype(BF)
    bias_rows = spread_bias(bias, range(4))
    for head in range(HEADS):
        part = slice(head * ROW, (head + 1) * ROW)
        scores = mm(keys[:ROW, :], query[part, :], NT) * (LOG2E * HD**-0.5) + bias_rows
        peak_before = peaks[head : head + 1, :]
        peak = jnp.maximum(peak_before, jnp.max(scores, axis=0, keepdims=True))
        weights = jnp.exp2(scores - peak)
        before = jnp.exp2(peak_before - peak)
        total = before * peaks[HEADS + head : HEADS + head + 1, :] + jnp.sum(weights, axis=0, keepdims=True)
        scale = 1.0 / total
        far_probs = (weights * scale).astype(BF)
        other_probs = (exps[head] * (before * scale)).astype(BF)
        probs_out[:ROW, part] = far_probs
        probs_out[ROW:, part] = other_probs
        probs_t[part, :ROW] = far_probs.T
        probs_t[part, ROW:] = other_probs.T
    att_out[...] = pick_heads(mm(probs_t[...], values[...]))
    store_halves(far_t, a_far[...].T, 0, core)


def weight_terms(half, partners, act_t, far_t, near_t, cot_t, gq, grad_key, grad_value, att, out, dw_s):
    rows = slice(half * (D // 2), (half + 1) * (D // 2))
    dw_s[0] = mm(act_t[rows, :], gq[...])
    for index, grad in ((1, grad_key), (2, grad_value)):
        dw_s[index] = (
            mm(act_t[rows, :], grad[ROW : 2 * ROW, :])
            + mm(far_t[rows, :], grad[:ROW, :])
            + mm(near_t[rows, :], grad[2 * ROW :, :])
        )
    dw_s[3] = mm(cot_t[rows, :], att[...])
    core, y, z, _ = places()
    tables = [target_rows(z, y, *pair) for pair in PARTNERS]
    for number in range(32):
        zero, one = (table[number] * 16 for table in tables)
        row = pl.multiple_of(jnp.where(partners == 0, zero, one), 16)
        out[4 * number : 4 * number + 4] = dw_s[:, pl.ds(row, 16), :].astype(BF)


def backward_kernel(
    keys, values, probs_in, att, far_t, near_t, wo, query, act_t, grad_in, cot_own, c2, c1, c3,
    gq, far_out, own_out, grad_key, grad_value, cot_t, send_out,
    grad_s, scores_s, scores_t, dw_s,
):
    core, y, z, x = places()
    grad_att = grad_in[...]
    blocks = ((x ^ 2, c2), (x ^ 1, c1), (x ^ 3, c3))
    for place, block in blocks:
        grad_att += mm(block[...], columns(wo, place), NT)
    stack_heads(grad_att.astype(BF), grad_s)
    for head in range(HEADS):
        part = slice(head * ROW, (head + 1) * ROW)
        probs = probs_in[:, part].astype(F32)
        grad_probs = mm(values[...], grad_s[part, :], NT)
        centre = jnp.sum(probs * grad_probs, axis=0, keepdims=True)
        grad_scores = (probs * ((grad_probs - centre) * HD**-0.5)).astype(BF)
        scores_s[:, part] = grad_scores
        scores_t[part, :] = grad_scores.T
    gq[...] = pick_heads(mm(scores_t[...], keys[...]))
    for index, (grad, out) in enumerate(
        ((mm(scores_s[...], query[...]), grad_key), (mm(probs_in[...], grad_s[...]), grad_value))
    ):
        low = grad.astype(BF)
        out[...] = low
        far_out[index] = low[:ROW]
        own_out[index] = grad[ROW : 2 * ROW]
        for block in range(16):
            rows = slice(2 * ROW + 16 * block, 2 * ROW + 16 * (block + 1))
            send_out[128 + 16 * index + block] = low[rows]
    for place, block_t in ((x, cot_own[...]), *((place, block[...].T) for place, block in blocks)):
        store_halves(cot_t, block_t, place * (WIDTH // 2), core)
    weight_terms(
        0, 1 - core, act_t, far_t, near_t, cot_t, gq, grad_key, grad_value, att, send_out, dw_s
    )


def keep_kernel(far, act_t, far_t, near_t, cot_t, gq, grad_key, grad_value, att, far_out, keep_out, dw_s):
    core = places()[0]
    weight_terms(
        1, core, act_t, far_t, near_t, cot_t, gq, grad_key, grad_value, att, keep_out, dw_s
    )


def share_kernel(count, *refs):
    terms, outs = refs[:count], refs[count:]
    size = outs[0].shape[0]
    for place, out in enumerate(outs):
        part = slice(size * place, size * (place + 1))
        total = terms[0][part].astype(F32)
        for term in terms[1:]:
            total += term[part].astype(F32)
        out[...] = total.astype(out.dtype)


def input_kernel(att, gq, own, near, far, wq, wk, wv, wo, keep, send):
    core, _, _, x = places()
    grads = []
    for part in range(2):
        from_near = near[128 + 16 * part : 144 + 16 * part].reshape(ROW, WIDTH)
        grads.append((own[part] + from_near.astype(F32) + far[part].astype(F32)).astype(BF))
    grad_key, grad_value = grads
    first, second = (mp_partner(core, x, step) for step in range(2))
    for out, targets in ((keep, (x, second)), (send, (first, x ^ 2))):
        for place, target in enumerate(targets):
            block = pl.ds(pl.multiple_of(target * WIDTH, WIDTH), WIDTH)
            out[2 * place] = mm(att[...], wo[:, block]).astype(out.dtype)
            out[2 * place + 1] = (
                mm(gq[...], wq[block, :], NT)
                + mm(grad_key, wk[block, :], NT)
                + mm(grad_value, wv[block, :], NT)
            ).astype(out.dtype)


def mp_sum_kernel(kept, got, out, grad):
    for part, ref in ((0, out), (1, grad)):
        ref[...] = (kept[part] + got[part].astype(F32)).astype(BF)


def last_sum_kernel(after, kept, got, dw):
    dw[...] = kept[...] + got[...].astype(F32)


def on_chip(*arrays):
    return [pltpu.with_memory_space_constraint(a, pltpu.VMEM) for a in arrays]


def call(
    kernel, name, outs, arrays, apart=(), scratch=(), limit=16, flops=0, moved=1_000_000, keep=True,
    aliases=(),
):
    kept = [pltpu.VMEM(shape, dtype) if keep else jax.ShapeDtypeStruct(shape, dtype) for shape, dtype in outs]
    return pl.pallas_call(
        kernel,
        out_shape=tuple(kept),
        in_specs=[pl.BlockSpec(memory_space=pltpu.HBM)] * len(apart)
        + [pl.BlockSpec(memory_space=pltpu.VMEM)] * len(arrays),
        out_specs=(pl.BlockSpec(memory_space=pltpu.VMEM),) * len(kept),
        scratch_shapes=list(scratch),
        input_output_aliases=dict(aliases),
        compiler_params=pltpu.CompilerParams(vmem_limit_bytes=limit * 1024 * 1024),
        cost_estimate=pl.CostEstimate(flops=flops, bytes_accessed=moved, transcendentals=0),
        name=name,
    )(*[pltpu.with_memory_space_constraint(a, pltpu.HBM) for a in apart], *on_chip(*arrays))


def move(value, axis, target):
    count = lax.axis_size(axis)
    return lax.ppermute(
        value, axis, [(i, target(i)) for i in range(count) if 0 <= target(i) < count]
    )


def over_mp(value, step):
    def target(i):
        return i // 4 * 4 + mp_partner(i // 4 % 2, i % 4, step)

    return move(value, SPACE + ("mp",), target)


def near_row(value):
    return move(value, SPACE, lambda i: i ^ 1)


def far_row(value):
    def target(i):
        row, x = i // 4, i % 4
        if row in (0, 63):
            return row * 4 + (x ^ 1)
        return (row + 1 if row % 2 else row - 1) * 4 + x

    return move(value, SPACE + ("mp",), target)


def body(activations, w_query, w_key, w_value, w_out, grad_output, neighbours, pad_mask):
    act_far = far_row(activations)
    cots = [move(grad_output, "mp", lambda i, step=step: i ^ step) for step in (2, 1, 3)]
    act_near = near_row(activations)

    square = (ROW, WIDTH)
    stacked = (HEADS * ROW, WIDTH)
    wq, wk, wv, wo, query, keys, values, exps, peaks, act_t, near_t, grad_own, cot_own, bias = call(
        own_kernel,
        "own_part",
        [((D, WIDTH), BF)] * 3
        + [((WIDTH, D), BF), (stacked, BF), ((2 * ROW, WIDTH), BF), ((2 * ROW, WIDTH), BF)]
        + [((HEADS, 2 * ROW, ROW), F32), ((2 * HEADS, ROW), F32)]
        + [((D, ROW), BF), ((D, ROW), BF), (square, F32), (square, BF), ((16, ROW), F32)],
        [act_near],
        apart=(activations, w_query, w_key, w_value, w_out, grad_output, neighbours, pad_mask),
        scratch=[
            pltpu.VMEM((ROW, D), BF),
            pltpu.VMEM(square, BF),
            pltpu.SMEM((4, 9), jnp.int32),
            pltpu.SMEM((4, 9), jnp.int32),
            pltpu.SemaphoreType.DMA((8,)),
        ],
        flops=600_000_000,
        moved=6_000_000,
    )

    block = (16, WIDTH)
    keys, values, probs, att, far_t = call(
        forward_kernel,
        "forward",
        [((KEYS, WIDTH), BF)] * 2 + [((KEYS, HEADS * ROW), BF), (square, BF), ((D, ROW), BF)],
        [act_far, wk, wv, query, keys, values, exps, peaks, bias],
        scratch=[pltpu.VMEM((HEADS * ROW, KEYS), BF)],
        limit=20,
        flops=2_000_000_000,
        moved=6_000_000,
    )
    gq, far, own, grad_key, grad_value, cot_t, dw_send = call(
        backward_kernel,
        "backward",
        [
            (square, BF),
            ((2, ROW, WIDTH), BF),
            ((2, ROW, WIDTH), F32),
            ((KEYS, WIDTH), BF),
            ((KEYS, WIDTH), BF),
            ((D, ROW), BF),
            ((160,) + block, BF),
        ],
        [keys, values, probs, att, far_t, near_t, wo, query, act_t, grad_own, cot_own, *cots],
        scratch=[
            pltpu.VMEM(stacked, BF),
            pltpu.VMEM((KEYS, HEADS * ROW), BF),
            pltpu.VMEM((HEADS * ROW, KEYS), BF),
            pltpu.VMEM((4, D // 2, WIDTH), F32),
        ],
        limit=24,
        flops=2_000_000_000,
        moved=8_000_000,
    )
    far, dw_keep = call(
        keep_kernel,
        "keep_terms",
        [((2, ROW, WIDTH), BF), ((128,) + block, BF)],
        [far, act_t, far_t, near_t, cot_t, gq, grad_key, grad_value, att],
        scratch=[pltpu.VMEM((4, D // 2, WIDTH), F32)],
        flops=1_000_000_000,
        moved=4_000_000,
        aliases={0: 0},
    )

    def share(name, terms, ways, kept_as, flops=0):
        part = (terms[0].shape[0] // ways,) + terms[0].shape[1:]
        outs = [(part, kept_as)] + [(part, BF)] * (ways - 1)
        return call(functools.partial(share_kernel, len(terms)), name, outs, terms, flops=flops)

    def over_chips(value, y_step, z_step):
        def target(i):
            z, y, c = i // 8, i // 2 % 4, i % 2
            y_partners, z_partners = PARTNERS[c]
            y = y if y_step is None else y_partners[y_step](y)
            z = z if z_step is None else z_partners[z_step](z)
            return z * 8 + y * 2 + c

        return move(value, SPACE, target)

    def four_ways(parts, step):
        along_z, along_y = over_chips(parts[1], None, step), over_chips(parts[2], step, None)
        return [parts[0], over_chips(parts[3], step, step), along_y, along_z]

    from_core = near_row(dw_send)
    grad_far = far_row(far)
    parts = four_ways(share("core_sum", [dw_keep, from_core], 4, BF), 0)

    mp_keep, mp_send = call(
        input_kernel,
        "input_grad",
        [((4, ROW, WIDTH), F32), ((4, ROW, WIDTH), BF)],
        [att, gq, own, from_core, grad_far, wq, wk, wv, wo],
        flops=540_000_000,
        moved=4_000_000,
    )
    mp_keep, mp_send = share("mp_share", [mp_keep, over_mp(mp_send, 0)], 2, F32)
    parts = four_ways(share("first_sum", parts, 4, F32, FIRST_FLOPS), 1)
    keep, send = share("second_sum", parts, 2, F32, SECOND_FLOPS)
    got = over_chips(send, None, 2)
    output, grad_input = call(
        mp_sum_kernel, "mp_sum", [(square, BF)] * 2, [mp_keep, over_mp(mp_send, 1)], keep=False
    )
    (dw,) = call(last_sum_kernel, "last_sum", [((4,) + block, F32)], [keep, got], apart=(output,), keep=False)
    return output, grad_input, dw


def solution(mesh):
    fine = Mesh(mesh.devices.reshape(8, 4, 2, 4), SPACE + ("mp",))
    in_specs = (
        P(SPACE, None),
        P(None, "mp"),
        P(None, "mp"),
        P(None, "mp"),
        P("mp", None),
        P(SPACE, "mp"),
        P(SPACE, None),
        P(SPACE, None),
    )
    out_specs = (P(SPACE, "mp"), P(SPACE, "mp"), P(None, SPACE, "mp"))
    return jax.shard_map(body, mesh=fine, in_specs=in_specs, out_specs=out_specs, check_vma=False)
```

```python
import functools

import jax
import jax.numpy as jnp
from jax import lax
from jax.experimental import pallas as pl
from jax.experimental.pallas import tpu as pltpu
from jax.sharding import Mesh
from jax.sharding import PartitionSpec as P

HD = 64
PATCH = 64
D = 1024
ROW = 256
WIDTH = 256
HEADS = WIDTH // HD
FIRST_FLOPS, SECOND_FLOPS = 4_000_000_000, 4_000_000_000
KEYS = 3 * ROW
LOG2E = 1.4426950408889634
BF = jnp.bfloat16
F32 = jnp.float32
SPACE = ("z", "y", "core")

NN = (((1,), (0,)), ((), ()))
NT = (((1,), (1,)), ((), ()))


def mm(a, b, dims=NN):
    return lax.dot_general(a, b, dims, preferred_element_type=F32)


def places():
    return [lax.axis_index(a) for a in ("core", "y", "z", "mp")]


def slot_bias(nb, mask, core, y, z):
    row = (z * 4 + y) * 2 + core
    sign = 1 - 2 * core
    patch_of_lane = lax.broadcasted_iota(jnp.int32, (16, ROW), 1) // PATCH
    patch_of_row = lax.broadcasted_iota(jnp.int32, (16, ROW), 0)
    count = jnp.zeros((16, ROW), F32)
    for slot in range(9):
        named = jnp.zeros((16, ROW), jnp.int32)
        for patch in range(4):
            number = nb[patch, slot]
            band = 1 + sign * ((number >> 2) - row)
            place = jnp.where(mask[patch, slot] > 0, band * 4 + (number & 3), -1)
            named = jnp.where(patch_of_lane == patch, place, named)
        count += jnp.where(named == patch_of_row, 1.0, 0.0)
    return jnp.where(count > 0, jnp.where(count > 1, jnp.log(count) * LOG2E, 0.0), -1e30)


def y_pair(y):
    return y ^ 1


def y_other(y):
    return y ^ 3


def z_pair(z):
    return z ^ 1


def z_other(z):
    return (z + 2 * (z & 1) + 7) & 7


def z_far(z):
    return z ^ (3 + 4 * ((z ^ (z >> 1)) & 1))


def z_far_too(z):
    return z ^ 5


def target_rows(z, y, y_partners, z_partners):
    def reached(start, partners):
        places = [start]
        for partner in partners:
            places = [there for here in places for there in (here, partner(here))]
        return places

    ys, zs = reached(y, y_partners), reached(z, z_partners)
    rows = []
    for number in range(32):
        y1, z1, y2, z2, z3 = ((number >> (4 - bit)) & 1 for bit in range(5))
        rows.append(zs[4 * z1 + 2 * z2 + z3] * 4 + ys[2 * y1 + y2])
    return rows


PARTNERS = (
    ((y_other, y_pair), (z_pair, z_other, z_far)),
    ((y_pair, y_other), (z_other, z_pair, z_far_too)),
)


def mp_partner(core, x, step):
    near, across = x ^ 1, 3 - x
    if isinstance(core, int):
        return (near, across)[(core + step) % 2]
    return jnp.where(core == step, near, across)


def columns(ref, place):
    return ref[:, pl.ds(pl.multiple_of(place * WIDTH, WIDTH), WIDTH)]


def head_lanes():
    return lax.broadcasted_iota(jnp.int32, (ROW, WIDTH), 1) // HD


def stack_heads(rows, out):
    for head in range(HEADS):
        out[head * ROW : (head + 1) * ROW, :] = jnp.where(head_lanes() == head, rows, jnp.zeros_like(rows))


def pick_heads(stacked):
    total = jnp.zeros((ROW, WIDTH), F32)
    for head in range(HEADS):
        total = jnp.where(head_lanes() == head, stacked[head * ROW : (head + 1) * ROW], total)
    return total.astype(BF)


def store_halves(out, rows, start, core):
    for block in range(rows.shape[0] // 32):
        for c in range(2):
            half = jnp.where(core == c, D // 2, 0)
            there = pl.ds(pl.multiple_of(half + start + 16 * block, 16), 16)
            out[there, :] = rows[32 * block + 16 * c : 32 * block + 16 * (c + 1)]


def spread_bias(bias, patches):
    return jnp.concatenate(
        [jnp.broadcast_to(bias[patch : patch + 1, :], (PATCH, ROW)) for patch in patches], axis=0
    )


def own_kernel(
    act, w_q, w_k, w_v, w_o, cot, slots, live, a_near,
    wq, wk, wv, wo, query_out, keys_out, values_out, exps_out, peaks_out, act_t, near_t, grad_out, cot_t, bias_out,
    act_s, cot_s, nb, mask, sems,
):
    core, y, z, x = places()
    pairs = (
        (slots, nb), (live, mask), (act, act_s), (w_k, wk), (w_v, wv), (w_q, wq), (cot, cot_s), (w_o, wo)
    )
    copies = [pltpu.make_async_copy(a, b, sems.at[i]) for i, (a, b) in enumerate(pairs)]
    for copy in copies:
        copy.start()
    store_halves(near_t, a_near[...].T, 0, core)
    copies[0].wait()
    copies[1].wait()
    bias = slot_bias(nb, mask, core, y, z)
    bias_out[...] = bias
    copies[2].wait()
    store_halves(act_t, act_s[...].T, 0, core)
    for index, weight, out in ((3, wk, keys_out), (4, wv, values_out)):
        copies[index].wait()
        out[:ROW, :] = mm(act_s[...], weight[...]).astype(BF)
        out[ROW:, :] = mm(a_near[...], weight[...]).astype(BF)
    copies[5].wait()
    stack_heads(mm(act_s[...], wq[...]).astype(BF), query_out)
    bias_rows = spread_bias(bias, range(4, 12))
    for head in range(HEADS):
        scores = mm(keys_out[...], query_out[head * ROW : (head + 1) * ROW, :], NT)
        scores = scores * (LOG2E * HD**-0.5) + bias_rows
        peak = jnp.max(scores, axis=0, keepdims=True)
        exps = jnp.exp2(scores - peak)
        exps_out[head] = exps
        peaks_out[head : head + 1, :] = peak
        peaks_out[HEADS + head : HEADS + head + 1, :] = jnp.sum(exps, axis=0, keepdims=True)
    copies[6].wait()
    cot_t[...] = cot_s[...].T
    copies[7].wait()
    grad_out[...] = mm(cot_s[...], columns(wo, x), NT)


def forward_kernel(
    a_far, wk, wv, query, keys_in, values_in, exps, peaks, bias,
    keys, values, probs_out, att_out, far_t,
    probs_t,
):
    core = places()[0]
    keys[ROW:, :] = keys_in[...]
    values[ROW:, :] = values_in[...]
    keys[:ROW, :] = mm(a_far[...], wk[...]).astype(BF)
    values[:ROW, :] = mm(a_far[...], wv[...]).astype(BF)
    bias_rows = spread_bias(bias, range(4))
    for head in range(HEADS):
        part = slice(head * ROW, (head + 1) * ROW)
        scores = mm(keys[:ROW, :], query[part, :], NT) * (LOG2E * HD**-0.5) + bias_rows
        peak_before = peaks[head : head + 1, :]
        peak = jnp.maximum(peak_before, jnp.max(scores, axis=0, keepdims=True))
        weights = jnp.exp2(scores - peak)
        before = jnp.exp2(peak_before - peak)
        total = before * peaks[HEADS + head : HEADS + head + 1, :] + jnp.sum(weights, axis=0, keepdims=True)
        scale = 1.0 / total
        far_probs = (weights * scale).astype(BF)
        other_probs = (exps[head] * (before * scale)).astype(BF)
        probs_out[:ROW, part] = far_probs
        probs_out[ROW:, part] = other_probs
        probs_t[part, :ROW] = far_probs.T
        probs_t[part, ROW:] = other_probs.T
    att_out[...] = pick_heads(mm(probs_t[...], values[...]))
    store_halves(far_t, a_far[...].T, 0, core)


def weight_terms(half, partners, act_t, far_t, near_t, cot_t, gq, grad_key, grad_value, att, out, dw_s):
    rows = slice(half * (D // 2), (half + 1) * (D // 2))
    dw_s[0] = mm(act_t[rows, :], gq[...])
    for index, grad in ((1, grad_key), (2, grad_value)):
        dw_s[index] = (
            mm(act_t[rows, :], grad[ROW : 2 * ROW, :])
            + mm(far_t[rows, :], grad[:ROW, :])
            + mm(near_t[rows, :], grad[2 * ROW :, :])
        )
    dw_s[3] = mm(cot_t[rows, :], att[...])
    core, y, z, _ = places()
    tables = [target_rows(z, y, *pair) for pair in PARTNERS]
    for number in range(32):
        zero, one = (table[number] * 16 for table in tables)
        row = pl.multiple_of(jnp.where(partners == 0, zero, one), 16)
        out[4 * number : 4 * number + 4] = dw_s[:, pl.ds(row, 16), :].astype(BF)


def backward_kernel(
    keys, values, probs_in, att, far_t, near_t, wo, query, act_t, grad_in, cot_own, c2, c1, c3,
    gq, far_out, own_out, grad_key, grad_value, cot_t, send_out,
    grad_s, scores_s, scores_t, dw_s,
):
    core, y, z, x = places()
    grad_att = grad_in[...]
    blocks = ((x ^ 2, c2), (x ^ 1, c1), (x ^ 3, c3))
    for place, block in blocks:
        grad_att += mm(block[...], columns(wo, place), NT)
    stack_heads(grad_att.astype(BF), grad_s)
    for head in range(HEADS):
        part = slice(head * ROW, (head + 1) * ROW)
        probs = probs_in[:, part].astype(F32)
        grad_probs = mm(values[...], grad_s[part, :], NT)
        centre = jnp.sum(probs * grad_probs, axis=0, keepdims=True)
        grad_scores = (probs * ((grad_probs - centre) * HD**-0.5)).astype(BF)
        scores_s[:, part] = grad_scores
        scores_t[part, :] = grad_scores.T
    gq[...] = pick_heads(mm(scores_t[...], keys[...]))
    for index, (grad, out) in enumerate(
        ((mm(scores_s[...], query[...]), grad_key), (mm(probs_in[...], grad_s[...]), grad_value))
    ):
        low = grad.astype(BF)
        out[...] = low
        far_out[index] = low[:ROW]
        own_out[index] = grad[ROW : 2 * ROW]
        for block in range(16):
            rows = slice(2 * ROW + 16 * block, 2 * ROW + 16 * (block + 1))
            send_out[128 + 16 * index + block] = low[rows]
    for place, block_t in ((x, cot_own[...]), *((place, block[...].T) for place, block in blocks)):
        store_halves(cot_t, block_t, place * (WIDTH // 2), core)
    weight_terms(
        0, 1 - core, act_t, far_t, near_t, cot_t, gq, grad_key, grad_value, att, send_out, dw_s
    )


def keep_kernel(act_t, far_t, near_t, cot_t, gq, grad_key, grad_value, att, keep_out, dw_s):
    core = places()[0]
    weight_terms(
        1, core, act_t, far_t, near_t, cot_t, gq, grad_key, grad_value, att, keep_out, dw_s
    )


def share_kernel(count, *refs):
    terms, outs = refs[:count], refs[count:]
    size = outs[0].shape[0]
    for place, out in enumerate(outs):
        part = slice(size * place, size * (place + 1))
        total = terms[0][part].astype(F32)
        for term in terms[1:]:
            total += term[part].astype(F32)
        out[...] = total.astype(out.dtype)


def input_kernel(att, gq, own, near, far, wq, wk, wv, wo, keep, send):
    core, _, _, x = places()
    grads = []
    for part in range(2):
        from_near = near[128 + 16 * part : 144 + 16 * part].reshape(ROW, WIDTH)
        grads.append((own[part] + from_near.astype(F32) + far[part].astype(F32)).astype(BF))
    grad_key, grad_value = grads
    first, second = (mp_partner(core, x, step) for step in range(2))
    for out, targets in ((keep, (x, second)), (send, (first, x ^ 2))):
        for place, target in enumerate(targets):
            block = pl.ds(pl.multiple_of(target * WIDTH, WIDTH), WIDTH)
            out[2 * place] = mm(att[...], wo[:, block]).astype(out.dtype)
            out[2 * place + 1] = (
                mm(gq[...], wq[block, :], NT)
                + mm(grad_key, wk[block, :], NT)
                + mm(grad_value, wv[block, :], NT)
            ).astype(out.dtype)


def mp_sum_kernel(kept, got, out, grad):
    for part, ref in ((0, out), (1, grad)):
        ref[...] = (kept[part] + got[part].astype(F32)).astype(BF)


def last_sum_kernel(after, kept, got, dw):
    dw[...] = kept[...] + got[...].astype(F32)


def on_chip(*arrays):
    return [pltpu.with_memory_space_constraint(a, pltpu.VMEM) for a in arrays]


def call(
    kernel, name, outs, arrays, apart=(), scratch=(), limit=16, flops=0, moved=1_000_000, keep=True
):
    kept = [pltpu.VMEM(shape, dtype) if keep else jax.ShapeDtypeStruct(shape, dtype) for shape, dtype in outs]
    return pl.pallas_call(
        kernel,
        out_shape=tuple(kept),
        in_specs=[pl.BlockSpec(memory_space=pltpu.HBM)] * len(apart)
        + [pl.BlockSpec(memory_space=pltpu.VMEM)] * len(arrays),
        out_specs=(pl.BlockSpec(memory_space=pltpu.VMEM),) * len(kept),
        scratch_shapes=list(scratch),
        compiler_params=pltpu.CompilerParams(vmem_limit_bytes=limit * 1024 * 1024),
        cost_estimate=pl.CostEstimate(flops=flops, bytes_accessed=moved, transcendentals=0),
        name=name,
    )(*[pltpu.with_memory_space_constraint(a, pltpu.HBM) for a in apart], *on_chip(*arrays))


def move(value, axis, target):
    count = lax.axis_size(axis)
    return lax.ppermute(
        value, axis, [(i, target(i)) for i in range(count) if 0 <= target(i) < count]
    )


def over_mp(value, step):
    def target(i):
        return i // 4 * 4 + mp_partner(i // 4 % 2, i % 4, step)

    return move(value, SPACE + ("mp",), target)


def near_row(value):
    return move(value, SPACE, lambda i: i ^ 1)


def far_row(value):
    def target(i):
        row, x = i // 4, i % 4
        if row in (0, 63):
            return row * 4 + (x ^ 1)
        return (row + 1 if row % 2 else row - 1) * 4 + x

    return move(value, SPACE + ("mp",), target)


def body(activations, w_query, w_key, w_value, w_out, grad_output, neighbours, pad_mask):
    act_far = far_row(activations)
    cots = [move(grad_output, "mp", lambda i, step=step: i ^ step) for step in (2, 1, 3)]
    act_near = near_row(activations)

    square = (ROW, WIDTH)
    stacked = (HEADS * ROW, WIDTH)
    wq, wk, wv, wo, query, keys, values, exps, peaks, act_t, near_t, grad_own, cot_own, bias = call(
        own_kernel,
        "own_part",
        [((D, WIDTH), BF)] * 3
        + [((WIDTH, D), BF), (stacked, BF), ((2 * ROW, WIDTH), BF), ((2 * ROW, WIDTH), BF)]
        + [((HEADS, 2 * ROW, ROW), F32), ((2 * HEADS, ROW), F32)]
        + [((D, ROW), BF), ((D, ROW), BF), (square, F32), (square, BF), ((16, ROW), F32)],
        [act_near],
        apart=(activations, w_query, w_key, w_value, w_out, grad_output, neighbours, pad_mask),
        scratch=[
            pltpu.VMEM((ROW, D), BF),
            pltpu.VMEM(square, BF),
            pltpu.SMEM((4, 9), jnp.int32),
            pltpu.SMEM((4, 9), jnp.int32),
            pltpu.SemaphoreType.DMA((8,)),
        ],
        flops=600_000_000,
        moved=6_000_000,
    )

    block = (16, WIDTH)
    keys, values, probs, att, far_t = call(
        forward_kernel,
        "forward",
        [((KEYS, WIDTH), BF)] * 2 + [((KEYS, HEADS * ROW), BF), (square, BF), ((D, ROW), BF)],
        [act_far, wk, wv, query, keys, values, exps, peaks, bias],
        scratch=[pltpu.VMEM((HEADS * ROW, KEYS), BF)],
        limit=20,
        flops=2_000_000_000,
        moved=6_000_000,
    )
    gq, far, own, grad_key, grad_value, cot_t, dw_send = call(
        backward_kernel,
        "backward",
        [
            (square, BF),
            ((2, ROW, WIDTH), BF),
            ((2, ROW, WIDTH), F32),
            ((KEYS, WIDTH), BF),
            ((KEYS, WIDTH), BF),
            ((D, ROW), BF),
            ((160,) + block, BF),
        ],
        [keys, values, probs, att, far_t, near_t, wo, query, act_t, grad_own, cot_own, *cots],
        scratch=[
            pltpu.VMEM(stacked, BF),
            pltpu.VMEM((KEYS, HEADS * ROW), BF),
            pltpu.VMEM((HEADS * ROW, KEYS), BF),
            pltpu.VMEM((4, D // 2, WIDTH), F32),
        ],
        limit=24,
        flops=2_000_000_000,
        moved=8_000_000,
    )
    (dw_keep,) = call(
        keep_kernel,
        "keep_terms",
        [((128,) + block, BF)],
        [act_t, far_t, near_t, cot_t, gq, grad_key, grad_value, att],
        scratch=[pltpu.VMEM((4, D // 2, WIDTH), F32)],
        flops=1_000_000_000,
        moved=4_000_000,
    )

    def share(name, terms, ways, kept_as, flops=0):
        part = (terms[0].shape[0] // ways,) + terms[0].shape[1:]
        outs = [(part, kept_as)] + [(part, BF)] * (ways - 1)
        return call(functools.partial(share_kernel, len(terms)), name, outs, terms, flops=flops)

    def over_chips(value, y_step, z_step):
        def target(i):
            z, y, c = i // 8, i // 2 % 4, i % 2
            y_partners, z_partners = PARTNERS[c]
            y = y if y_step is None else y_partners[y_step](y)
            z = z if z_step is None else z_partners[z_step](z)
            return z * 8 + y * 2 + c

        return move(value, SPACE, target)

    def four_ways(parts, step):
        along_z, along_y = over_chips(parts[1], None, step), over_chips(parts[2], step, None)
        return [parts[0], over_chips(parts[3], step, step), along_y, along_z]

    from_core = near_row(dw_send)
    grad_far = far_row(far)
    parts = four_ways(share("core_sum", [dw_keep, from_core], 4, BF), 0)

    mp_keep, mp_send = call(
        input_kernel,
        "input_grad",
        [((4, ROW, WIDTH), F32), ((4, ROW, WIDTH), BF)],
        [att, gq, own, from_core, grad_far, wq, wk, wv, wo],
        flops=540_000_000,
        moved=4_000_000,
    )
    mp_keep, mp_send = share("mp_share", [mp_keep, over_mp(mp_send, 0)], 2, F32)
    parts = four_ways(share("first_sum", parts, 4, F32, FIRST_FLOPS), 1)
    keep, send = share("second_sum", parts, 2, F32, SECOND_FLOPS)
    got = over_chips(send, None, 2)
    output, grad_input = call(
        mp_sum_kernel, "mp_sum", [(square, BF)] * 2, [mp_keep, over_mp(mp_send, 1)], keep=False
    )
    (dw,) = call(last_sum_kernel, "last_sum", [((4,) + block, F32)], [keep, got], apart=(output,), keep=False)
    return output, grad_input, dw


def solution(mesh):
    fine = Mesh(mesh.devices.reshape(8, 4, 2, 4), SPACE + ("mp",))
    in_specs = (
        P(SPACE, None),
        P(None, "mp"),
        P(None, "mp"),
        P(None, "mp"),
        P("mp", None),
        P(SPACE, "mp"),
        P(SPACE, None),
        P(SPACE, None),
    )
    out_specs = (P(SPACE, "mp"), P(SPACE, "mp"), P(None, SPACE, "mp"))
    return jax.shard_map(body, mesh=fine, in_specs=in_specs, out_specs=out_specs, check_vma=False)
```

```python
import functools

import jax
import jax.numpy as jnp
from jax import lax
from jax.experimental import pallas as pl
from jax.experimental.pallas import tpu as pltpu
from jax.sharding import Mesh
from jax.sharding import PartitionSpec as P

HD = 64
PATCH = 64
D = 1024
ROW = 256
WIDTH = 256
HEADS = WIDTH // HD
FIRST_FLOPS, SECOND_FLOPS = 4_000_000_000, 4_000_000_000
KEYS = 3 * ROW
LOG2E = 1.4426950408889634
BF = jnp.bfloat16
F32 = jnp.float32
SPACE = ("z", "y", "core")

NN = (((1,), (0,)), ((), ()))
NT = (((1,), (1,)), ((), ()))


def mm(a, b, dims=NN):
    return lax.dot_general(a, b, dims, preferred_element_type=F32)


def places():
    return [lax.axis_index(a) for a in ("core", "y", "z", "mp")]


def slot_bias(nb, mask, core, y, z):
    row = (z * 4 + y) * 2 + core
    sign = 1 - 2 * core
    patch_of_lane = lax.broadcasted_iota(jnp.int32, (16, ROW), 1) // PATCH
    patch_of_row = lax.broadcasted_iota(jnp.int32, (16, ROW), 0)
    count = jnp.zeros((16, ROW), F32)
    for slot in range(9):
        named = jnp.zeros((16, ROW), jnp.int32)
        for patch in range(4):
            number = nb[patch, slot]
            band = 1 + sign * ((number >> 2) - row)
            place = jnp.where(mask[patch, slot] > 0, band * 4 + (number & 3), -1)
            named = jnp.where(patch_of_lane == patch, place, named)
        count += jnp.where(named == patch_of_row, 1.0, 0.0)
    return jnp.where(count > 0, jnp.where(count > 1, jnp.log(count) * LOG2E, 0.0), -1e30)


def y_pair(y):
    return y ^ 1


def y_other(y):
    return y ^ 3


def z_pair(z):
    return z ^ 1


def z_other(z):
    return (z + 2 * (z & 1) + 7) & 7


def z_far(z):
    return z ^ (3 + 4 * ((z ^ (z >> 1)) & 1))


def z_far_too(z):
    return z ^ 5


def target_rows(z, y, y_partners, z_partners):
    def reached(start, partners):
        places = [start]
        for partner in partners:
            places = [there for here in places for there in (here, partner(here))]
        return places

    ys, zs = reached(y, y_partners), reached(z, z_partners)
    rows = []
    for number in range(32):
        y1, z1, y2, z2, z3 = ((number >> (4 - bit)) & 1 for bit in range(5))
        rows.append(zs[4 * z1 + 2 * z2 + z3] * 4 + ys[2 * y1 + y2])
    return rows


PARTNERS = (
    ((y_pair, y_other), (z_pair, z_other, z_far)),
    ((y_other, y_pair), (z_other, z_pair, z_far_too)),
)


def mp_partner(core, x, step):
    near, across = x ^ 1, 3 - x
    if isinstance(core, int):
        return (near, across)[(core + step) % 2]
    return jnp.where(core == step, near, across)


def columns(ref, place):
    return ref[:, pl.ds(pl.multiple_of(place * WIDTH, WIDTH), WIDTH)]


def head_lanes():
    return lax.broadcasted_iota(jnp.int32, (ROW, WIDTH), 1) // HD


def stack_heads(rows, out):
    for head in range(HEADS):
        out[head * ROW : (head + 1) * ROW, :] = jnp.where(head_lanes() == head, rows, jnp.zeros_like(rows))


def pick_heads(stacked):
    total = jnp.zeros((ROW, WIDTH), F32)
    for head in range(HEADS):
        total = jnp.where(head_lanes() == head, stacked[head * ROW : (head + 1) * ROW], total)
    return total.astype(BF)


def store_halves(out, rows, start, core):
    for block in range(rows.shape[0] // 32):
        for c in range(2):
            half = jnp.where(core == c, D // 2, 0)
            there = pl.ds(pl.multiple_of(half + start + 16 * block, 16), 16)
            out[there, :] = rows[32 * block + 16 * c : 32 * block + 16 * (c + 1)]


def spread_bias(bias, patches):
    return jnp.concatenate(
        [jnp.broadcast_to(bias[patch : patch + 1, :], (PATCH, ROW)) for patch in patches], axis=0
    )


def own_kernel(
    act, w_q, w_k, w_v, w_o, cot, slots, live, a_near,
    wq, wk, wv, wo, query_out, keys_out, values_out, exps_out, peaks_out, act_t, near_t, grad_out, cot_t, bias_out,
    act_s, cot_s, nb, mask, sems,
):
    core, y, z, x = places()
    pairs = (
        (slots, nb), (live, mask), (act, act_s), (w_k, wk), (w_v, wv), (w_q, wq), (cot, cot_s), (w_o, wo)
    )
    copies = [pltpu.make_async_copy(a, b, sems.at[i]) for i, (a, b) in enumerate(pairs)]
    for copy in copies:
        copy.start()
    store_halves(near_t, a_near[...].T, 0, core)
    copies[0].wait()
    copies[1].wait()
    bias = slot_bias(nb, mask, core, y, z)
    bias_out[...] = bias
    copies[2].wait()
    store_halves(act_t, act_s[...].T, 0, core)
    for index, weight, out in ((3, wk, keys_out), (4, wv, values_out)):
        copies[index].wait()
        out[:ROW, :] = mm(act_s[...], weight[...]).astype(BF)
        out[ROW:, :] = mm(a_near[...], weight[...]).astype(BF)
    copies[5].wait()
    stack_heads(mm(act_s[...], wq[...]).astype(BF), query_out)
    bias_rows = spread_bias(bias, range(4, 12))
    for head in range(HEADS):
        scores = mm(keys_out[...], query_out[head * ROW : (head + 1) * ROW, :], NT)
        scores = scores * (LOG2E * HD**-0.5) + bias_rows
        peak = jnp.max(scores, axis=0, keepdims=True)
        exps = jnp.exp2(scores - peak)
        exps_out[head] = exps
        peaks_out[head : head + 1, :] = peak
        peaks_out[HEADS + head : HEADS + head + 1, :] = jnp.sum(exps, axis=0, keepdims=True)
    copies[6].wait()
    cot_t[...] = cot_s[...].T
    copies[7].wait()
    grad_out[...] = mm(cot_s[...], columns(wo, x), NT)


def forward_kernel(
    a_far, wk, wv, query, keys_in, values_in, exps, peaks, bias,
    keys, values, probs_out, att_out, far_t,
    probs_t,
):
    core = places()[0]
    keys[ROW:, :] = keys_in[...]
    values[ROW:, :] = values_in[...]
    keys[:ROW, :] = mm(a_far[...], wk[...]).astype(BF)
    values[:ROW, :] = mm(a_far[...], wv[...]).astype(BF)
    bias_rows = spread_bias(bias, range(4))
    for head in range(HEADS):
        part = slice(head * ROW, (head + 1) * ROW)
        scores = mm(keys[:ROW, :], query[part, :], NT) * (LOG2E * HD**-0.5) + bias_rows
        peak_before = peaks[head : head + 1, :]
        peak = jnp.maximum(peak_before, jnp.max(scores, axis=0, keepdims=True))
        weights = jnp.exp2(scores - peak)
        before = jnp.exp2(peak_before - peak)
        total = before * peaks[HEADS + head : HEADS + head + 1, :] + jnp.sum(weights, axis=0, keepdims=True)
        scale = 1.0 / total
        far_probs = (weights * scale).astype(BF)
        other_probs = (exps[head] * (before * scale)).astype(BF)
        probs_out[:ROW, part] = far_probs
        probs_out[ROW:, part] = other_probs
        probs_t[part, :ROW] = far_probs.T
        probs_t[part, ROW:] = other_probs.T
    att_out[...] = pick_heads(mm(probs_t[...], values[...]))
    store_halves(far_t, a_far[...].T, 0, core)


def weight_terms(half, partners, act_t, far_t, near_t, cot_t, gq, grad_key, grad_value, att, out, dw_s):
    rows = slice(half * (D // 2), (half + 1) * (D // 2))
    dw_s[0] = mm(act_t[rows, :], gq[...])
    for index, grad in ((1, grad_key), (2, grad_value)):
        dw_s[index] = (
            mm(act_t[rows, :], grad[ROW : 2 * ROW, :])
            + mm(far_t[rows, :], grad[:ROW, :])
            + mm(near_t[rows, :], grad[2 * ROW :, :])
        )
    dw_s[3] = mm(cot_t[rows, :], att[...])
    core, y, z, _ = places()
    tables = [target_rows(z, y, *pair) for pair in PARTNERS]
    for number in range(32):
        zero, one = (table[number] * 16 for table in tables)
        row = pl.multiple_of(jnp.where(partners == 0, zero, one), 16)
        out[4 * number : 4 * number + 4] = dw_s[:, pl.ds(row, 16), :].astype(BF)


def backward_kernel(
    keys, values, probs_in, att, far_t, near_t, wo, query, act_t, grad_in, cot_own, c2, c1, c3,
    gq, far_out, own_out, grad_key, grad_value, cot_t, send_out,
    grad_s, scores_s, scores_t, dw_s,
):
    core, y, z, x = places()
    grad_att = grad_in[...]
    blocks = ((x ^ 2, c2), (x ^ 1, c1), (x ^ 3, c3))
    for place, block in blocks:
        grad_att += mm(block[...], columns(wo, place), NT)
    stack_heads(grad_att.astype(BF), grad_s)
    for head in range(HEADS):
        part = slice(head * ROW, (head + 1) * ROW)
        probs = probs_in[:, part].astype(F32)
        grad_probs = mm(values[...], grad_s[part, :], NT)
        centre = jnp.sum(probs * grad_probs, axis=0, keepdims=True)
        grad_scores = (probs * ((grad_probs - centre) * HD**-0.5)).astype(BF)
        scores_s[:, part] = grad_scores
        scores_t[part, :] = grad_scores.T
    gq[...] = pick_heads(mm(scores_t[...], keys[...]))
    for index, (grad, out) in enumerate(
        ((mm(scores_s[...], query[...]), grad_key), (mm(probs_in[...], grad_s[...]), grad_value))
    ):
        low = grad.astype(BF)
        out[...] = low
        far_out[index] = low[:ROW]
        own_out[index] = grad[ROW : 2 * ROW]
        for block in range(16):
            rows = slice(2 * ROW + 16 * block, 2 * ROW + 16 * (block + 1))
            send_out[128 + 16 * index + block] = low[rows]
    for place, block_t in ((x, cot_own[...]), *((place, block[...].T) for place, block in blocks)):
        store_halves(cot_t, block_t, place * (WIDTH // 2), core)
    weight_terms(
        0, 1 - core, act_t, far_t, near_t, cot_t, gq, grad_key, grad_value, att, send_out, dw_s
    )


def keep_kernel(act_t, far_t, near_t, cot_t, gq, grad_key, grad_value, att, keep_out, dw_s):
    core = places()[0]
    weight_terms(
        1, core, act_t, far_t, near_t, cot_t, gq, grad_key, grad_value, att, keep_out, dw_s
    )


def share_kernel(count, *refs):
    terms, outs = refs[:count], refs[count:]
    size = outs[0].shape[0]
    for place, out in enumerate(outs):
        part = slice(size * place, size * (place + 1))
        total = terms[0][part].astype(F32)
        for term in terms[1:]:
            total += term[part].astype(F32)
        out[...] = total.astype(out.dtype)


def input_kernel(att, gq, own, near, far, wq, wk, wv, wo, keep, send):
    core, _, _, x = places()
    grads = []
    for part in range(2):
        from_near = near[128 + 16 * part : 144 + 16 * part].reshape(ROW, WIDTH)
        grads.append((own[part] + from_near.astype(F32) + far[part].astype(F32)).astype(BF))
    grad_key, grad_value = grads
    first, second = (mp_partner(core, x, step) for step in range(2))
    for out, targets in ((keep, (x, second)), (send, (first, x ^ 2))):
        for place, target in enumerate(targets):
            block = pl.ds(pl.multiple_of(target * WIDTH, WIDTH), WIDTH)
            out[2 * place] = mm(att[...], wo[:, block]).astype(out.dtype)
            out[2 * place + 1] = (
                mm(gq[...], wq[block, :], NT)
                + mm(grad_key, wk[block, :], NT)
                + mm(grad_value, wv[block, :], NT)
            ).astype(out.dtype)


def mp_sum_kernel(kept, got, out, grad):
    for part, ref in ((0, out), (1, grad)):
        ref[...] = (kept[part] + got[part].astype(F32)).astype(BF)


def last_sum_kernel(after, kept, got, dw):
    dw[...] = kept[...] + got[...].astype(F32)


def on_chip(*arrays):
    return [pltpu.with_memory_space_constraint(a, pltpu.VMEM) for a in arrays]


def call(
    kernel, name, outs, arrays, apart=(), scratch=(), limit=16, flops=0, moved=1_000_000, keep=True
):
    kept = [pltpu.VMEM(shape, dtype) if keep else jax.ShapeDtypeStruct(shape, dtype) for shape, dtype in outs]
    return pl.pallas_call(
        kernel,
        out_shape=tuple(kept),
        in_specs=[pl.BlockSpec(memory_space=pltpu.HBM)] * len(apart)
        + [pl.BlockSpec(memory_space=pltpu.VMEM)] * len(arrays),
        out_specs=(pl.BlockSpec(memory_space=pltpu.VMEM),) * len(kept),
        scratch_shapes=list(scratch),
        compiler_params=pltpu.CompilerParams(vmem_limit_bytes=limit * 1024 * 1024),
        cost_estimate=pl.CostEstimate(flops=flops, bytes_accessed=moved, transcendentals=0),
        name=name,
    )(*[pltpu.with_memory_space_constraint(a, pltpu.HBM) for a in apart], *on_chip(*arrays))


def move(value, axis, target):
    count = lax.axis_size(axis)
    return lax.ppermute(
        value, axis, [(i, target(i)) for i in range(count) if 0 <= target(i) < count]
    )


def over_mp(value, step):
    def target(i):
        return i // 4 * 4 + mp_partner(i // 4 % 2, i % 4, step)

    return move(value, SPACE + ("mp",), target)


def near_row(value):
    return move(value, SPACE, lambda i: i ^ 1)


def far_row(value):
    def target(i):
        row, x = i // 4, i % 4
        if row in (0, 63):
            return row * 4 + (x ^ 1)
        return (row + 1 if row % 2 else row - 1) * 4 + x

    return move(value, SPACE + ("mp",), target)


def body(activations, w_query, w_key, w_value, w_out, grad_output, neighbours, pad_mask):
    act_far = far_row(activations)
    cots = [move(grad_output, "mp", lambda i, step=step: i ^ step) for step in (2, 1, 3)]
    act_near = near_row(activations)

    square = (ROW, WIDTH)
    stacked = (HEADS * ROW, WIDTH)
    wq, wk, wv, wo, query, keys, values, exps, peaks, act_t, near_t, grad_own, cot_own, bias = call(
        own_kernel,
        "own_part",
        [((D, WIDTH), BF)] * 3
        + [((WIDTH, D), BF), (stacked, BF), ((2 * ROW, WIDTH), BF), ((2 * ROW, WIDTH), BF)]
        + [((HEADS, 2 * ROW, ROW), F32), ((2 * HEADS, ROW), F32)]
        + [((D, ROW), BF), ((D, ROW), BF), (square, F32), (square, BF), ((16, ROW), F32)],
        [act_near],
        apart=(activations, w_query, w_key, w_value, w_out, grad_output, neighbours, pad_mask),
        scratch=[
            pltpu.VMEM((ROW, D), BF),
            pltpu.VMEM(square, BF),
            pltpu.SMEM((4, 9), jnp.int32),
            pltpu.SMEM((4, 9), jnp.int32),
            pltpu.SemaphoreType.DMA((8,)),
        ],
        flops=600_000_000,
        moved=6_000_000,
    )

    block = (16, WIDTH)
    keys, values, probs, att, far_t = call(
        forward_kernel,
        "forward",
        [((KEYS, WIDTH), BF)] * 2 + [((KEYS, HEADS * ROW), BF), (square, BF), ((D, ROW), BF)],
        [act_far, wk, wv, query, keys, values, exps, peaks, bias],
        scratch=[pltpu.VMEM((HEADS * ROW, KEYS), BF)],
        limit=20,
        flops=2_000_000_000,
        moved=6_000_000,
    )
    gq, far, own, grad_key, grad_value, cot_t, dw_send = call(
        backward_kernel,
        "backward",
        [
            (square, BF),
            ((2, ROW, WIDTH), BF),
            ((2, ROW, WIDTH), F32),
            ((KEYS, WIDTH), BF),
            ((KEYS, WIDTH), BF),
            ((D, ROW), BF),
            ((160,) + block, BF),
        ],
        [keys, values, probs, att, far_t, near_t, wo, query, act_t, grad_own, cot_own, *cots],
        scratch=[
            pltpu.VMEM(stacked, BF),
            pltpu.VMEM((KEYS, HEADS * ROW), BF),
            pltpu.VMEM((HEADS * ROW, KEYS), BF),
            pltpu.VMEM((4, D // 2, WIDTH), F32),
        ],
        limit=24,
        flops=2_000_000_000,
        moved=8_000_000,
    )
    (dw_keep,) = call(
        keep_kernel,
        "keep_terms",
        [((128,) + block, BF)],
        [act_t, far_t, near_t, cot_t, gq, grad_key, grad_value, att],
        scratch=[pltpu.VMEM((4, D // 2, WIDTH), F32)],
        flops=1_000_000_000,
        moved=4_000_000,
    )

    def share(name, terms, ways, kept_as, flops=0):
        part = (terms[0].shape[0] // ways,) + terms[0].shape[1:]
        outs = [(part, kept_as)] + [(part, BF)] * (ways - 1)
        return call(functools.partial(share_kernel, len(terms)), name, outs, terms, flops=flops)

    def over_chips(value, y_step, z_step):
        def target(i):
            z, y, c = i // 8, i // 2 % 4, i % 2
            y_partners, z_partners = PARTNERS[c]
            y = y if y_step is None else y_partners[y_step](y)
            z = z if z_step is None else z_partners[z_step](z)
            return z * 8 + y * 2 + c

        return move(value, SPACE, target)

    def four_ways(parts, step):
        along_z, along_y = over_chips(parts[1], None, step), over_chips(parts[2], step, None)
        return [parts[0], over_chips(parts[3], step, step), along_y, along_z]

    from_core = near_row(dw_send)
    grad_far = far_row(far)
    parts = four_ways(share("core_sum", [dw_keep, from_core], 4, BF), 0)

    mp_keep, mp_send = call(
        input_kernel,
        "input_grad",
        [((4, ROW, WIDTH), F32), ((4, ROW, WIDTH), BF)],
        [att, gq, own, from_core, grad_far, wq, wk, wv, wo],
        flops=540_000_000,
        moved=4_000_000,
    )
    mp_keep, mp_send = share("mp_share", [mp_keep, over_mp(mp_send, 0)], 2, F32)
    parts = four_ways(share("first_sum", parts, 4, F32, FIRST_FLOPS), 1)
    keep, send = share("second_sum", parts, 2, F32, SECOND_FLOPS)
    got = over_chips(send, None, 2)
    output, grad_input = call(
        mp_sum_kernel, "mp_sum", [(square, BF)] * 2, [mp_keep, over_mp(mp_send, 1)], keep=False
    )
    (dw,) = call(last_sum_kernel, "last_sum", [((4,) + block, F32)], [keep, got], apart=(output,), keep=False)
    return output, grad_input, dw


def solution(mesh):
    fine = Mesh(mesh.devices.reshape(8, 4, 2, 4), SPACE + ("mp",))
    in_specs = (
        P(SPACE, None),
        P(None, "mp"),
        P(None, "mp"),
        P(None, "mp"),
        P("mp", None),
        P(SPACE, "mp"),
        P(SPACE, None),
        P(SPACE, None),
    )
    out_specs = (P(SPACE, "mp"), P(SPACE, "mp"), P(None, SPACE, "mp"))
    return jax.shard_map(body, mesh=fine, in_specs=in_specs, out_specs=out_specs, check_vma=False)
```

```python
import functools

import jax
import jax.numpy as jnp
from jax import lax
from jax.experimental import pallas as pl
from jax.experimental.pallas import tpu as pltpu
from jax.sharding import Mesh
from jax.sharding import PartitionSpec as P

HD = 64
PATCH = 64
D = 1024
ROW = 256
WIDTH = 256
HEADS = WIDTH // HD
FIRST_FLOPS, SECOND_FLOPS = 4_000_000_000, 4_000_000_000
KEYS = 3 * ROW
LOG2E = 1.4426950408889634
BF = jnp.bfloat16
F32 = jnp.float32
SPACE = ("z", "y", "core")

NN = (((1,), (0,)), ((), ()))
NT = (((1,), (1,)), ((), ()))


def mm(a, b, dims=NN):
    return lax.dot_general(a, b, dims, preferred_element_type=F32)


def places():
    return [lax.axis_index(a) for a in ("core", "y", "z", "mp")]


def slot_bias(nb, mask, core, y, z):
    row = (z * 4 + y) * 2 + core
    sign = 1 - 2 * core
    patch_of_lane = lax.broadcasted_iota(jnp.int32, (16, ROW), 1) // PATCH
    patch_of_row = lax.broadcasted_iota(jnp.int32, (16, ROW), 0)
    count = jnp.zeros((16, ROW), F32)
    for slot in range(9):
        named = jnp.zeros((16, ROW), jnp.int32)
        for patch in range(4):
            number = nb[patch, slot]
            band = 1 + sign * ((number >> 2) - row)
            place = jnp.where(mask[patch, slot] > 0, band * 4 + (number & 3), -1)
            named = jnp.where(patch_of_lane == patch, place, named)
        count += jnp.where(named == patch_of_row, 1.0, 0.0)
    return jnp.where(count > 0, jnp.where(count > 1, jnp.log(count) * LOG2E, 0.0), -1e30)


def y_pair(y):
    return y ^ 1


def y_other(y):
    return y ^ 3


def z_pair(z):
    return z ^ 1


def z_other(z):
    return (z + 2 * (z & 1) + 7) & 7


def z_far(z):
    return z ^ (3 + 4 * ((z ^ (z >> 1)) & 1))


def z_far_too(z):
    return z ^ 5


def target_rows(z, y, y_partners, z_partners):
    def reached(start, partners):
        places = [start]
        for partner in partners:
            places = [there for here in places for there in (here, partner(here))]
        return places

    ys, zs = reached(y, y_partners), reached(z, z_partners)
    rows = []
    for number in range(32):
        y1, z1, y2, z2, z3 = ((number >> (4 - bit)) & 1 for bit in range(5))
        rows.append(zs[4 * z1 + 2 * z2 + z3] * 4 + ys[2 * y1 + y2])
    return rows


PARTNERS = (
    ((y_pair, y_other), (z_pair, z_other, z_far)),
    ((y_other, y_pair), (z_other, z_pair, z_far_too)),
)


def mp_partner(core, x, step):
    near, across = x ^ 1, 3 - x
    if isinstance(core, int):
        return (near, across)[(core + step) % 2]
    return jnp.where(core == step, near, across)


def columns(ref, place):
    return ref[:, pl.ds(pl.multiple_of(place * WIDTH, WIDTH), WIDTH)]


def head_lanes():
    return lax.broadcasted_iota(jnp.int32, (ROW, WIDTH), 1) // HD


def stack_heads(rows, out):
    for head in range(HEADS):
        out[head * ROW : (head + 1) * ROW, :] = jnp.where(head_lanes() == head, rows, jnp.zeros_like(rows))


def pick_heads(stacked):
    total = jnp.zeros((ROW, WIDTH), F32)
    for head in range(HEADS):
        total = jnp.where(head_lanes() == head, stacked[head * ROW : (head + 1) * ROW], total)
    return total.astype(BF)


def store_halves(out, rows, start, core):
    for block in range(rows.shape[0] // 32):
        for c in range(2):
            half = jnp.where(core == c, D // 2, 0)
            there = pl.ds(pl.multiple_of(half + start + 16 * block, 16), 16)
            out[there, :] = rows[32 * block + 16 * c : 32 * block + 16 * (c + 1)]


def spread_bias(bias, patches):
    return jnp.concatenate(
        [jnp.broadcast_to(bias[patch : patch + 1, :], (PATCH, ROW)) for patch in patches], axis=0
    )


def own_kernel(
    act, w_q, w_k, w_v, w_o, cot, slots, live, a_near,
    wq, wk, wv, wo, query_out, keys_out, values_out, exps_out, peaks_out, act_t, near_t, grad_out, cot_t, bias_out,
    act_s, cot_s, nb, mask, sems,
):
    core, y, z, x = places()
    pairs = (
        (slots, nb), (live, mask), (act, act_s), (w_k, wk), (w_v, wv), (w_q, wq), (cot, cot_s), (w_o, wo)
    )
    copies = [pltpu.make_async_copy(a, b, sems.at[i]) for i, (a, b) in enumerate(pairs)]
    for copy in copies:
        copy.start()
    store_halves(near_t, a_near[...].T, 0, core)
    copies[0].wait()
    copies[1].wait()
    bias = slot_bias(nb, mask, core, y, z)
    bias_out[...] = bias
    copies[2].wait()
    store_halves(act_t, act_s[...].T, 0, core)
    for index, weight, out in ((3, wk, keys_out), (4, wv, values_out)):
        copies[index].wait()
        out[:ROW, :] = mm(act_s[...], weight[...]).astype(BF)
        out[ROW:, :] = mm(a_near[...], weight[...]).astype(BF)
    copies[5].wait()
    stack_heads(mm(act_s[...], wq[...]).astype(BF), query_out)
    bias_rows = spread_bias(bias, range(4, 12))
    for head in range(HEADS):
        scores = mm(keys_out[...], query_out[head * ROW : (head + 1) * ROW, :], NT)
        scores = scores * (LOG2E * HD**-0.5) + bias_rows
        peak = jnp.max(scores, axis=0, keepdims=True)
        exps = jnp.exp2(scores - peak)
        exps_out[head] = exps
        peaks_out[head : head + 1, :] = peak
        peaks_out[HEADS + head : HEADS + head + 1, :] = jnp.sum(exps, axis=0, keepdims=True)
    copies[6].wait()
    cot_t[...] = cot_s[...].T
    copies[7].wait()
    grad_out[...] = mm(cot_s[...], columns(wo, x), NT)


def forward_kernel(
    a_far, wk, wv, query, keys_in, values_in, exps, peaks, bias,
    keys, values, probs_out, att_out, far_t,
    probs_t,
):
    core = places()[0]
    keys[ROW:, :] = keys_in[...]
    values[ROW:, :] = values_in[...]
    keys[:ROW, :] = mm(a_far[...], wk[...]).astype(BF)
    values[:ROW, :] = mm(a_far[...], wv[...]).astype(BF)
    bias_rows = spread_bias(bias, range(4))
    for head in range(HEADS):
        part = slice(head * ROW, (head + 1) * ROW)
        scores = mm(keys[:ROW, :], query[part, :], NT) * (LOG2E * HD**-0.5) + bias_rows
        peak_before = peaks[head : head + 1, :]
        peak = jnp.maximum(peak_before, jnp.max(scores, axis=0, keepdims=True))
        weights = jnp.exp2(scores - peak)
        before = jnp.exp2(peak_before - peak)
        total = before * peaks[HEADS + head : HEADS + head + 1, :] + jnp.sum(weights, axis=0, keepdims=True)
        scale = 1.0 / total
        far_probs = (weights * scale).astype(BF)
        other_probs = (exps[head] * (before * scale)).astype(BF)
        probs_out[:ROW, part] = far_probs
        probs_out[ROW:, part] = other_probs
        probs_t[part, :ROW] = far_probs.T
        probs_t[part, ROW:] = other_probs.T
    att_out[...] = pick_heads(mm(probs_t[...], values[...]))
    store_halves(far_t, a_far[...].T, 0, core)


def weight_terms(half, partners, act_t, far_t, near_t, cot_t, gq, grad_key, grad_value, att, out, dw_s):
    rows = slice(half * (D // 2), (half + 1) * (D // 2))
    dw_s[0] = mm(act_t[rows, :], gq[...])
    for index, grad in ((1, grad_key), (2, grad_value)):
        dw_s[index] = (
            mm(act_t[rows, :], grad[ROW : 2 * ROW, :])
            + mm(far_t[rows, :], grad[:ROW, :])
            + mm(near_t[rows, :], grad[2 * ROW :, :])
        )
    dw_s[3] = mm(cot_t[rows, :], att[...])
    core, y, z, _ = places()
    tables = [target_rows(z, y, *pair) for pair in PARTNERS]
    for number in range(32):
        zero, one = (table[number] * 16 for table in tables)
        row = pl.multiple_of(jnp.where(partners == 0, zero, one), 16)
        out[4 * number : 4 * number + 4] = dw_s[:, pl.ds(row, 16), :].astype(BF)


def backward_kernel(
    keys, values, probs_in, att, far_t, near_t, wo, query, act_t, grad_in, cot_own, c2, c1, c3,
    gq, far_out, own_out, grad_key, grad_value, cot_t, send_out,
    grad_s, scores_s, scores_t, dw_s,
):
    core, y, z, x = places()
    grad_att = grad_in[...]
    blocks = ((x ^ 2, c2), (x ^ 1, c1), (x ^ 3, c3))
    for place, block in blocks:
        grad_att += mm(block[...], columns(wo, place), NT)
    stack_heads(grad_att.astype(BF), grad_s)
    for head in range(HEADS):
        part = slice(head * ROW, (head + 1) * ROW)
        probs = probs_in[:, part].astype(F32)
        grad_probs = mm(values[...], grad_s[part, :], NT)
        centre = jnp.sum(probs * grad_probs, axis=0, keepdims=True)
        grad_scores = (probs * ((grad_probs - centre) * HD**-0.5)).astype(BF)
        scores_s[:, part] = grad_scores
        scores_t[part, :] = grad_scores.T
    gq[...] = pick_heads(mm(scores_t[...], keys[...]))
    for index, (grad, out) in enumerate(
        ((mm(scores_s[...], query[...]), grad_key), (mm(probs_in[...], grad_s[...]), grad_value))
    ):
        low = grad.astype(BF)
        out[...] = low
        far_out[index] = low[:ROW]
        own_out[index] = grad[ROW : 2 * ROW]
        for block in range(16):
            rows = slice(2 * ROW + 16 * block, 2 * ROW + 16 * (block + 1))
            send_out[128 + 16 * index + block] = low[rows]
    for place, block_t in ((x, cot_own[...]), *((place, block[...].T) for place, block in blocks)):
        store_halves(cot_t, block_t, place * (WIDTH // 2), core)
    weight_terms(
        0, 1 - core, act_t, far_t, near_t, cot_t, gq, grad_key, grad_value, att, send_out, dw_s
    )


def keep_kernel(act_t, far_t, near_t, cot_t, gq, grad_key, grad_value, att, keep_out, dw_s):
    core = places()[0]
    weight_terms(
        1, core, act_t, far_t, near_t, cot_t, gq, grad_key, grad_value, att, keep_out, dw_s
    )


def share_kernel(count, *refs):
    terms, outs = refs[:count], refs[count:]
    size = outs[0].shape[0]
    for place, out in enumerate(outs):
        part = slice(size * place, size * (place + 1))
        total = terms[0][part].astype(F32)
        for term in terms[1:]:
            total += term[part].astype(F32)
        out[...] = total.astype(out.dtype)


def input_kernel(att, gq, own, near, far, wq, wk, wv, wo, keep, send):
    core, _, _, x = places()
    grads = []
    for part in range(2):
        from_near = near[128 + 16 * part : 144 + 16 * part].reshape(ROW, WIDTH)
        grads.append((own[part] + from_near.astype(F32) + far[part].astype(F32)).astype(BF))
    grad_key, grad_value = grads
    first, second = (mp_partner(core, x, step) for step in range(2))
    for out, targets in ((keep, (x, second)), (send, (first, x ^ 2))):
        for place, target in enumerate(targets):
            block = pl.ds(pl.multiple_of(target * WIDTH, WIDTH), WIDTH)
            out[2 * place] = mm(att[...], wo[:, block]).astype(out.dtype)
            out[2 * place + 1] = (
                mm(gq[...], wq[block, :], NT)
                + mm(grad_key, wk[block, :], NT)
                + mm(grad_value, wv[block, :], NT)
            ).astype(out.dtype)


def mp_sum_kernel(kept, got, out, grad):
    for part, ref in ((0, out), (1, grad)):
        ref[...] = (kept[part] + got[part].astype(F32)).astype(BF)


def last_sum_kernel(after, kept, got, dw):
    dw[...] = kept[...] + got[...].astype(F32)


def on_chip(*arrays):
    return [pltpu.with_memory_space_constraint(a, pltpu.VMEM) for a in arrays]


def call(
    kernel, name, outs, arrays, apart=(), scratch=(), limit=16, flops=0, moved=1_000_000, keep=True
):
    kept = [pltpu.VMEM(shape, dtype) if keep else jax.ShapeDtypeStruct(shape, dtype) for shape, dtype in outs]
    return pl.pallas_call(
        kernel,
        out_shape=tuple(kept),
        in_specs=[pl.BlockSpec(memory_space=pltpu.HBM)] * len(apart)
        + [pl.BlockSpec(memory_space=pltpu.VMEM)] * len(arrays),
        out_specs=(pl.BlockSpec(memory_space=pltpu.VMEM),) * len(kept),
        scratch_shapes=list(scratch),
        compiler_params=pltpu.CompilerParams(vmem_limit_bytes=limit * 1024 * 1024),
        cost_estimate=pl.CostEstimate(flops=flops, bytes_accessed=moved, transcendentals=0),
        name=name,
    )(*[pltpu.with_memory_space_constraint(a, pltpu.HBM) for a in apart], *on_chip(*arrays))


def move(value, axis, target):
    count = lax.axis_size(axis)
    return lax.ppermute(
        value, axis, [(i, target(i)) for i in range(count) if 0 <= target(i) < count]
    )


def over_mp(value, step):
    def target(i):
        return i // 4 * 4 + mp_partner(i // 4 % 2, i % 4, step)

    return move(value, SPACE + ("mp",), target)


def near_row(value):
    return move(value, SPACE, lambda i: i ^ 1)


def far_row(value):
    def target(i):
        row, x = i // 4, i % 4
        if row in (0, 63):
            return row * 4 + (x ^ 3)
        return (row + 1 if row % 2 else row - 1) * 4 + x

    return move(value, SPACE + ("mp",), target)


def body(activations, w_query, w_key, w_value, w_out, grad_output, neighbours, pad_mask):
    act_far = far_row(activations)
    cots = [move(grad_output, "mp", lambda i, step=step: i ^ step) for step in (2, 1, 3)]
    act_near = near_row(activations)

    square = (ROW, WIDTH)
    stacked = (HEADS * ROW, WIDTH)
    wq, wk, wv, wo, query, keys, values, exps, peaks, act_t, near_t, grad_own, cot_own, bias = call(
        own_kernel,
        "own_part",
        [((D, WIDTH), BF)] * 3
        + [((WIDTH, D), BF), (stacked, BF), ((2 * ROW, WIDTH), BF), ((2 * ROW, WIDTH), BF)]
        + [((HEADS, 2 * ROW, ROW), F32), ((2 * HEADS, ROW), F32)]
        + [((D, ROW), BF), ((D, ROW), BF), (square, F32), (square, BF), ((16, ROW), F32)],
        [act_near],
        apart=(activations, w_query, w_key, w_value, w_out, grad_output, neighbours, pad_mask),
        scratch=[
            pltpu.VMEM((ROW, D), BF),
            pltpu.VMEM(square, BF),
            pltpu.SMEM((4, 9), jnp.int32),
            pltpu.SMEM((4, 9), jnp.int32),
            pltpu.SemaphoreType.DMA((8,)),
        ],
        flops=600_000_000,
        moved=6_000_000,
    )

    block = (16, WIDTH)
    keys, values, probs, att, far_t = call(
        forward_kernel,
        "forward",
        [((KEYS, WIDTH), BF)] * 2 + [((KEYS, HEADS * ROW), BF), (square, BF), ((D, ROW), BF)],
        [act_far, wk, wv, query, keys, values, exps, peaks, bias],
        scratch=[pltpu.VMEM((HEADS * ROW, KEYS), BF)],
        limit=20,
        flops=2_000_000_000,
        moved=6_000_000,
    )
    gq, far, own, grad_key, grad_value, cot_t, dw_send = call(
        backward_kernel,
        "backward",
        [
            (square, BF),
            ((2, ROW, WIDTH), BF),
            ((2, ROW, WIDTH), F32),
            ((KEYS, WIDTH), BF),
            ((KEYS, WIDTH), BF),
            ((D, ROW), BF),
            ((160,) + block, BF),
        ],
        [keys, values, probs, att, far_t, near_t, wo, query, act_t, grad_own, cot_own, *cots],
        scratch=[
            pltpu.VMEM(stacked, BF),
            pltpu.VMEM((KEYS, HEADS * ROW), BF),
            pltpu.VMEM((HEADS * ROW, KEYS), BF),
            pltpu.VMEM((4, D // 2, WIDTH), F32),
        ],
        limit=24,
        flops=2_000_000_000,
        moved=8_000_000,
    )
    (dw_keep,) = call(
        keep_kernel,
        "keep_terms",
        [((128,) + block, BF)],
        [act_t, far_t, near_t, cot_t, gq, grad_key, grad_value, att],
        scratch=[pltpu.VMEM((4, D // 2, WIDTH), F32)],
        flops=1_000_000_000,
        moved=4_000_000,
    )

    def share(name, terms, ways, kept_as, flops=0):
        part = (terms[0].shape[0] // ways,) + terms[0].shape[1:]
        outs = [(part, kept_as)] + [(part, BF)] * (ways - 1)
        return call(functools.partial(share_kernel, len(terms)), name, outs, terms, flops=flops)

    def over_chips(value, y_step, z_step):
        def target(i):
            z, y, c = i // 8, i // 2 % 4, i % 2
            y_partners, z_partners = PARTNERS[c]
            y = y if y_step is None else y_partners[y_step](y)
            z = z if z_step is None else z_partners[z_step](z)
            return z * 8 + y * 2 + c

        return move(value, SPACE, target)

    def four_ways(parts, step):
        along_z, along_y = over_chips(parts[1], None, step), over_chips(parts[2], step, None)
        return [parts[0], over_chips(parts[3], step, step), along_y, along_z]

    from_core = near_row(dw_send)
    grad_far = far_row(far)
    parts = four_ways(share("core_sum", [dw_keep, from_core], 4, BF), 0)

    mp_keep, mp_send = call(
        input_kernel,
        "input_grad",
        [((4, ROW, WIDTH), F32), ((4, ROW, WIDTH), BF)],
        [att, gq, own, from_core, grad_far, wq, wk, wv, wo],
        flops=540_000_000,
        moved=4_000_000,
    )
    mp_keep, mp_send = share("mp_share", [mp_keep, over_mp(mp_send, 0)], 2, F32)
    parts = four_ways(share("first_sum", parts, 4, F32, FIRST_FLOPS), 1)
    keep, send = share("second_sum", parts, 2, F32, SECOND_FLOPS)
    got = over_chips(send, None, 2)
    output, grad_input = call(
        mp_sum_kernel, "mp_sum", [(square, BF)] * 2, [mp_keep, over_mp(mp_send, 1)], keep=False
    )
    (dw,) = call(last_sum_kernel, "last_sum", [((4,) + block, F32)], [keep, got], apart=(output,), keep=False)
    return output, grad_input, dw


def solution(mesh):
    fine = Mesh(mesh.devices.reshape(8, 4, 2, 4), SPACE + ("mp",))
    in_specs = (
        P(SPACE, None),
        P(None, "mp"),
        P(None, "mp"),
        P(None, "mp"),
        P("mp", None),
        P(SPACE, "mp"),
        P(SPACE, None),
        P(SPACE, None),
    )
    out_specs = (P(SPACE, "mp"), P(SPACE, "mp"), P(None, SPACE, "mp"))
    return jax.shard_map(body, mesh=fine, in_specs=in_specs, out_specs=out_specs, check_vma=False)
```

```python
import functools

import jax
import jax.numpy as jnp
from jax import lax
from jax.experimental import pallas as pl
from jax.experimental.pallas import tpu as pltpu
from jax.sharding import Mesh
from jax.sharding import PartitionSpec as P

HD = 64
PATCH = 64
D = 1024
ROW = 256
WIDTH = 256
HEADS = WIDTH // HD
FIRST_FLOPS, SECOND_FLOPS = 4_000_000_000, 4_000_000_000
KEYS = 3 * ROW
LOG2E = 1.4426950408889634
BF = jnp.bfloat16
F32 = jnp.float32
SPACE = ("z", "y", "core")

NN = (((1,), (0,)), ((), ()))
NT = (((1,), (1,)), ((), ()))


def mm(a, b, dims=NN):
    return lax.dot_general(a, b, dims, preferred_element_type=F32)


def places():
    return [lax.axis_index(a) for a in ("core", "y", "z", "mp")]


def slot_bias(nb, mask, core, y, z):
    row = (z * 4 + y) * 2 + core
    sign = 1 - 2 * core
    patch_of_lane = lax.broadcasted_iota(jnp.int32, (16, ROW), 1) // PATCH
    patch_of_row = lax.broadcasted_iota(jnp.int32, (16, ROW), 0)
    count = jnp.zeros((16, ROW), F32)
    for slot in range(9):
        named = jnp.zeros((16, ROW), jnp.int32)
        for patch in range(4):
            number = nb[patch, slot]
            band = 1 + sign * ((number >> 2) - row)
            place = jnp.where(mask[patch, slot] > 0, band * 4 + (number & 3), -1)
            named = jnp.where(patch_of_lane == patch, place, named)
        count += jnp.where(named == patch_of_row, 1.0, 0.0)
    return jnp.where(count > 0, jnp.where(count > 1, jnp.log(count) * LOG2E, 0.0), -1e30)


def y_pair(y):
    return y ^ 1


def y_other(y):
    return y ^ 3


def z_pair(z):
    return z ^ 1


def z_other(z):
    return (z + 2 * (z & 1) + 7) & 7


def z_far(z):
    return z ^ (3 + 4 * ((z ^ (z >> 1)) & 1))


def z_far_too(z):
    return z ^ 5


def target_rows(z, y, y_partners, z_partners):
    def reached(start, partners):
        places = [start]
        for partner in partners:
            places = [there for here in places for there in (here, partner(here))]
        return places

    ys, zs = reached(y, y_partners), reached(z, z_partners)
    rows = []
    for number in range(32):
        y1, z1, y2, z2, z3 = ((number >> (4 - bit)) & 1 for bit in range(5))
        rows.append(zs[4 * z1 + 2 * z2 + z3] * 4 + ys[2 * y1 + y2])
    return rows


PARTNERS = (
    ((y_pair, y_other), (z_pair, z_other, z_far)),
    ((y_other, y_pair), (z_other, z_pair, z_far_too)),
)


def mp_partner(core, x, step):
    near, across = x ^ 1, 3 - x
    if isinstance(core, int):
        return (near, across)[(core + step) % 2]
    return jnp.where(core == step, near, across)


def columns(ref, place):
    return ref[:, pl.ds(pl.multiple_of(place * WIDTH, WIDTH), WIDTH)]


def head_lanes():
    return lax.broadcasted_iota(jnp.int32, (ROW, WIDTH), 1) // HD


def stack_heads(rows, out):
    for head in range(HEADS):
        out[head * ROW : (head + 1) * ROW, :] = jnp.where(head_lanes() == head, rows, jnp.zeros_like(rows))


def pick_heads(stacked):
    total = jnp.zeros((ROW, WIDTH), F32)
    for head in range(HEADS):
        total = jnp.where(head_lanes() == head, stacked[head * ROW : (head + 1) * ROW], total)
    return total.astype(BF)


def store_halves(out, rows, start, core):
    for block in range(rows.shape[0] // 32):
        for c in range(2):
            half = jnp.where(core == c, D // 2, 0)
            there = pl.ds(pl.multiple_of(half + start + 16 * block, 16), 16)
            out[there, :] = rows[32 * block + 16 * c : 32 * block + 16 * (c + 1)]


def spread_bias(bias, patches):
    return jnp.concatenate(
        [jnp.broadcast_to(bias[patch : patch + 1, :], (PATCH, ROW)) for patch in patches], axis=0
    )


def own_kernel(
    act, w_q, w_k, w_v, w_o, cot, slots, live, a_near,
    wq, wk, wv, wo, query_out, keys_out, values_out, exps_out, peaks_out, act_t, near_t, grad_out, cot_t, bias_out,
    act_s, cot_s, nb, mask, sems,
):
    core, y, z, x = places()
    pairs = (
        (slots, nb), (live, mask), (act, act_s), (w_k, wk), (w_v, wv), (w_q, wq), (cot, cot_s), (w_o, wo)
    )
    copies = [pltpu.make_async_copy(a, b, sems.at[i]) for i, (a, b) in enumerate(pairs)]
    for copy in copies:
        copy.start()
    store_halves(near_t, a_near[...].T, 0, core)
    copies[0].wait()
    copies[1].wait()
    bias = slot_bias(nb, mask, core, y, z)
    bias_out[...] = bias
    copies[2].wait()
    store_halves(act_t, act_s[...].T, 0, core)
    for index, weight, out in ((3, wk, keys_out), (4, wv, values_out)):
        copies[index].wait()
        out[:ROW, :] = mm(act_s[...], weight[...]).astype(BF)
        out[ROW:, :] = mm(a_near[...], weight[...]).astype(BF)
    copies[5].wait()
    stack_heads(mm(act_s[...], wq[...]).astype(BF), query_out)
    bias_rows = spread_bias(bias, range(4, 12))
    for head in range(HEADS):
        scores = mm(keys_out[...], query_out[head * ROW : (head + 1) * ROW, :], NT)
        scores = scores * (LOG2E * HD**-0.5) + bias_rows
        peak = jnp.max(scores, axis=0, keepdims=True)
        exps = jnp.exp2(scores - peak)
        exps_out[head] = exps
        peaks_out[head : head + 1, :] = peak
        peaks_out[HEADS + head : HEADS + head + 1, :] = jnp.sum(exps, axis=0, keepdims=True)
    copies[6].wait()
    cot_t[...] = cot_s[...].T
    copies[7].wait()
    grad_out[...] = mm(cot_s[...], columns(wo, x), NT)


def forward_kernel(
    a_far, wk, wv, query, keys_in, values_in, exps, peaks, bias,
    keys, values, probs_out, att_out, far_t,
    probs_t,
):
    core = places()[0]
    keys[ROW:, :] = keys_in[...]
    values[ROW:, :] = values_in[...]
    keys[:ROW, :] = mm(a_far[...], wk[...]).astype(BF)
    values[:ROW, :] = mm(a_far[...], wv[...]).astype(BF)
    bias_rows = spread_bias(bias, range(4))
    for head in range(HEADS):
        part = slice(head * ROW, (head + 1) * ROW)
        scores = mm(keys[:ROW, :], query[part, :], NT) * (LOG2E * HD**-0.5) + bias_rows
        peak_before = peaks[head : head + 1, :]
        peak = jnp.maximum(peak_before, jnp.max(scores, axis=0, keepdims=True))
        weights = jnp.exp2(scores - peak)
        before = jnp.exp2(peak_before - peak)
        total = before * peaks[HEADS + head : HEADS + head + 1, :] + jnp.sum(weights, axis=0, keepdims=True)
        scale = 1.0 / total
        far_probs = (weights * scale).astype(BF)
        other_probs = (exps[head] * (before * scale)).astype(BF)
        probs_out[:ROW, part] = far_probs
        probs_out[ROW:, part] = other_probs
        probs_t[part, :ROW] = far_probs.T
        probs_t[part, ROW:] = other_probs.T
    att_out[...] = pick_heads(mm(probs_t[...], values[...]))
    store_halves(far_t, a_far[...].T, 0, core)


def weight_terms(half, partners, act_t, far_t, near_t, cot_t, gq, grad_key, grad_value, att, out, dw_s):
    rows = slice(half * (D // 2), (half + 1) * (D // 2))
    dw_s[0] = mm(act_t[rows, :], gq[...])
    for index, grad in ((1, grad_key), (2, grad_value)):
        dw_s[index] = (
            mm(act_t[rows, :], grad[ROW : 2 * ROW, :])
            + mm(far_t[rows, :], grad[:ROW, :])
            + mm(near_t[rows, :], grad[2 * ROW :, :])
        )
    dw_s[3] = mm(cot_t[rows, :], att[...])
    core, y, z, _ = places()
    tables = [target_rows(z, y, *pair) for pair in PARTNERS]
    for number in range(32):
        zero, one = (table[number] * 16 for table in tables)
        row = pl.multiple_of(jnp.where(partners == 0, zero, one), 16)
        out[4 * number : 4 * number + 4] = dw_s[:, pl.ds(row, 16), :].astype(BF)


def backward_kernel(
    keys, values, probs_in, att, far_t, near_t, wo, query, act_t, grad_in, cot_own, c3, c2, c1,
    gq, far_out, own_out, grad_key, grad_value, cot_t, send_out,
    grad_s, scores_s, scores_t, dw_s,
):
    core, y, z, x = places()
    grad_att = grad_in[...]
    blocks = ((x ^ 3, c3), (x ^ 2, c2), (x ^ 1, c1))
    for place, block in blocks:
        grad_att += mm(block[...], columns(wo, place), NT)
    stack_heads(grad_att.astype(BF), grad_s)
    for head in range(HEADS):
        part = slice(head * ROW, (head + 1) * ROW)
        probs = probs_in[:, part].astype(F32)
        grad_probs = mm(values[...], grad_s[part, :], NT)
        centre = jnp.sum(probs * grad_probs, axis=0, keepdims=True)
        grad_scores = (probs * ((grad_probs - centre) * HD**-0.5)).astype(BF)
        scores_s[:, part] = grad_scores
        scores_t[part, :] = grad_scores.T
    gq[...] = pick_heads(mm(scores_t[...], keys[...]))
    for index, (grad, out) in enumerate(
        ((mm(scores_s[...], query[...]), grad_key), (mm(probs_in[...], grad_s[...]), grad_value))
    ):
        low = grad.astype(BF)
        out[...] = low
        far_out[index] = low[:ROW]
        own_out[index] = grad[ROW : 2 * ROW]
        for block in range(16):
            rows = slice(2 * ROW + 16 * block, 2 * ROW + 16 * (block + 1))
            send_out[128 + 16 * index + block] = low[rows]
    for place, block_t in ((x, cot_own[...]), *((place, block[...].T) for place, block in blocks)):
        store_halves(cot_t, block_t, place * (WIDTH // 2), core)
    weight_terms(
        0, 1 - core, act_t, far_t, near_t, cot_t, gq, grad_key, grad_value, att, send_out, dw_s
    )


def keep_kernel(act_t, far_t, near_t, cot_t, gq, grad_key, grad_value, att, keep_out, dw_s):
    core = places()[0]
    weight_terms(
        1, core, act_t, far_t, near_t, cot_t, gq, grad_key, grad_value, att, keep_out, dw_s
    )


def share_kernel(count, *refs):
    terms, outs = refs[:count], refs[count:]
    size = outs[0].shape[0]
    for place, out in enumerate(outs):
        part = slice(size * place, size * (place + 1))
        total = terms[0][part].astype(F32)
        for term in terms[1:]:
            total += term[part].astype(F32)
        out[...] = total.astype(out.dtype)


def input_kernel(att, gq, own, near, far, wq, wk, wv, wo, keep, send):
    core, _, _, x = places()
    grads = []
    for part in range(2):
        from_near = near[128 + 16 * part : 144 + 16 * part].reshape(ROW, WIDTH)
        grads.append((own[part] + from_near.astype(F32) + far[part].astype(F32)).astype(BF))
    grad_key, grad_value = grads
    first, second = (mp_partner(core, x, step) for step in range(2))
    for out, targets in ((keep, (x, second)), (send, (first, x ^ 2))):
        for place, target in enumerate(targets):
            block = pl.ds(pl.multiple_of(target * WIDTH, WIDTH), WIDTH)
            out[2 * place] = mm(att[...], wo[:, block]).astype(out.dtype)
            out[2 * place + 1] = (
                mm(gq[...], wq[block, :], NT)
                + mm(grad_key, wk[block, :], NT)
                + mm(grad_value, wv[block, :], NT)
            ).astype(out.dtype)


def mp_sum_kernel(kept, got, out, grad):
    for part, ref in ((0, out), (1, grad)):
        ref[...] = (kept[part] + got[part].astype(F32)).astype(BF)


def last_sum_kernel(after, kept, got, dw):
    dw[...] = kept[...] + got[...].astype(F32)


def on_chip(*arrays):
    return [pltpu.with_memory_space_constraint(a, pltpu.VMEM) for a in arrays]


def call(
    kernel, name, outs, arrays, apart=(), scratch=(), limit=16, flops=0, moved=1_000_000, keep=True
):
    kept = [pltpu.VMEM(shape, dtype) if keep else jax.ShapeDtypeStruct(shape, dtype) for shape, dtype in outs]
    return pl.pallas_call(
        kernel,
        out_shape=tuple(kept),
        in_specs=[pl.BlockSpec(memory_space=pltpu.HBM)] * len(apart)
        + [pl.BlockSpec(memory_space=pltpu.VMEM)] * len(arrays),
        out_specs=(pl.BlockSpec(memory_space=pltpu.VMEM),) * len(kept),
        scratch_shapes=list(scratch),
        compiler_params=pltpu.CompilerParams(vmem_limit_bytes=limit * 1024 * 1024),
        cost_estimate=pl.CostEstimate(flops=flops, bytes_accessed=moved, transcendentals=0),
        name=name,
    )(*[pltpu.with_memory_space_constraint(a, pltpu.HBM) for a in apart], *on_chip(*arrays))


def move(value, axis, target):
    count = lax.axis_size(axis)
    return lax.ppermute(
        value, axis, [(i, target(i)) for i in range(count) if 0 <= target(i) < count]
    )


def over_mp(value, step):
    def target(i):
        return i // 4 * 4 + mp_partner(i // 4 % 2, i % 4, step)

    return move(value, SPACE + ("mp",), target)


def near_row(value):
    return move(value, SPACE, lambda i: i ^ 1)


def far_row(value):
    def target(i):
        row, x = i // 4, i % 4
        if row in (0, 63):
            return row * 4 + (x ^ 1)
        return (row + 1 if row % 2 else row - 1) * 4 + x

    return move(value, SPACE + ("mp",), target)


def body(activations, w_query, w_key, w_value, w_out, grad_output, neighbours, pad_mask):
    act_far = far_row(activations)
    cots = [move(grad_output, "mp", lambda i, step=step: i ^ step) for step in (3, 2, 1)]
    act_near = near_row(activations)

    square = (ROW, WIDTH)
    stacked = (HEADS * ROW, WIDTH)
    wq, wk, wv, wo, query, keys, values, exps, peaks, act_t, near_t, grad_own, cot_own, bias = call(
        own_kernel,
        "own_part",
        [((D, WIDTH), BF)] * 3
        + [((WIDTH, D), BF), (stacked, BF), ((2 * ROW, WIDTH), BF), ((2 * ROW, WIDTH), BF)]
        + [((HEADS, 2 * ROW, ROW), F32), ((2 * HEADS, ROW), F32)]
        + [((D, ROW), BF), ((D, ROW), BF), (square, F32), (square, BF), ((16, ROW), F32)],
        [act_near],
        apart=(activations, w_query, w_key, w_value, w_out, grad_output, neighbours, pad_mask),
        scratch=[
            pltpu.VMEM((ROW, D), BF),
            pltpu.VMEM(square, BF),
            pltpu.SMEM((4, 9), jnp.int32),
            pltpu.SMEM((4, 9), jnp.int32),
            pltpu.SemaphoreType.DMA((8,)),
        ],
        flops=600_000_000,
        moved=6_000_000,
    )

    block = (16, WIDTH)
    keys, values, probs, att, far_t = call(
        forward_kernel,
        "forward",
        [((KEYS, WIDTH), BF)] * 2 + [((KEYS, HEADS * ROW), BF), (square, BF), ((D, ROW), BF)],
        [act_far, wk, wv, query, keys, values, exps, peaks, bias],
        scratch=[pltpu.VMEM((HEADS * ROW, KEYS), BF)],
        limit=20,
        flops=2_000_000_000,
        moved=6_000_000,
    )
    gq, far, own, grad_key, grad_value, cot_t, dw_send = call(
        backward_kernel,
        "backward",
        [
            (square, BF),
            ((2, ROW, WIDTH), BF),
            ((2, ROW, WIDTH), F32),
            ((KEYS, WIDTH), BF),
            ((KEYS, WIDTH), BF),
            ((D, ROW), BF),
            ((160,) + block, BF),
        ],
        [keys, values, probs, att, far_t, near_t, wo, query, act_t, grad_own, cot_own, *cots],
        scratch=[
            pltpu.VMEM(stacked, BF),
            pltpu.VMEM((KEYS, HEADS * ROW), BF),
            pltpu.VMEM((HEADS * ROW, KEYS), BF),
            pltpu.VMEM((4, D // 2, WIDTH), F32),
        ],
        limit=24,
        flops=2_000_000_000,
        moved=8_000_000,
    )
    (dw_keep,) = call(
        keep_kernel,
        "keep_terms",
        [((128,) + block, BF)],
        [act_t, far_t, near_t, cot_t, gq, grad_key, grad_value, att],
        scratch=[pltpu.VMEM((4, D // 2, WIDTH), F32)],
        flops=1_000_000_000,
        moved=4_000_000,
    )

    def share(name, terms, ways, kept_as, flops=0):
        part = (terms[0].shape[0] // ways,) + terms[0].shape[1:]
        outs = [(part, kept_as)] + [(part, BF)] * (ways - 1)
        return call(functools.partial(share_kernel, len(terms)), name, outs, terms, flops=flops)

    def over_chips(value, y_step, z_step):
        def target(i):
            z, y, c = i // 8, i // 2 % 4, i % 2
            y_partners, z_partners = PARTNERS[c]
            y = y if y_step is None else y_partners[y_step](y)
            z = z if z_step is None else z_partners[z_step](z)
            return z * 8 + y * 2 + c

        return move(value, SPACE, target)

    def four_ways(parts, step):
        along_z, along_y = over_chips(parts[1], None, step), over_chips(parts[2], step, None)
        return [parts[0], over_chips(parts[3], step, step), along_y, along_z]

    from_core = near_row(dw_send)
    grad_far = far_row(far)
    parts = four_ways(share("core_sum", [dw_keep, from_core], 4, BF), 0)

    mp_keep, mp_send = call(
        input_kernel,
        "input_grad",
        [((4, ROW, WIDTH), F32), ((4, ROW, WIDTH), BF)],
        [att, gq, own, from_core, grad_far, wq, wk, wv, wo],
        flops=540_000_000,
        moved=4_000_000,
    )
    mp_keep, mp_send = share("mp_share", [mp_keep, over_mp(mp_send, 0)], 2, F32)
    parts = four_ways(share("first_sum", parts, 4, F32, FIRST_FLOPS), 1)
    keep, send = share("second_sum", parts, 2, F32, SECOND_FLOPS)
    got = over_chips(send, None, 2)
    output, grad_input = call(
        mp_sum_kernel, "mp_sum", [(square, BF)] * 2, [mp_keep, over_mp(mp_send, 1)], keep=False
    )
    (dw,) = call(last_sum_kernel, "last_sum", [((4,) + block, F32)], [keep, got], apart=(output,), keep=False)
    return output, grad_input, dw


def solution(mesh):
    fine = Mesh(mesh.devices.reshape(8, 4, 2, 4), SPACE + ("mp",))
    in_specs = (
        P(SPACE, None),
        P(None, "mp"),
        P(None, "mp"),
        P(None, "mp"),
        P("mp", None),
        P(SPACE, "mp"),
        P(SPACE, None),
        P(SPACE, None),
    )
    out_specs = (P(SPACE, "mp"), P(SPACE, "mp"), P(None, SPACE, "mp"))
    return jax.shard_map(body, mesh=fine, in_specs=in_specs, out_specs=out_specs, check_vma=False)
```
